128 devices in a mesh: dp: 8 (over y_hi, x), cuts: 16 (over z, y_lo, core).
Axes of the slice: x: 4, y: 4 (y_hi: 2, y_lo: 2; y = y_hi * 2 + y_lo), z: 4, core: 2. Of those that a mesh axis runs over, the one named last changes fastest.
Arguments:
- feat_table: bfloat16 [1024, 131072], P('cuts', 'dp'), may hold values from -6 to 6
- self_one: int32 [32768], P('dp'), may hold values from 0 to 16383
- near_one: int32 [5, 32768], P(None, 'dp'), may hold values from 0 to 16383
- self_two: int32 [16384], P(('dp', 'cuts')), may hold values from 0 to 255
- near_two: int32 [10, 16384], P(None, ('dp', 'cuts')), may hold values from 0 to 255
- self_three: int32 [4096], P(('dp', 'cuts')), may hold values from 0 to 127
- near_three: int32 [15, 4096], P(None, ('dp', 'cuts')), may hold values from 0 to 127
- targets: int32 [4096, 112], P(('dp', 'cuts')), may hold values 0 or 1
- seed_count: int32 [128], replicated, may hold values from 8 to 32, as said below
- w_one: bfloat16 [2, 1024, 512], P(None, 'cuts'), may hold values from -0.1875 to 0.1875
- bias_one: float32 [512], replicated, may hold values from -3 to 3
- w_two: bfloat16 [2, 512, 512], replicated, may hold values from -0.25 to 0.25
- bias_two: float32 [512], replicated, may hold values from -3 to 3
- w_three: bfloat16 [2, 512, 112], replicated, may hold values from -0.25 to 0.25
- bias_three: float32 [112], replicated, may hold values from -4 to 4
Outputs:
- grad_one: float32 [2, 1024, 512], P(None, 'cuts')
- grad_bias_one: float32 [512], replicated
- grad_two: float32 [2, 512, 512], replicated
- grad_bias_two: float32 [512], replicated
- grad_three: float32 [2, 512, 112], replicated
- grad_bias_three: float32 [112], replicated
The draws below stay inside these ranges and needn't reach their ends.
Inputs may be any that keep to these rules, and one draw needn't show every extreme that they name: `seed_count`: one owner has all 32 seeds live; the others have at least a quarter of them.
All inputs are finite; a program needn't handle non-finite values. No bound on the sum of `targets` on one device may be relied on, other than what follows from the above.
Results may differ from the reference program's by a relative error of at most 0.0065.
Values may be sent and summed in bfloat16 or wider, within the bound.
No kernel may reach another device: no remote copies, remote signals or barrier semaphores. Data moves between devices by JAX's collectives and lax.ppermute only.
A program may use at most 64 MiB of HBM per device.

```python
import math
import jax
import jax.numpy as jnp
import numpy as np
from jax import lax

F = 1024
H = 512
C = 112
FAN1 = 5
FAN2 = 10
FAN3 = 15
NODES = 16384
CAP = 256
H1CAP = 128
SEEDS = 32
TGT_G = 4096
OWNERS = 128
N_DP = 8
N_CUTS = 16


def draw_seed_count(key, part):
    key = jax.random.fold_in(key, 11)
    count_key, spot_key = jax.random.split(key)
    counts = jax.random.randint(count_key, (OWNERS,), SEEDS // 4, SEEDS + 1)
    special_owner = jax.random.randint(spot_key, (), 0, OWNERS)
    return jnp.where(jnp.arange(OWNERS) == special_owner, SEEDS, counts).astype(jnp.int32)


def with_ends(drawn, key, smallest, high):
    shape = drawn.shape
    index_at = [jax.random.randint(jax.random.fold_in(key, axis), (), 0, shape[axis]) for axis in range(len(shape))]
    drawn = drawn.at[tuple(index_at)].set(smallest)
    longest = shape.index(max(shape))
    index_at[longest] = (index_at[longest] + 1) % shape[longest]
    return drawn.at[tuple(index_at)].set(high)


def level_of(rng, dims, pieces, least, top_value):
    level = 1.0
    for dim, parts in pieces:
        steps = jax.random.uniform(jax.random.fold_in(jax.random.fold_in(rng, 6), dim), (parts,), jnp.float32, least / len(pieces), top_value / len(pieces))
        level = level * jnp.repeat(jnp.exp(steps), dims[dim] // parts).reshape((-1,) + (1,) * (len(dims) - 1 - dim))
    return level


def rank_table(count, lean):
    loads = [(1 << 20) // math.isqrt(standing ** lean) + 1 for standing in range(1, count + 1)]
    width = 1 + sum(loads) // (1 << 30)
    return np.cumsum(np.array([max(1, weight // width) for weight in loads]))


def skewed_ids(key, shape, amount, skew):
    table = rank_table(amount, skew)
    pick = jax.random.randint(jax.random.fold_in(key, 1), shape, 0, int(table[amount - 1]))
    grade = jnp.searchsorted(jnp.asarray(table, jnp.int32), pick, side="right")
    return jax.random.permutation(jax.random.fold_in(key, 2), amount)[grade].astype(jnp.int32)


def scatter_about(key, dims, width, limit, cuts=(), held_as=jnp.bfloat16):
    array = jax.random.normal(key, dims, jnp.float32) * width
    if len(cuts) > 0:
        array = level_of(key, dims, cuts, -0.22, 0.18) * array
    return jnp.clip(array, min=-limit, max=limit).astype(held_as)


def setup_inputs(seed: int = 0) -> dict:
    arg_keys = jax.random.split(jax.random.key(seed), 16)
    return {
        "feat_table": scatter_about(arg_keys[0], (F, NODES * N_DP), 1.0, 6.0, ((0, 16), (1, 8))),
        "self_one": with_ends(jax.random.randint(arg_keys[1], (TGT_G * N_DP,), 0, NODES), jax.random.fold_in(arg_keys[1], 1), 0, NODES - 1).astype(jnp.int32),
        "near_one": with_ends(jax.random.randint(arg_keys[2], (FAN1, TGT_G * N_DP), 0, NODES), jax.random.fold_in(arg_keys[2], 1), 0, NODES - 1).astype(jnp.int32),
        "self_two": with_ends(jax.random.randint(arg_keys[3], (H1CAP * OWNERS,), 0, CAP), jax.random.fold_in(arg_keys[3], 1), 0, CAP - 1).astype(jnp.int32),
        "near_two": with_ends(skewed_ids(arg_keys[4], (FAN2, H1CAP * OWNERS), CAP, 2), jax.random.fold_in(arg_keys[4], 3), 0, CAP - 1).astype(jnp.int32),
        "self_three": with_ends(jax.random.randint(arg_keys[5], (SEEDS * OWNERS,), 0, H1CAP), jax.random.fold_in(arg_keys[5], 1), 0, H1CAP - 1).astype(jnp.int32),
        "near_three": with_ends(skewed_ids(arg_keys[6], (FAN3, SEEDS * OWNERS), H1CAP, 2), jax.random.fold_in(arg_keys[6], 3), 0, H1CAP - 1).astype(jnp.int32),
        "targets": with_ends((jax.random.randint(arg_keys[7], (SEEDS * OWNERS, C), 0, 4) < 1).astype(jnp.int32), jax.random.fold_in(arg_keys[7], 1), 0, 1),
        "seed_count": draw_seed_count(jax.random.fold_in(arg_keys[15], 71), 0),
        "w_one": scatter_about(arg_keys[9], (2, F, H), F ** -0.5, 0.1875, ((1, 16),)),
        "bias_one": scatter_about(arg_keys[10], (H,), 0.5, 3.0, (), jnp.float32),
        "w_two": scatter_about(arg_keys[11], (2, H, H), H ** -0.5, 0.25),
        "bias_two": scatter_about(arg_keys[12], (H,), 0.5, 3.0, (), jnp.float32),
        "w_three": scatter_about(arg_keys[13], (2, H, C), H ** -0.5, 0.25),
        "bias_three": scatter_about(arg_keys[14], (C,), 1.0, 4.0, (), jnp.float32),
    }


def gelu_tanh(values):
    return jax.nn.gelu(values, approximate=True)

def gelu_back(pre_act, upstream):
    return jax.vjp(gelu_tanh, pre_act)[1](upstream)[0]

def lead_dot(first_mat, second_mat):
    return lax.dot_general(first_mat, second_mat, (((0,), (0,)), ((), ())), preferred_element_type=jnp.float32)

def plain_dot(first_mat, second_mat):
    return jnp.dot(first_mat, second_mat, preferred_element_type=jnp.float32)

def back_dot(first_mat, second_mat):
    return lax.dot_general(first_mat, second_mat, (((1,), (1,)), ((), ())), preferred_element_type=jnp.float32)

def gather_mean(row_table, near_ids):
    fan_count = near_ids.shape[0]
    running_sum = jnp.zeros((near_ids.shape[1], row_table.shape[1]), jnp.float32)
    for offset in range(fan_count):
        running_sum = running_sum + row_table[near_ids[offset]].astype(jnp.float32)
    return (running_sum / fan_count).astype(jnp.bfloat16)

def spread_back(row_total, self_ids, near_ids, self_grad, near_grad):
    result = jnp.zeros((row_total, self_grad.shape[1]), jnp.float32).at[self_ids].add(self_grad)
    for offset in range(near_ids.shape[0]):
        result = result.at[near_ids[offset]].add(near_grad)
    return result

def owner_pass(hidden_one, self_two, near_two, self_three, near_three, targets, live_mask, loss_scale, w_two, bias_two, w_three, bias_three):
    self_mid = hidden_one[self_two]
    near_mid = gather_mean(hidden_one, near_two)
    pre_two = plain_dot(self_mid, w_two[0]) + plain_dot(near_mid, w_two[1]) + bias_two
    hidden_two = gelu_tanh(pre_two).astype(jnp.bfloat16)
    self_top = hidden_two[self_three]
    near_top = gather_mean(hidden_two, near_three)
    logits = plain_dot(self_top, w_three[0]) + plain_dot(near_top, w_three[1]) + bias_three
    logit_grad = ((jax.nn.sigmoid(logits) - targets.astype(jnp.float32)) * (live_mask[:, None] * loss_scale)).astype(jnp.bfloat16)
    grad_three = jnp.stack([lead_dot(self_top, logit_grad), lead_dot(near_top, logit_grad)])
    bias_grad_three = lax.optimization_barrier(jnp.sum(logit_grad.astype(jnp.float32), axis=0))
    hidden_grad_two = spread_back(hidden_two.shape[0], self_three, near_three, back_dot(logit_grad, w_three[0]), back_dot(logit_grad, w_three[1]) / near_three.shape[0])
    pre_grad_two = gelu_back(pre_two, hidden_grad_two).astype(jnp.bfloat16)
    grad_two = jnp.stack([lead_dot(self_mid, pre_grad_two), lead_dot(near_mid, pre_grad_two)])
    bias_grad_two = lax.optimization_barrier(jnp.sum(pre_grad_two.astype(jnp.float32), axis=0))
    hidden_grad_one = spread_back(hidden_one.shape[0], self_two, near_two, back_dot(pre_grad_two, w_two[0]), back_dot(pre_grad_two, w_two[1]) / near_two.shape[0])
    return (hidden_grad_one, grad_two, bias_grad_two, grad_three, bias_grad_three)

def reference(feat_table, self_one, near_one, self_two, near_two, self_three, near_three, targets, seed_count, w_one, bias_one, w_two, bias_two, w_three, bias_three):
    owner_total = N_DP * N_CUTS
    tables = jnp.transpose(feat_table.reshape(F, N_DP, NODES), (1, 0, 2))
    group_self = self_one.reshape(N_DP, TGT_G)
    group_near = jnp.transpose(near_one.reshape(FAN1, N_DP, TGT_G), (1, 0, 2))

    def group_rows(inputs_tuple):
        feature_table, self_ids, near_ids = inputs_tuple
        self_cols = jnp.take(feature_table, self_ids, axis=1)
        running_sum = jnp.zeros((F, TGT_G), jnp.float32)
        for offset in range(FAN1):
            running_sum = running_sum + jnp.take(feature_table, near_ids[offset], axis=1).astype(jnp.float32)
        return (self_cols, (running_sum / FAN1).astype(jnp.bfloat16))
    self_feat, near_feat = lax.map(group_rows, (tables, group_self, group_near))

    def group_pre(inputs_tuple):
        self_part, near_part = inputs_tuple
        return lead_dot(self_part, w_one[0]) + lead_dot(near_part, w_one[1]) + bias_one
    pre_one = lax.map(group_pre, (self_feat, near_feat))
    hidden_one = gelu_tanh(pre_one).astype(jnp.bfloat16).reshape(owner_total, CAP, H)
    live_mask = (jnp.arange(SEEDS)[None, :] < seed_count[:, None]).astype(jnp.float32)
    loss_scale = 1.0 / jnp.sqrt(jnp.sum(seed_count).astype(jnp.float32))

    def owner_step(inputs_tuple):
        hidden_rows, self_mid_ids, near_mid_ids, self_top_ids, near_top_ids, target_rows, mask_rows = inputs_tuple
        return owner_pass(hidden_rows, self_mid_ids, near_mid_ids, self_top_ids, near_top_ids, target_rows, mask_rows, loss_scale, w_two, bias_two, w_three, bias_three)
    hidden_grad, grad_two, bias_grad_two, grad_three, bias_grad_three = lax.map(owner_step, (hidden_one, self_two.reshape(owner_total, H1CAP), jnp.transpose(near_two.reshape(FAN2, owner_total, H1CAP), (1, 0, 2)), self_three.reshape(owner_total, SEEDS), jnp.transpose(near_three.reshape(FAN3, owner_total, SEEDS), (1, 0, 2)), targets.reshape(owner_total, SEEDS, C), live_mask))
    pre_grad_one = gelu_back(pre_one, hidden_grad.reshape(N_DP, TGT_G, H)).astype(jnp.bfloat16)

    def group_grad(inputs_tuple):
        self_part, near_part, grad_part = inputs_tuple
        return jnp.stack([plain_dot(self_part, grad_part), plain_dot(near_part, grad_part)])
    grad_one = lax.optimization_barrier(jnp.sum(lax.map(group_grad, (self_feat, near_feat, pre_grad_one)), axis=0))
    bias_grad_one = lax.optimization_barrier(jnp.sum(pre_grad_one.astype(jnp.float32), axis=(0, 1)))
    return (grad_one, bias_grad_one, lax.optimization_barrier(jnp.sum(grad_two, axis=0)), lax.optimization_barrier(jnp.sum(bias_grad_two, axis=0)), lax.optimization_barrier(jnp.sum(grad_three, axis=0)), lax.optimization_barrier(jnp.sum(bias_grad_three, axis=0)))
```

```python
import functools

import jax
import jax.numpy as jnp
from jax import lax
from jax.experimental import pallas as pl
from jax.experimental.pallas import tpu as pltpu
from jax.sharding import Mesh, PartitionSpec as P

BF16 = jnp.bfloat16
F32 = jnp.float32
VMEM = pltpu.VMEM
SMEM = pltpu.SMEM

LANES = 128
GATHER_UNROLL = 16
ONE_ROWS = 64
TWO_ROWS = 32
TOP_ROWS = 16
LATE_ROWS = TWO_ROWS + TOP_ROWS
CHUNK_ROWS = ONE_ROWS + LATE_ROWS
PEERS = 64

DP = ("y_hi", "x")
CUTS = ("z", "y_lo", "core")
SAME_CORE = ("y_hi", "x", "z", "y_lo")


def dot(first, second, contract=((1,), (0,))):
    return lax.dot_general(first, second, (contract, ((), ())), preferred_element_type=F32)


def lead_dot(first, second):
    return dot(first, second, ((0,), (0,)))


def back_dot(first, second):
    return dot(first, second, ((1,), (1,)))


def exact_dot(picks, values):
    high = values.astype(BF16)
    low = (values - high.astype(F32)).astype(BF16)
    return dot(picks, high) + dot(picks, low)


def gelu_parts(values):
    inner = 0.7978845608028654 * (values + 0.044715 * values * values * values)
    cdf = 0.5 * (1.0 + jnp.tanh(inner))
    return cdf


def gelu_slope(values):
    square = values * values
    tanh = jnp.tanh(0.7978845608028654 * (values + 0.044715 * values * square))
    inner_slope = 0.7978845608028654 * (1.0 + 3.0 * 0.044715 * square)
    return 0.5 * (1.0 + tanh) + 0.5 * values * (1.0 - tanh * tanh) * inner_slope


def vmem(count):
    return [pl.BlockSpec(memory_space=VMEM)] * count


def gather_kernel(feat_ref, self_ref, near_ref, out_ref, table, rows):
    nodes = feat_ref.shape[1]
    targets = out_ref.shape[0]
    fan = near_ref.shape[0] // targets

    @pl.loop(0, nodes // LANES, unroll=4)
    def _(block):
        spot = pl.ds(pl.multiple_of(block * LANES, LANES), LANES)
        part = feat_ref[:, spot].astype(F32)
        table[spot, :] = jnp.concatenate([part, part], axis=0).T

    half = lax.broadcasted_iota(jnp.int32, (1, LANES), 1) < LANES // 2

    @pl.loop(0, targets // GATHER_UNROLL)
    def _(group):
        base = group * GATHER_UNROLL
        for step in range(GATHER_UNROLL):
            spot = base + step
            total = table[pl.ds(near_ref[spot], 1), :]
            for offset in range(1, fan):
                total = total + table[pl.ds(near_ref[offset * targets + spot], 1), :]
            own = table[pl.ds(self_ref[spot], 1), :]
            rows[pl.ds(spot, 1), :] = jnp.where(half, own, total)

    step_rows = 64
    wide_half = lax.broadcasted_iota(jnp.int32, (step_rows, LANES), 1) < LANES // 2

    @pl.loop(0, targets // step_rows)
    def _(group):
        spot = pl.ds(pl.multiple_of(group * step_rows, step_rows), step_rows)
        value = rows[spot, :]
        out_ref[spot, :] = jnp.where(wide_half, value, value / fan).astype(BF16)


def gather_rows(feat_table, self_one, near_one):
    nodes = feat_table.shape[1]
    targets = self_one.shape[0]
    return pl.pallas_call(
        gather_kernel,
        out_shape=jax.ShapeDtypeStruct((targets, LANES), BF16),
        in_specs=[
            pl.BlockSpec(memory_space=VMEM),
            pl.BlockSpec(memory_space=SMEM),
            pl.BlockSpec(memory_space=SMEM),
        ],
        out_specs=pl.BlockSpec(memory_space=VMEM),
        scratch_shapes=[VMEM((nodes, LANES), F32), VMEM((targets, LANES), F32)],
        compiler_params=pltpu.CompilerParams(vmem_limit_bytes=48 << 20),
        cost_estimate=pl.CostEstimate(flops=1 << 27, bytes_accessed=40 << 20, transcendentals=0),
        name="gather_rows",
    )(feat_table, self_one, near_one.reshape(-1))


def owner_kernel(
    place_ref,
    count_ref,
    rows_ref,
    w_one_ref,
    bias_one_ref,
    self_two_ref,
    near_two_ref,
    self_three_ref,
    near_three_ref,
    targets_ref,
    w_two_ref,
    bias_two_ref,
    w_three_ref,
    bias_three_ref,
    keep_ref,
    send_ref,
    pre_one,
    mids,
    tops,
):
    core = place_ref[0]
    owner = place_ref[1]
    cuts, cap, _ = rows_ref.shape
    hidden = w_two_ref.shape[2]
    labels = w_three_ref.shape[2]
    mid_rows = self_two_ref.shape[1]
    seeds = self_three_ref.shape[1]
    fan_two = near_two_ref.shape[0]
    fan_three = near_three_ref.shape[0]

    total = None
    for pair in range(cuts // 2):
        wide = jnp.concatenate([rows_ref[2 * pair], rows_ref[2 * pair + 1]], axis=1)
        part = dot(wide, w_one_ref[pl.ds(pair * 2 * LANES, 2 * LANES), :])
        total = part if total is None else total + part
    pre_one[...] = total + bias_one_ref[...]
    values = pre_one[...]
    hidden_one = (values * gelu_parts(values)).astype(BF16)

    spots = lax.broadcasted_iota(jnp.int32, (cap, mid_rows), 0)
    self_two_t = (spots == self_two_ref[...]).astype(F32)
    near_two_t = jnp.zeros((cap, mid_rows), F32)
    for offset in range(fan_two):
        near_two_t += (spots == near_two_ref[pl.ds(offset, 1), :]).astype(F32)
    self_mid = dot(self_two_t.T.astype(BF16), hidden_one).astype(BF16)
    near_mid = (dot(near_two_t.T.astype(BF16), hidden_one) / fan_two).astype(BF16)
    mids[0] = self_mid
    mids[1] = near_mid
    pre_two = dot(self_mid, w_two_ref[0]) + dot(near_mid, w_two_ref[1]) + bias_two_ref[...]
    hidden_two = (pre_two * gelu_parts(pre_two)).astype(BF16)

    spots = lax.broadcasted_iota(jnp.int32, (mid_rows, seeds), 0)
    self_three_t = (spots == self_three_ref[...]).astype(F32)
    near_three_t = jnp.zeros((mid_rows, seeds), F32)
    for offset in range(fan_three):
        near_three_t += (spots == near_three_ref[pl.ds(offset, 1), :]).astype(F32)
    self_top = dot(self_three_t.T.astype(BF16), hidden_two).astype(BF16)
    near_top = (dot(near_three_t.T.astype(BF16), hidden_two) / fan_three).astype(BF16)
    tops[0] = self_top
    tops[1] = near_top
    logits = dot(self_top, w_three_ref[0]) + dot(near_top, w_three_ref[1]) + bias_three_ref[...]

    live_total = lax.fori_loop(0, count_ref.shape[0], lambda i, t: t + count_ref[i], jnp.int32(0))
    scale = 1.0 / jnp.sqrt(jnp.full((1, labels), live_total, jnp.int32).astype(F32))
    live = lax.broadcasted_iota(jnp.int32, (seeds, labels), 0) < count_ref[owner]
    slope = jax.nn.sigmoid(logits) - targets_ref[...].astype(F32)
    logit_grad = jnp.where(live, slope * scale, 0.0).astype(BF16)

    self_grad = back_dot(logit_grad, w_three_ref[0])
    near_grad = back_dot(logit_grad, w_three_ref[1]) / fan_three
    upstream = exact_dot(self_three_t.astype(BF16), self_grad)
    upstream += exact_dot(near_three_t.astype(BF16), near_grad)
    pre_grad_two = (gelu_slope(pre_two) * upstream).astype(BF16)

    self_grad = back_dot(pre_grad_two, w_two_ref[0])
    near_grad = back_dot(pre_grad_two, w_two_ref[1]) / fan_two
    upstream = exact_dot(self_two_t.astype(BF16), self_grad)
    upstream += exact_dot(near_two_t.astype(BF16), near_grad)
    pre_grad_one = (gelu_slope(pre_one[...]) * upstream).astype(BF16)

    wide_logit = jnp.concatenate([logit_grad, jnp.zeros((seeds, LANES - labels), BF16)], axis=1)
    bias_one = jnp.sum(pre_grad_one.astype(F32), axis=0, keepdims=True)
    bias_two = jnp.sum(pre_grad_two.astype(F32), axis=0, keepdims=True)
    bias_three = jnp.sum(wide_logit.astype(F32), axis=0, keepdims=True)
    tiles = hidden // LANES
    dp_count = PEERS // (cuts // 2)
    share = LANES // dp_count

    for out_ref, side in ((send_ref, 1 - core), (keep_ref, core)):
        for pair in range(cuts // 2):
            block = lead_dot(rows_ref[2 * pair + side], pre_grad_one).astype(BF16)
            for group in range(dp_count):
                for tile in range(tiles):
                    out_ref[group * (cuts // 2) + pair, pl.ds(tile * share, share), :] = block[
                        group * share : (group + 1) * share, tile * LANES : (tile + 1) * LANES
                    ]
        two = lead_dot(mids[side], pre_grad_two)
        top = lead_dot(tops[side], wide_logit)
        count = hidden // PEERS
        first = (side == 0).astype(F32)
        for peer in range(PEERS):
            late = [
                two[peer * count : (peer + 1) * count, tile * LANES : (tile + 1) * LANES]
                for tile in range(tiles)
            ]
            late.append(top[peer * count : (peer + 1) * count, :])
            if peer < tiles:
                spread = slice(peer * LANES, (peer + 1) * LANES)
                lines = [bias_one[:, spread], bias_two[:, spread]]
                lines.append(bias_three if peer == 0 else jnp.zeros((1, LANES), F32))
                lines.append(jnp.zeros((count - 3, LANES), F32))
                late.append(jnp.concatenate(lines, axis=0) * first)
            else:
                late.append(jnp.zeros((count, LANES), F32))
            out_ref[peer, pl.ds(ONE_ROWS, LATE_ROWS), :] = jnp.concatenate(late, axis=0).astype(BF16)


def owner_pass(place, seed_count, rows, w_one, bias_one, self_two, near_two, self_three, near_three,
               targets, w_two, bias_two, w_three, bias_three):
    cap = rows.shape[1]
    hidden = w_two.shape[2]
    chunk = jax.ShapeDtypeStruct((PEERS, CHUNK_ROWS, LANES), BF16)
    return pl.pallas_call(
        owner_kernel,
        out_shape=(chunk, chunk),
        in_specs=[pl.BlockSpec(memory_space=SMEM)] * 2 + vmem(12),
        out_specs=tuple(vmem(2)),
        scratch_shapes=[
            VMEM((cap, hidden), F32),
            VMEM((2, near_two.shape[1], hidden), BF16),
            VMEM((2, near_three.shape[1], hidden), BF16),
        ],
        compiler_params=pltpu.CompilerParams(vmem_limit_bytes=48 << 20),
        cost_estimate=pl.CostEstimate(flops=1 << 31, bytes_accessed=10 << 20, transcendentals=1 << 19),
        name="owner_pass",
    )(
        place, seed_count, rows, w_one, bias_one.reshape(1, -1), self_two.reshape(1, -1), near_two,
        self_three.reshape(1, -1), near_three, targets, w_two, bias_two.reshape(1, -1), w_three,
        bias_three.reshape(1, -1),
    )


def sum_kernel(parts_ref, one_ref, late_ref):
    total = jnp.sum(parts_ref[...].astype(F32), axis=0)
    one_ref[...] = total[:ONE_ROWS].astype(BF16)
    late = total[ONE_ROWS:].astype(BF16)
    for peer in range(PEERS):
        late_ref[peer] = late


def sum_parts(parts):
    return pl.pallas_call(
        sum_kernel,
        out_shape=(
            jax.ShapeDtypeStruct((ONE_ROWS, LANES), BF16),
            jax.ShapeDtypeStruct((PEERS, LATE_ROWS, LANES), BF16),
        ),
        in_specs=vmem(1),
        out_specs=tuple(vmem(2)),
        compiler_params=pltpu.CompilerParams(vmem_limit_bytes=48 << 20),
        name="sum_parts",
    )(parts)


def unpack_kernel(place_ref, one_ref, own_ref, other_ref, grad_one, bias_one, grad_two, bias_two, grad_three, bias_three):
    core = place_ref[0]
    hidden = grad_one.shape[2]
    tiles = hidden // LANES
    groups = one_ref.shape[0]
    share = ONE_ROWS // tiles
    for group in range(groups):
        layer, line = divmod(group * share, grad_one.shape[1])
        for tile in range(tiles):
            grad_one[layer, pl.ds(line, share), pl.ds(tile * LANES, LANES)] = one_ref[
                group, pl.ds(tile * share, share), :
            ].astype(F32)
    count = hidden // PEERS
    labels = grad_three.shape[2]
    for ref, side in ((own_ref, core), (other_ref, 1 - core)):
        for peer in range(PEERS):
            late = ref[peer].astype(F32)
            for tile in range(tiles):
                grad_two[side, pl.ds(peer * count, count), pl.ds(tile * LANES, LANES)] = late[
                    tile * count : (tile + 1) * count
                ]
            grad_three[side, pl.ds(peer * count, count), :] = late[TWO_ROWS : TWO_ROWS + count, :labels]
    line = TWO_ROWS + count
    for peer in range(tiles):
        late = own_ref[peer].astype(F32)[line : line + count] + other_ref[peer].astype(F32)[line : line + count]
        bias_one[:, pl.ds(peer * LANES, LANES)] = late[0:1]
        bias_two[:, pl.ds(peer * LANES, LANES)] = late[1:2]
        if peer == 0:
            bias_three[...] = late[2:3, :labels]


def unpack(place, one, own, other, cut_rows, hidden, labels):
    return pl.pallas_call(
        unpack_kernel,
        out_shape=(
            jax.ShapeDtypeStruct((2, cut_rows, hidden), F32),
            jax.ShapeDtypeStruct((1, hidden), F32),
            jax.ShapeDtypeStruct((2, hidden, hidden), F32),
            jax.ShapeDtypeStruct((1, hidden), F32),
            jax.ShapeDtypeStruct((2, hidden, labels), F32),
            jax.ShapeDtypeStruct((1, labels), F32),
        ),
        in_specs=[pl.BlockSpec(memory_space=SMEM)] + vmem(3),
        out_specs=tuple(vmem(6)),
        compiler_params=pltpu.CompilerParams(vmem_limit_bytes=48 << 20),
        name="unpack",
    )(place, one, own, other)


def exchange(values, axes):
    return lax.all_to_all(values, axes, 0, 0, tiled=True)


def swap_core(values):
    return lax.ppermute(values, "core", [(0, 1), (1, 0)])


def local(
    feat_table,
    self_one,
    near_one,
    self_two,
    near_two,
    self_three,
    near_three,
    targets,
    seed_count,
    w_one,
    bias_one,
    w_two,
    bias_two,
    w_three,
    bias_three,
):
    cut_rows, hidden = w_one.shape[1:]
    labels = w_three.shape[2]
    cuts = lax.axis_size(CUTS)
    owner = lax.axis_index(DP) * cuts + lax.axis_index(CUTS)
    place = jnp.stack([lax.axis_index("core"), owner]).astype(jnp.int32)
    whole_w_one = lax.all_gather(w_one.reshape(-1, hidden), CUTS, axis=0, tiled=True)
    rows = gather_rows(feat_table, self_one, near_one)
    rows = exchange(rows, CUTS).reshape(cuts, -1, LANES)
    keep, send = owner_pass(
        place, seed_count, rows, whole_w_one, bias_one, self_two, near_two, self_three, near_three,
        targets, w_two, bias_two, w_three, bias_three,
    )
    parts = (keep.astype(F32) + swap_core(send).astype(F32)).astype(BF16)
    parts = exchange(parts, SAME_CORE)
    one, late = sum_parts(parts)
    groups = lax.axis_size(DP)
    one = exchange(jnp.broadcast_to(one[None], (groups,) + one.shape), DP)
    own = exchange(late, SAME_CORE)
    other = swap_core(own)
    grad_one, bias_one, grad_two, bias_two, grad_three, bias_three = unpack(
        place, one, own, other, cut_rows, hidden, labels
    )
    return (
        grad_one,
        bias_one.reshape(-1),
        grad_two,
        bias_two.reshape(-1),
        grad_three,
        bias_three.reshape(-1),
    )


def solution(mesh):
    fine = Mesh(mesh.devices.reshape(2, 4, 4, 2, 2), ("y_hi", "x", "z", "y_lo", "core"))
    both = DP + CUTS
    return jax.shard_map(
        local,
        mesh=fine,
        in_specs=(
            P(CUTS, DP),
            P(DP),
            P(None, DP),
            P(both),
            P(None, both),
            P(both),
            P(None, both),
            P(both, None),
            P(),
            P(None, CUTS, None),
            P(),
            P(),
            P(),
            P(),
            P(),
        ),
        out_specs=(P(None, CUTS, None), P(), P(), P(), P(), P()),
        check_vma=False,
    )
```

```python
import jax
import jax.numpy as jnp
from jax import lax
from jax.experimental import pallas as pl
from jax.experimental.pallas import tpu as pltpu
from jax.sharding import Mesh, PartitionSpec as P

BF16 = jnp.bfloat16
F32 = jnp.float32
VMEM = pltpu.VMEM
SMEM = pltpu.SMEM

LANES = 128
GATHER_UNROLL = 16
ONE_ROWS = 64
TWO_ROWS = 32
TOP_ROWS = 8
LATE_ROWS = TWO_ROWS + TOP_ROWS
CHUNK_ROWS = ONE_ROWS + LATE_ROWS
PEERS = 64

DP = ("y_hi", "x")
CUTS = ("z", "y_lo", "core")
CHIPS = ("z", "y_lo")
SAME_CORE = DP + CHIPS


def dot(first, second, contract=((1,), (0,))):
    return lax.dot_general(first, second, (contract, ((), ())), preferred_element_type=F32)


def lead_dot(first, second):
    return dot(first, second, ((0,), (0,)))


def back_dot(first, second):
    return dot(first, second, ((1,), (1,)))


def exact_dot(picks, values):
    high = values.astype(BF16)
    low = (values - high.astype(F32)).astype(BF16)
    return dot(picks, high) + dot(picks, low)


def gelu_cdf(values):
    return 0.5 * (1.0 + jnp.tanh(0.7978845608028654 * (values + 0.044715 * values * values * values)))


def gelu_slope(values):
    square = values * values
    tanh = jnp.tanh(0.7978845608028654 * (values + 0.044715 * values * square))
    inner_slope = 0.7978845608028654 * (1.0 + 3.0 * 0.044715 * square)
    return 0.5 * (1.0 + tanh) + 0.5 * values * (1.0 - tanh * tanh) * inner_slope


def vmem(count):
    return [pl.BlockSpec(memory_space=VMEM)] * count


def gather_kernel(place_ref, own_ref, other_ref, w_one_ref, self_ref, near_ref, out_ref, table, rows):
    core = place_ref[0]
    nodes = own_ref.shape[1]
    targets = self_ref.shape[0]
    fan = near_ref.shape[0] // targets
    chips = out_ref.shape[0]
    cap = targets // (2 * chips)

    @pl.loop(0, nodes // LANES, unroll=4)
    def _(block):
        spot = pl.ds(pl.multiple_of(block * LANES, LANES), LANES)
        part = jnp.concatenate([own_ref[:, spot], other_ref[:, spot]], axis=0).astype(F32)
        table[spot, :] = part.T

    tiles = w_one_ref.shape[1] // LANES
    for tile in range(tiles):
        block = w_one_ref[:, pl.ds(tile * LANES, LANES)]
        for chip in range(chips):
            out_ref[chip, pl.ds(2 * cap + tile * LANES, LANES), :] = block

    @pl.loop(0, chips)
    def _(chip):
        first = (2 * chip + core) * cap

        @pl.loop(0, cap // GATHER_UNROLL)
        def _(group):
            for step in range(GATHER_UNROLL):
                line = group * GATHER_UNROLL + step
                spot = first + line
                total = table[pl.ds(near_ref[spot], 1), :]
                for offset in range(1, fan):
                    total = total + table[pl.ds(near_ref[offset * targets + spot], 1), :]
                rows[pl.ds(line, 1), :] = table[pl.ds(self_ref[spot], 1), :]
                rows[pl.ds(cap + line, 1), :] = total

        out_ref[chip, pl.ds(0, cap), :] = rows[pl.ds(0, cap), :].astype(BF16)
        out_ref[chip, pl.ds(cap, cap), :] = (rows[pl.ds(cap, cap), :] / fan).astype(BF16)


def gather_rows(place, own_table, other_table, w_one, self_one, near_one, chips):
    nodes = own_table.shape[1]
    cap = self_one.shape[0] // (2 * chips)
    chunk = 2 * cap + w_one.shape[0] * w_one.shape[1] // LANES
    return pl.pallas_call(
        gather_kernel,
        out_shape=jax.ShapeDtypeStruct((chips, chunk, LANES), BF16),
        in_specs=[pl.BlockSpec(memory_space=SMEM)] + vmem(3) + [pl.BlockSpec(memory_space=SMEM)] * 2,
        out_specs=pl.BlockSpec(memory_space=VMEM),
        scratch_shapes=[VMEM((nodes, LANES), F32), VMEM((2 * cap, LANES), F32)],
        compiler_params=pltpu.CompilerParams(vmem_limit_bytes=48 << 20),
        cost_estimate=pl.CostEstimate(flops=1 << 27, bytes_accessed=40 << 20, transcendentals=0),
        name="gather_rows",
    )(place, own_table, other_table, w_one, self_one, near_one.reshape(-1))


def owner_kernel(
    place_ref,
    count_ref,
    rows_ref,
    w_other_ref,
    bias_one_ref,
    self_two_ref,
    near_two_ref,
    self_three_ref,
    near_three_ref,
    targets_ref,
    w_two_ref,
    bias_two_ref,
    w_three_ref,
    bias_three_ref,
    keep_ref,
    send_ref,
    pre_one,
    mids,
    tops,
):
    core = place_ref[0]
    owner = place_ref[1]
    chips = rows_ref.shape[0]
    cap, hidden = pre_one.shape
    labels = w_three_ref.shape[1]
    mid_rows = self_two_ref.shape[1]
    seeds = self_three_ref.shape[1]
    fan_two = near_two_ref.shape[0]
    fan_three = near_three_ref.shape[0]
    tiles = hidden // LANES
    half = LANES // 2

    total = None
    for chip in range(chips):
        columns = []
        for tile in range(tiles):
            mine = 2 * cap + tile * LANES
            other = tile * LANES
            columns.append(
                jnp.concatenate(
                    [
                        rows_ref[chip, pl.ds(mine, half), :],
                        w_other_ref[chip, pl.ds(other, half), :],
                        rows_ref[chip, pl.ds(mine + half, half), :],
                        w_other_ref[chip, pl.ds(other + half, half), :],
                    ],
                    axis=0,
                )
            )
        wide = jnp.concatenate([rows_ref[chip, pl.ds(0, cap), :], rows_ref[chip, pl.ds(cap, cap), :]], axis=1)
        part = dot(wide, jnp.concatenate(columns, axis=1))
        total = part if total is None else total + part
    pre_one[...] = total + bias_one_ref[...]
    values = pre_one[...]
    hidden_one = (values * gelu_cdf(values)).astype(BF16)

    spots = lax.broadcasted_iota(jnp.int32, (cap, mid_rows), 0)
    self_two_t = (spots == self_two_ref[...]).astype(F32)
    near_two_t = jnp.zeros((cap, mid_rows), F32)
    for offset in range(fan_two):
        near_two_t += (spots == near_two_ref[pl.ds(offset, 1), :]).astype(F32)
    self_mid = dot(self_two_t.T.astype(BF16), hidden_one).astype(BF16)
    near_mid = (dot(near_two_t.T.astype(BF16), hidden_one) / fan_two).astype(BF16)
    mids[0] = self_mid
    mids[1] = near_mid
    pre_two = dot(self_mid, w_two_ref[0]) + dot(near_mid, w_two_ref[1]) + bias_two_ref[...]
    hidden_two = (pre_two * gelu_cdf(pre_two)).astype(BF16)

    spots = lax.broadcasted_iota(jnp.int32, (mid_rows, seeds), 0)
    self_three_t = (spots == self_three_ref[...]).astype(F32)
    near_three_t = jnp.zeros((mid_rows, seeds), F32)
    for offset in range(fan_three):
        near_three_t += (spots == near_three_ref[pl.ds(offset, 1), :]).astype(F32)
    self_top = dot(self_three_t.T.astype(BF16), hidden_two).astype(BF16)
    near_top = (dot(near_three_t.T.astype(BF16), hidden_two) / fan_three).astype(BF16)
    tops[0] = self_top
    tops[1] = near_top
    logits = back_dot(self_top, w_three_ref[0]) + back_dot(near_top, w_three_ref[1]) + bias_three_ref[...]

    live_total = lax.fori_loop(0, count_ref.shape[0], lambda i, t: t + count_ref[i], jnp.int32(0))
    scale = 1.0 / jnp.sqrt(jnp.full((1, labels), live_total, jnp.int32).astype(F32))
    live = lax.broadcasted_iota(jnp.int32, (seeds, labels), 0) < count_ref[owner]
    slope = jax.nn.sigmoid(logits) - targets_ref[...].astype(F32)
    logit_grad = jnp.where(live, slope * scale, 0.0).astype(BF16)

    self_grad = dot(logit_grad, w_three_ref[0])
    near_grad = dot(logit_grad, w_three_ref[1]) / fan_three
    upstream = exact_dot(self_three_t.astype(BF16), self_grad)
    upstream += exact_dot(near_three_t.astype(BF16), near_grad)
    pre_grad_two = (gelu_slope(pre_two) * upstream).astype(BF16)

    self_grad = back_dot(pre_grad_two, w_two_ref[0])
    near_grad = back_dot(pre_grad_two, w_two_ref[1]) / fan_two
    upstream = exact_dot(self_two_t.astype(BF16), self_grad)
    upstream += exact_dot(near_two_t.astype(BF16), near_grad)
    pre_grad_one = (gelu_slope(pre_one[...]) * upstream).astype(BF16)

    wide_logit = jnp.concatenate([logit_grad, jnp.zeros((seeds, LANES - labels), BF16)], axis=1)
    bias_three = jnp.sum(wide_logit.astype(F32), axis=0, keepdims=True)
    biases = jnp.concatenate(
        [
            jnp.sum(pre_grad_one.astype(F32), axis=0, keepdims=True),
            jnp.sum(pre_grad_two.astype(F32), axis=0, keepdims=True),
            jnp.concatenate([bias_three, jnp.zeros((1, hidden - LANES), F32)], axis=1),
            jnp.zeros((LANES - labels - 3, hidden), F32),
        ],
        axis=0,
    )
    groups = PEERS // chips
    share = LANES // groups
    count = hidden // PEERS

    for chip in range(chips):
        for line in (0, 1):
            block = lead_dot(rows_ref[chip, pl.ds(line * cap, cap), :], pre_grad_one).astype(BF16)
            for out_ref, start in ((keep_ref, 0), (send_ref, half)):
                for group in range(groups // 2):
                    first = start + group * share
                    peer = (line * (groups // 2) + group) * chips + chip
                    for tile in range(tiles):
                        out_ref[peer, pl.ds(tile * share, share), :] = block[
                            first : first + share, tile * LANES : (tile + 1) * LANES
                        ]
    for out_ref, side in ((send_ref, 1 - core), (keep_ref, core)):
        two = lead_dot(mids[side], pre_grad_two)
        top = lead_dot(wide_logit, tops[side])
        top = jnp.concatenate([top[:labels], biases * (side == 0).astype(F32)], axis=0).T
        for peer in range(PEERS):
            late = [
                two[peer * count : (peer + 1) * count, tile * LANES : (tile + 1) * LANES]
                for tile in range(tiles)
            ]
            late.append(top[peer * count : (peer + 1) * count, :])
            out_ref[peer, pl.ds(ONE_ROWS, LATE_ROWS), :] = jnp.concatenate(late, axis=0).astype(BF16)


def owner_pass(place, seed_count, rows, w_other, bias_one, self_two, near_two, self_three, near_three,
               targets, w_two, bias_two, w_three, bias_three, cap):
    hidden = w_two.shape[2]
    chunk = jax.ShapeDtypeStruct((PEERS, CHUNK_ROWS, LANES), BF16)
    return pl.pallas_call(
        owner_kernel,
        out_shape=(chunk, chunk),
        in_specs=[pl.BlockSpec(memory_space=SMEM)] * 2 + vmem(12),
        out_specs=tuple(vmem(2)),
        scratch_shapes=[
            VMEM((cap, hidden), F32),
            VMEM((2, near_two.shape[1], hidden), BF16),
            VMEM((2, near_three.shape[1], hidden), BF16),
        ],
        compiler_params=pltpu.CompilerParams(vmem_limit_bytes=48 << 20),
        cost_estimate=pl.CostEstimate(flops=1 << 31, bytes_accessed=10 << 20, transcendentals=1 << 19),
        name="owner_pass",
    )(
        place, seed_count, rows, w_other, bias_one.reshape(1, -1), self_two.reshape(1, -1), near_two,
        self_three.reshape(1, -1), near_three, targets, w_two, bias_two.reshape(1, -1),
        jnp.transpose(w_three, (0, 2, 1)), bias_three.reshape(1, -1),
    )


def sum_kernel(parts_ref, out_ref):
    total = parts_ref[0].astype(F32)
    for peer in range(1, PEERS):
        total = total + parts_ref[peer].astype(F32)
    total = total.astype(BF16)
    for peer in range(PEERS):
        out_ref[peer] = total


def sum_parts(parts):
    return pl.pallas_call(
        sum_kernel,
        out_shape=jax.ShapeDtypeStruct(parts.shape, BF16),
        in_specs=vmem(1),
        out_specs=pl.BlockSpec(memory_space=VMEM),
        compiler_params=pltpu.CompilerParams(vmem_limit_bytes=48 << 20),
        name="sum_parts",
    )(parts)


def unpack_kernel(place_ref, own_ref, other_ref, grad_one, bias_one, grad_two, bias_two, grad_three, bias_three, top):
    core = place_ref[0]
    chip = place_ref[2]
    hidden = grad_one.shape[2]
    tiles = hidden // LANES
    share = ONE_ROWS // tiles
    groups = 2 * grad_one.shape[1] // share
    chips = PEERS // groups
    for group in range(groups):
        layer, line = divmod(group * share, grad_one.shape[1])
        for tile in range(tiles):
            grad_one[layer, pl.ds(line, share), pl.ds(tile * LANES, LANES)] = own_ref[
                group * chips + chip, pl.ds(tile * share, share), :
            ].astype(F32)
    count = hidden // PEERS
    labels = grad_three.shape[1]
    for ref, start, side in ((own_ref, ONE_ROWS, core), (other_ref, 0, 1 - core)):
        for peer in range(PEERS):
            late = ref[peer, pl.ds(start, LATE_ROWS), :].astype(F32)
            for tile in range(tiles):
                grad_two[side, pl.ds(peer * count, count), pl.ds(tile * LANES, LANES)] = late[
                    tile * count : (tile + 1) * count
                ]
            top[side, pl.ds(peer * count, count), :] = late[TWO_ROWS:]
    for side in (0, 1):
        flipped = top[side].T
        grad_three[side] = flipped[:labels]
        if side == 0:
            bias_one[...] = flipped[labels : labels + 1]
            bias_two[...] = flipped[labels + 1 : labels + 2]
            bias_three[...] = flipped[labels + 2 : labels + 3, :labels]


def unpack(place, own, other, cut_rows, hidden, labels):
    return pl.pallas_call(
        unpack_kernel,
        out_shape=(
            jax.ShapeDtypeStruct((2, cut_rows, hidden), F32),
            jax.ShapeDtypeStruct((1, hidden), F32),
            jax.ShapeDtypeStruct((2, hidden, hidden), F32),
            jax.ShapeDtypeStruct((1, hidden), F32),
            jax.ShapeDtypeStruct((2, labels, hidden), F32),
            jax.ShapeDtypeStruct((1, labels), F32),
        ),
        in_specs=[pl.BlockSpec(memory_space=SMEM)] + vmem(2),
        out_specs=tuple(vmem(6)),
        scratch_shapes=[VMEM((2, hidden, LANES), F32)],
        compiler_params=pltpu.CompilerParams(vmem_limit_bytes=48 << 20),
        name="unpack",
    )(place, own, other)


def exchange(values, axes):
    return lax.all_to_all(values, axes, 0, 0, tiled=True)


def swap_core(values):
    return lax.ppermute(values, "core", [(0, 1), (1, 0)])


def local(
    feat_table,
    self_one,
    near_one,
    self_two,
    near_two,
    self_three,
    near_three,
    targets,
    seed_count,
    w_one,
    bias_one,
    w_two,
    bias_two,
    w_three,
    bias_three,
):
    cut_rows, hidden = w_one.shape[1:]
    labels = w_three.shape[2]
    chips = lax.axis_size(CHIPS)
    cap = self_one.shape[0] // (2 * chips)
    owner = lax.axis_index(DP) * lax.axis_size(CUTS) + lax.axis_index(CUTS)
    place = jnp.stack([lax.axis_index("core"), owner, lax.axis_index(CHIPS)]).astype(jnp.int32)
    other_table = swap_core(feat_table)
    rows = gather_rows(place, feat_table, other_table, w_one.reshape(-1, hidden), self_one, near_one, chips)
    rows = exchange(rows, CHIPS)
    w_other = swap_core(rows[:, 2 * cap :])
    keep, send = owner_pass(
        place, seed_count, rows, w_other, bias_one, self_two, near_two, self_three, near_three,
        targets, w_two, bias_two, w_three, bias_three, cap,
    )
    parts = (keep.astype(F32) + swap_core(send).astype(F32)).astype(BF16)
    sums = sum_parts(exchange(parts, SAME_CORE))
    own = exchange(sums, SAME_CORE)
    other = swap_core(own[:, ONE_ROWS:])
    grad_one, bias_one, grad_two, bias_two, grad_three, bias_three = unpack(
        place, own, other, cut_rows, hidden, labels
    )
    return (
        grad_one,
        bias_one.reshape(-1),
        grad_two,
        bias_two.reshape(-1),
        jnp.transpose(grad_three, (0, 2, 1)),
        bias_three.reshape(-1),
    )


def solution(mesh):
    fine = Mesh(mesh.devices.reshape(2, 4, 4, 2, 2), ("y_hi", "x", "z", "y_lo", "core"))
    both = DP + CUTS
    return jax.shard_map(
        local,
        mesh=fine,
        in_specs=(
            P(CUTS, DP),
            P(DP),
            P(None, DP),
            P(both),
            P(None, both),
            P(both),
            P(None, both),
            P(both, None),
            P(),
            P(None, CUTS, None),
            P(),
            P(),
            P(),
            P(),
            P(),
        ),
        out_specs=(P(None, CUTS, None), P(), P(), P(), P(), P()),
        check_vma=False,
    )
```

```python
import jax
import jax.numpy as jnp
from jax import lax
from jax.experimental import pallas as pl
from jax.experimental.pallas import tpu as pltpu
from jax.sharding import Mesh, PartitionSpec as P

BF16 = jnp.bfloat16
F32 = jnp.float32
VMEM = pltpu.VMEM
SMEM = pltpu.SMEM

LANES = 128
SUB = 8
GATHER_UNROLL = 16
TABLE_PIECES = 8
ONE_ROWS = 64
TWO_ROWS = 32
TOP_ROWS = 8
LATE_ROWS = TWO_ROWS + TOP_ROWS
CHUNK_ROWS = ONE_ROWS + LATE_ROWS
PEERS = 64

DP = ("y_hi", "x")
CUTS = ("z", "y_lo", "core")
CHIPS = ("z", "y_lo")
SAME_CORE = DP + CHIPS


def dot(first, second, contract=((1,), (0,))):
    return lax.dot_general(first, second, (contract, ((), ())), preferred_element_type=F32)


def lead_dot(first, second):
    return dot(first, second, ((0,), (0,)))


def back_dot(first, second):
    return dot(first, second, ((1,), (1,)))


def exact_dot(picks, values):
    high = values.astype(BF16)
    low = (values - high.astype(F32)).astype(BF16)
    return dot(picks, high) + dot(picks, low)


def gelu_cdf(values):
    return 0.5 * (1.0 + jnp.tanh(0.7978845608028654 * (values + 0.044715 * values * values * values)))


def gelu_slope(values):
    square = values * values
    tanh = jnp.tanh(0.7978845608028654 * (values + 0.044715 * values * square))
    inner_slope = 0.7978845608028654 * (1.0 + 3.0 * 0.044715 * square)
    return 0.5 * (1.0 + tanh) + 0.5 * values * (1.0 - tanh * tanh) * inner_slope


def vmem(count):
    return [pl.BlockSpec(memory_space=VMEM)] * count


def gather_kernel(
    place_ref, own_ref, other_ref, self_ref, near_ref, out_ref, own, other, self_ids, near_ids, table, rows, sems, id_sems
):
    core = place_ref[0]
    nodes = own_ref.shape[1]
    targets = self_ref.shape[0]
    fan = near_ref.shape[0] // targets
    chips = out_ref.shape[0]
    cap = targets // (2 * chips)
    width = nodes // TABLE_PIECES

    fetches = []
    for piece in range(TABLE_PIECES):
        spot = pl.ds(piece * width, width)
        for slot, (source, held) in enumerate(((own_ref, own), (other_ref, other))):
            fetch = pltpu.make_async_copy(source.at[:, spot], held.at[:, spot], sems.at[slot, piece])
            fetch.start()
            fetches.append(fetch)
    id_fetches = [
        pltpu.make_async_copy(self_ref, self_ids, id_sems.at[0]),
        pltpu.make_async_copy(near_ref, near_ids, id_sems.at[1]),
    ]
    for fetch in id_fetches:
        fetch.start()

    for piece in range(TABLE_PIECES):
        fetches[2 * piece].wait()
        fetches[2 * piece + 1].wait()

        @pl.loop(0, width // LANES, unroll=4)
        def _(block):
            spot = pl.ds(pl.multiple_of(piece * width + block * LANES, LANES), LANES)
            part = jnp.concatenate([own[:, spot], other[:, spot]], axis=0).astype(F32)
            table[spot, :] = part.T

    for fetch in id_fetches:
        fetch.wait()

    @pl.loop(0, chips)
    def _(chip):
        first = (2 * chip + core) * cap

        @pl.loop(0, cap // GATHER_UNROLL)
        def _(group):
            for step in range(GATHER_UNROLL):
                line = group * GATHER_UNROLL + step
                spot = first + line
                total = table[pl.ds(near_ids[spot], 1), :]
                for offset in range(1, fan):
                    total = total + table[pl.ds(near_ids[offset * targets + spot], 1), :]
                rows[pl.ds(line, 1), :] = table[pl.ds(self_ids[spot], 1), :]
                rows[pl.ds(cap + line, 1), :] = total

        out_ref[chip, pl.ds(0, cap), :] = rows[pl.ds(0, cap), :].astype(BF16)
        out_ref[chip, pl.ds(cap, cap), :] = (rows[pl.ds(cap, cap), :] / fan).astype(BF16)


def gather_rows(place, own_table, other_table, self_one, near_one, chips):
    features, nodes = own_table.shape
    targets = self_one.shape[0]
    near_one = near_one.reshape(-1)
    cap = targets // (2 * chips)
    anywhere = pl.BlockSpec(memory_space=pl.ANY)
    return pl.pallas_call(
        gather_kernel,
        out_shape=jax.ShapeDtypeStruct((chips, 2 * cap, LANES), BF16),
        in_specs=[pl.BlockSpec(memory_space=SMEM)] + [anywhere] * 4,
        out_specs=pl.BlockSpec(memory_space=VMEM),
        scratch_shapes=[
            VMEM((features, nodes), BF16),
            VMEM((features, nodes), BF16),
            SMEM(self_one.shape, jnp.int32),
            SMEM(near_one.shape, jnp.int32),
            VMEM((nodes, LANES), F32),
            VMEM((2 * cap, LANES), F32),
            pltpu.SemaphoreType.DMA((2, TABLE_PIECES)),
            pltpu.SemaphoreType.DMA((2,)),
        ],
        compiler_params=pltpu.CompilerParams(vmem_limit_bytes=48 << 20),
        cost_estimate=pl.CostEstimate(flops=1 << 27, bytes_accessed=40 << 20, transcendentals=0),
        name="gather_rows",
    )(place, own_table, other_table, self_one, near_one)


def owner_kernel(
    place_ref,
    count_ref,
    rows_ref,
    w_own_ref,
    w_other_ref,
    bias_one_ref,
    self_two_ref,
    near_two_ref,
    self_three_ref,
    near_three_ref,
    targets_ref,
    w_two_ref,
    bias_two_ref,
    w_three_ref,
    bias_three_ref,
    keep_ref,
    send_ref,
    pre_one,
    mids,
    tops,
):
    core = place_ref[0]
    owner = place_ref[1]
    chips = rows_ref.shape[0]
    cap, hidden = pre_one.shape
    labels = w_three_ref.shape[1]
    mid_rows = self_two_ref.shape[1]
    seeds = self_three_ref.shape[1]
    fan_two = near_two_ref.shape[0]
    fan_three = near_three_ref.shape[0]
    tiles = hidden // LANES
    half = LANES // 2

    total = None
    for chip in range(chips):
        depth = [ref[chip, pl.ds(line * half, half), :] for line in (0, 1) for ref in (w_own_ref, w_other_ref)]
        wide = jnp.concatenate([rows_ref[chip, pl.ds(0, cap), :], rows_ref[chip, pl.ds(cap, cap), :]], axis=1)
        part = dot(wide, jnp.concatenate(depth, axis=0))
        total = part if total is None else total + part
    pre_one[...] = total + bias_one_ref[...]
    values = pre_one[...]
    hidden_one = (values * gelu_cdf(values)).astype(BF16)

    spots = lax.broadcasted_iota(jnp.int32, (cap, mid_rows), 0)
    self_two_t = (spots == self_two_ref[...]).astype(F32)
    near_two_t = jnp.zeros((cap, mid_rows), F32)
    for offset in range(fan_two):
        near_two_t += (spots == near_two_ref[pl.ds(offset, 1), :]).astype(F32)
    self_mid = dot(self_two_t.T.astype(BF16), hidden_one).astype(BF16)
    near_mid = (dot(near_two_t.T.astype(BF16), hidden_one) / fan_two).astype(BF16)
    mids[0] = self_mid
    mids[1] = near_mid
    pre_two = dot(self_mid, w_two_ref[0]) + dot(near_mid, w_two_ref[1]) + bias_two_ref[...]
    hidden_two = (pre_two * gelu_cdf(pre_two)).astype(BF16)

    spots = lax.broadcasted_iota(jnp.int32, (mid_rows, seeds), 0)
    self_three_t = (spots == self_three_ref[...]).astype(F32)
    near_three_t = jnp.zeros((mid_rows, seeds), F32)
    for offset in range(fan_three):
        near_three_t += (spots == near_three_ref[pl.ds(offset, 1), :]).astype(F32)
    self_top = dot(self_three_t.T.astype(BF16), hidden_two).astype(BF16)
    near_top = (dot(near_three_t.T.astype(BF16), hidden_two) / fan_three).astype(BF16)
    tops[0] = self_top
    tops[1] = near_top
    logits = back_dot(self_top, w_three_ref[0]) + back_dot(near_top, w_three_ref[1]) + bias_three_ref[...]

    live_total = lax.fori_loop(0, count_ref.shape[0], lambda i, t: t + count_ref[i], jnp.int32(0))
    scale = 1.0 / jnp.sqrt(jnp.full((1, labels), live_total, jnp.int32).astype(F32))
    live = lax.broadcasted_iota(jnp.int32, (seeds, labels), 0) < count_ref[owner]
    slope = jax.nn.sigmoid(logits) - targets_ref[...].astype(F32)
    logit_grad = jnp.where(live, slope * scale, 0.0).astype(BF16)

    self_grad = dot(logit_grad, w_three_ref[0])
    near_grad = dot(logit_grad, w_three_ref[1]) / fan_three
    upstream = exact_dot(self_three_t.astype(BF16), self_grad)
    upstream += exact_dot(near_three_t.astype(BF16), near_grad)
    pre_grad_two = (gelu_slope(pre_two) * upstream).astype(BF16)

    self_grad = back_dot(pre_grad_two, w_two_ref[0])
    near_grad = back_dot(pre_grad_two, w_two_ref[1]) / fan_two
    upstream = exact_dot(self_two_t.astype(BF16), self_grad)
    upstream += exact_dot(near_two_t.astype(BF16), near_grad)
    pre_grad_one = (gelu_slope(pre_one[...]) * upstream).astype(BF16)

    wide_logit = jnp.concatenate([logit_grad, jnp.zeros((seeds, LANES - labels), BF16)], axis=1)
    bias_three = jnp.sum(wide_logit.astype(F32), axis=0, keepdims=True)
    biases = jnp.concatenate(
        [
            jnp.sum(pre_grad_one.astype(F32), axis=0, keepdims=True),
            jnp.sum(pre_grad_two.astype(F32), axis=0, keepdims=True),
            jnp.concatenate([bias_three, jnp.zeros((1, hidden - LANES), F32)], axis=1),
            jnp.zeros((LANES - labels - 3, hidden), F32),
        ],
        axis=0,
    )
    count = hidden // PEERS

    for pair in range(chips // 2):
        sides = []
        for chip in (2 * pair, 2 * pair + 1):
            blocks = [lead_dot(rows_ref[chip, pl.ds(line * cap, cap), :], pre_grad_one) for line in (0, 1)]
            sides.append(
                [jnp.concatenate([block[start : start + half] for block in blocks], axis=0) for start in (0, half)]
            )
        for out_ref, side in ((keep_ref, 0), (send_ref, 1)):
            for peer in range(PEERS):
                line, tile = divmod(peer, tiles)
                cell = [
                    both[side][line * SUB : (line + 1) * SUB, tile * LANES : (tile + 1) * LANES] for both in sides
                ]
                out_ref[peer, pl.ds(pair * 2 * SUB, 2 * SUB), :] = jnp.concatenate(cell, axis=0).astype(BF16)
    for out_ref, side in ((send_ref, 1 - core), (keep_ref, core)):
        two = lead_dot(mids[side], pre_grad_two)
        top = lead_dot(wide_logit, tops[side])
        top = jnp.concatenate([top[:labels], biases * (side == 0).astype(F32)], axis=0).T
        for peer in range(PEERS):
            late = [
                two[peer * count : (peer + 1) * count, tile * LANES : (tile + 1) * LANES]
                for tile in range(tiles)
            ]
            late.append(top[peer * count : (peer + 1) * count, :])
            out_ref[peer, pl.ds(ONE_ROWS, LATE_ROWS), :] = jnp.concatenate(late, axis=0).astype(BF16)


def owner_pass(place, seed_count, rows, w_own, w_other, bias_one, self_two, near_two, self_three, near_three,
               targets, w_two, bias_two, w_three, bias_three, cap):
    hidden = w_two.shape[2]
    chunk = jax.ShapeDtypeStruct((PEERS, CHUNK_ROWS, LANES), BF16)
    return pl.pallas_call(
        owner_kernel,
        out_shape=(chunk, chunk),
        in_specs=[pl.BlockSpec(memory_space=SMEM)] * 2 + vmem(13),
        out_specs=tuple(vmem(2)),
        scratch_shapes=[
            VMEM((cap, hidden), F32),
            VMEM((2, near_two.shape[1], hidden), BF16),
            VMEM((2, near_three.shape[1], hidden), BF16),
        ],
        compiler_params=pltpu.CompilerParams(vmem_limit_bytes=48 << 20),
        cost_estimate=pl.CostEstimate(flops=1 << 31, bytes_accessed=10 << 20, transcendentals=1 << 19),
        name="owner_pass",
    )(
        place, seed_count, rows, w_own, w_other, bias_one.reshape(1, -1), self_two.reshape(1, -1), near_two,
        self_three.reshape(1, -1), near_three, targets, w_two, bias_two.reshape(1, -1),
        jnp.transpose(w_three, (0, 2, 1)), bias_three.reshape(1, -1),
    )


def sum_kernel(parts_ref, out_ref):
    total = parts_ref[0].astype(F32)
    for peer in range(1, PEERS):
        total = total + parts_ref[peer].astype(F32)
    late = total[ONE_ROWS:]
    chips = ONE_ROWS // SUB
    for chip in range(chips):
        block = jnp.concatenate([total[chip * SUB : (chip + 1) * SUB], late], axis=0).astype(BF16)
        for group in range(PEERS // chips):
            out_ref[group * chips + chip] = block


def sum_parts(parts):
    return pl.pallas_call(
        sum_kernel,
        out_shape=jax.ShapeDtypeStruct((PEERS, SUB + LATE_ROWS, LANES), BF16),
        in_specs=vmem(1),
        out_specs=pl.BlockSpec(memory_space=VMEM),
        compiler_params=pltpu.CompilerParams(vmem_limit_bytes=48 << 20),
        name="sum_parts",
    )(parts)


def unpack_kernel(place_ref, own_ref, other_ref, grad_one, bias_one, grad_two, bias_two, grad_three, bias_three, top):
    core = place_ref[0]
    cut_rows, hidden = grad_one.shape[1:]
    tiles = hidden // LANES
    count = hidden // PEERS
    labels = grad_three.shape[1]
    for ref, side in ((own_ref, core), (other_ref, 1 - core)):
        for peer in range(PEERS):
            cells = ref[peer].astype(F32)
            if ref is own_ref:
                line, tile = divmod(peer, tiles)
                layer, line = divmod(line * SUB, cut_rows)
                grad_one[layer, pl.ds(line, SUB), pl.ds(tile * LANES, LANES)] = cells[:SUB]
            for tile in range(tiles):
                grad_two[side, pl.ds(peer * count, count), pl.ds(tile * LANES, LANES)] = cells[
                    SUB + tile * count : SUB + (tile + 1) * count
                ]
            top[side, pl.ds(peer * count, count), :] = cells[SUB + TWO_ROWS :]
    for side in (0, 1):
        flipped = top[side].T
        grad_three[side] = flipped[:labels]
        if side == 0:
            bias_one[...] = flipped[labels : labels + 1]
            bias_two[...] = flipped[labels + 1 : labels + 2]
            bias_three[...] = flipped[labels + 2 : labels + 3, :labels]


def unpack(place, own, other, cut_rows, hidden, labels):
    return pl.pallas_call(
        unpack_kernel,
        out_shape=(
            jax.ShapeDtypeStruct((2, cut_rows, hidden), F32),
            jax.ShapeDtypeStruct((1, hidden), F32),
            jax.ShapeDtypeStruct((2, hidden, hidden), F32),
            jax.ShapeDtypeStruct((1, hidden), F32),
            jax.ShapeDtypeStruct((2, labels, hidden), F32),
            jax.ShapeDtypeStruct((1, labels), F32),
        ),
        in_specs=[pl.BlockSpec(memory_space=SMEM)] + vmem(2),
        out_specs=tuple(vmem(6)),
        scratch_shapes=[VMEM((2, hidden, LANES), F32)],
        compiler_params=pltpu.CompilerParams(vmem_limit_bytes=48 << 20),
        name="unpack",
    )(place, own, other)


def exchange(values, axes):
    return lax.all_to_all(values, axes, 0, 0, tiled=True)


def swap_core(values):
    return lax.ppermute(values, "core", [(0, 1), (1, 0)])


def local(
    feat_table,
    self_one,
    near_one,
    self_two,
    near_two,
    self_three,
    near_three,
    targets,
    seed_count,
    w_one,
    bias_one,
    w_two,
    bias_two,
    w_three,
    bias_three,
):
    cut_rows, hidden = w_one.shape[1:]
    labels = w_three.shape[2]
    chips = lax.axis_size(CHIPS)
    cap = self_one.shape[0] // (2 * chips)
    owner = lax.axis_index(DP) * lax.axis_size(CUTS) + lax.axis_index(CUTS)
    place = jnp.stack([lax.axis_index("core"), owner]).astype(jnp.int32)
    other_table = swap_core(feat_table)
    w_own = exchange(jnp.broadcast_to(w_one.reshape(1, -1, hidden), (chips, 2 * cut_rows, hidden)), CHIPS)
    rows = gather_rows(place, feat_table, other_table, self_one, near_one, chips)
    w_own, rows = lax.optimization_barrier((w_own, rows))
    w_other = swap_core(w_own)
    rows = exchange(rows, CHIPS)
    keep, send = owner_pass(
        place, seed_count, rows, w_own, w_other, bias_one, self_two, near_two, self_three, near_three,
        targets, w_two, bias_two, w_three, bias_three, cap,
    )
    parts = (keep.astype(F32) + swap_core(send).astype(F32)).astype(BF16)
    sums = sum_parts(exchange(parts, SAME_CORE))
    own = exchange(sums, SAME_CORE)
    other = swap_core(own)
    grad_one, bias_one, grad_two, bias_two, grad_three, bias_three = unpack(
        place, own, other, cut_rows, hidden, labels
    )
    return (
        grad_one,
        bias_one.reshape(-1),
        grad_two,
        bias_two.reshape(-1),
        jnp.transpose(grad_three, (0, 2, 1)),
        bias_three.reshape(-1),
    )


def solution(mesh):
    fine = Mesh(mesh.devices.reshape(2, 4, 4, 2, 2), ("y_hi", "x", "z", "y_lo", "core"))
    both = DP + CUTS
    return jax.shard_map(
        local,
        mesh=fine,
        in_specs=(
            P(CUTS, DP),
            P(DP),
            P(None, DP),
            P(both),
            P(None, both),
            P(both),
            P(None, both),
            P(both, None),
            P(),
            P(None, CUTS, None),
            P(),
            P(),
            P(),
            P(),
            P(),
        ),
        out_specs=(P(None, CUTS, None), P(), P(), P(), P(), P()),
        check_vma=False,
    )
```

```python
import jax
import jax.numpy as jnp
from jax import lax
from jax.experimental import pallas as pl
from jax.experimental.pallas import tpu as pltpu
from jax.sharding import Mesh, PartitionSpec as P

BF16 = jnp.bfloat16
F32 = jnp.float32
VMEM = pltpu.VMEM
SMEM = pltpu.SMEM

LANES = 128
SUB = 8
GATHER_UNROLL = 32
TABLE_PIECES = 8
ONE_ROWS = 64
TWO_ROWS = 32
TOP_ROWS = 8
LATE_ROWS = TWO_ROWS + TOP_ROWS
CHUNK_ROWS = ONE_ROWS + LATE_ROWS
PEERS = 64

DP = ("y_hi", "x")
CUTS = ("z", "y_lo", "core")
CHIPS = ("z", "y_lo")
SAME_CORE = DP + CHIPS


def dot(first, second, contract=((1,), (0,))):
    return lax.dot_general(first, second, (contract, ((), ())), preferred_element_type=F32)


def lead_dot(first, second):
    return dot(first, second, ((0,), (0,)))


def back_dot(first, second):
    return dot(first, second, ((1,), (1,)))


def exact_dot(picks, values):
    high = values.astype(BF16)
    low = (values - high.astype(F32)).astype(BF16)
    return dot(picks, high) + dot(picks, low)


def gelu_cdf(values):
    return 0.5 * (1.0 + jnp.tanh(0.7978845608028654 * (values + 0.044715 * values * values * values)))


def gelu_slope(values):
    square = values * values
    tanh = jnp.tanh(0.7978845608028654 * (values + 0.044715 * values * square))
    inner_slope = 0.7978845608028654 * (1.0 + 3.0 * 0.044715 * square)
    return 0.5 * (1.0 + tanh) + 0.5 * values * (1.0 - tanh * tanh) * inner_slope


def vmem(count):
    return [pl.BlockSpec(memory_space=VMEM)] * count


def gather_kernel(
    place_ref, own_ref, other_ref, self_ref, near_ref, out_ref, own, other, self_ids, near_ids, table, rows, sems, id_sems
):
    core = place_ref[0]
    nodes = own_ref.shape[1]
    targets = self_ref.shape[0]
    fan = near_ref.shape[0] // targets
    chips = out_ref.shape[0]
    cap = targets // (2 * chips)
    width = nodes // TABLE_PIECES

    fetches = []
    for piece in range(TABLE_PIECES):
        spot = pl.ds(piece * width, width)
        for slot, (source, held) in enumerate(((own_ref, own), (other_ref, other))):
            fetch = pltpu.make_async_copy(source.at[:, spot], held.at[:, spot], sems.at[slot, piece])
            fetch.start()
            fetches.append(fetch)
    id_fetches = [
        pltpu.make_async_copy(self_ref, self_ids, id_sems.at[0]),
        pltpu.make_async_copy(near_ref, near_ids, id_sems.at[1]),
    ]
    for fetch in id_fetches:
        fetch.start()

    for piece in range(TABLE_PIECES):
        fetches[2 * piece].wait()
        fetches[2 * piece + 1].wait()

        @pl.loop(0, width // LANES, unroll=4)
        def _(block):
            spot = pl.ds(pl.multiple_of(piece * width + block * LANES, LANES), LANES)
            table[spot, :] = jnp.concatenate([own[:, spot], other[:, spot]], axis=0).T.astype(F32)

    for fetch in id_fetches:
        fetch.wait()

    @pl.loop(0, chips)
    def _(chip):
        first = (2 * chip + core) * cap

        @pl.loop(0, cap // GATHER_UNROLL)
        def _(group):
            start = group * GATHER_UNROLL
            mine = self_ids.at[pl.ds(first + start, GATHER_UNROLL)]
            others = [near_ids.at[pl.ds(offset * targets + first + start, GATHER_UNROLL)] for offset in range(fan)]
            for step in range(GATHER_UNROLL):
                total = table[pl.ds(others[0][step], 1), :]
                for ids in others[1:]:
                    total = total + table[pl.ds(ids[step], 1), :]
                rows[pl.ds(start + step, 1), :] = table[pl.ds(mine[step], 1), :]
                rows[pl.ds(cap + start + step, 1), :] = total

        out_ref[chip, pl.ds(0, cap), :] = rows[pl.ds(0, cap), :].astype(BF16)
        out_ref[chip, pl.ds(cap, cap), :] = (rows[pl.ds(cap, cap), :] / fan).astype(BF16)


def gather_rows(place, own_table, other_table, self_one, near_one, chips):
    features, nodes = own_table.shape
    targets = self_one.shape[0]
    near_one = near_one.reshape(-1)
    cap = targets // (2 * chips)
    anywhere = pl.BlockSpec(memory_space=pl.ANY)
    return pl.pallas_call(
        gather_kernel,
        out_shape=jax.ShapeDtypeStruct((chips, 2 * cap, LANES), BF16),
        in_specs=[pl.BlockSpec(memory_space=SMEM)] + [anywhere] * 4,
        out_specs=pl.BlockSpec(memory_space=VMEM),
        scratch_shapes=[
            VMEM((features, nodes), BF16),
            VMEM((features, nodes), BF16),
            SMEM(self_one.shape, jnp.int32),
            SMEM(near_one.shape, jnp.int32),
            VMEM((nodes, LANES), F32),
            VMEM((2 * cap, LANES), F32),
            pltpu.SemaphoreType.DMA((2, TABLE_PIECES)),
            pltpu.SemaphoreType.DMA((2,)),
        ],
        compiler_params=pltpu.CompilerParams(vmem_limit_bytes=24 << 20),
        cost_estimate=pl.CostEstimate(flops=1 << 27, bytes_accessed=40 << 20, transcendentals=0),
        name="gather_rows",
    )(place, own_table, other_table, self_one, near_one)


def spread_kernel(part_ref, out_ref, sems):
    copies = [pltpu.make_async_copy(part_ref, out_ref.at[chip], sems.at[chip]) for chip in range(out_ref.shape[0])]
    for copy in copies:
        copy.start()
    for copy in copies:
        copy.wait()


def spread(part, chips):
    return pl.pallas_call(
        spread_kernel,
        out_shape=jax.ShapeDtypeStruct((chips,) + part.shape, part.dtype),
        in_specs=vmem(1),
        out_specs=pl.BlockSpec(memory_space=pl.ANY),
        scratch_shapes=[pltpu.SemaphoreType.DMA((chips,))],
        name="spread",
    )(part)


def owner_kernel(
    place_ref,
    count_ref,
    counts_ref,
    rows_ref,
    w_own_ref,
    w_other_ref,
    bias_one_ref,
    self_two_ref,
    near_two_ref,
    self_three_ref,
    near_three_ref,
    targets_ref,
    w_two_ref,
    bias_two_ref,
    w_three_ref,
    bias_three_ref,
    send_ref,
    one_ref,
    two_ref,
    mids,
    tops,
    logit_ref,
    biases_ref,
    pre_one,
):
    core = place_ref[0]
    owner = place_ref[1]
    chips = rows_ref.shape[0]
    cap, hidden = pre_one.shape
    labels = w_three_ref.shape[1]
    mid_rows = self_two_ref.shape[1]
    seeds = self_three_ref.shape[1]
    fan_two = near_two_ref.shape[0]
    fan_three = near_three_ref.shape[0]
    tiles = hidden // LANES
    half = LANES // 2

    total = None
    for chip in range(chips):
        depth = [ref[chip, pl.ds(line * half, half), :] for line in (0, 1) for ref in (w_own_ref, w_other_ref)]
        wide = jnp.concatenate([rows_ref[chip, pl.ds(0, cap), :], rows_ref[chip, pl.ds(cap, cap), :]], axis=1)
        part = dot(wide, jnp.concatenate(depth, axis=0))
        total = part if total is None else total + part
    pre_one[...] = total + bias_one_ref[...]
    values = pre_one[...]
    hidden_one = (values * gelu_cdf(values)).astype(BF16)

    spots = lax.broadcasted_iota(jnp.int32, (cap, mid_rows), 0)
    self_two_t = (spots == self_two_ref[...]).astype(F32)
    near_two_t = jnp.zeros((cap, mid_rows), F32)
    for offset in range(fan_two):
        near_two_t += (spots == near_two_ref[pl.ds(offset, 1), :]).astype(F32)
    self_mid = dot(self_two_t.T.astype(BF16), hidden_one).astype(BF16)
    near_mid = (dot(near_two_t.T.astype(BF16), hidden_one) / fan_two).astype(BF16)
    mids[0] = self_mid
    mids[1] = near_mid
    pre_two = dot(self_mid, w_two_ref[0]) + dot(near_mid, w_two_ref[1]) + bias_two_ref[...]
    hidden_two = (pre_two * gelu_cdf(pre_two)).astype(BF16)

    spots = lax.broadcasted_iota(jnp.int32, (mid_rows, seeds), 0)
    self_three_t = (spots == self_three_ref[...]).astype(F32)
    near_three_t = jnp.zeros((mid_rows, seeds), F32)
    for offset in range(fan_three):
        near_three_t += (spots == near_three_ref[pl.ds(offset, 1), :]).astype(F32)
    self_top = dot(self_three_t.T.astype(BF16), hidden_two).astype(BF16)
    near_top = (dot(near_three_t.T.astype(BF16), hidden_two) / fan_three).astype(BF16)
    tops[0] = self_top
    tops[1] = near_top
    logits = back_dot(self_top, w_three_ref[0]) + back_dot(near_top, w_three_ref[1]) + bias_three_ref[...]

    scale = 1.0 / jnp.sqrt(jnp.sum(counts_ref[...].astype(F32), axis=1, keepdims=True))
    live = lax.broadcasted_iota(jnp.int32, (seeds, labels), 0) < count_ref[owner]
    slope = jax.nn.sigmoid(logits) - targets_ref[...].astype(F32)
    logit_grad = jnp.where(live, slope * scale, 0.0).astype(BF16)

    self_grad = dot(logit_grad, w_three_ref[0])
    near_grad = dot(logit_grad, w_three_ref[1]) / fan_three
    upstream = exact_dot(self_three_t.astype(BF16), self_grad)
    upstream += exact_dot(near_three_t.astype(BF16), near_grad)
    pre_grad_two = (gelu_slope(pre_two) * upstream).astype(BF16)

    self_grad = back_dot(pre_grad_two, w_two_ref[0])
    near_grad = back_dot(pre_grad_two, w_two_ref[1]) / fan_two
    upstream = exact_dot(self_two_t.astype(BF16), self_grad)
    upstream += exact_dot(near_two_t.astype(BF16), near_grad)
    pre_grad_one = (gelu_slope(pre_one[...]) * upstream).astype(BF16)

    wide_logit = jnp.concatenate([logit_grad, jnp.zeros((seeds, LANES - labels), BF16)], axis=1)
    bias_three = jnp.sum(wide_logit.astype(F32), axis=0, keepdims=True)
    biases_ref[...] = jnp.concatenate(
        [
            jnp.sum(pre_grad_one.astype(F32), axis=0, keepdims=True),
            jnp.sum(pre_grad_two.astype(F32), axis=0, keepdims=True),
            jnp.concatenate([bias_three, jnp.zeros((1, hidden - LANES), F32)], axis=1),
            jnp.zeros((LANES - labels - 3, hidden), F32),
        ],
        axis=0,
    )
    one_ref[...] = pre_grad_one
    two_ref[...] = pre_grad_two
    logit_ref[...] = wide_logit
    write_products(send_ref, 1, 1 - core, rows_ref, one_ref, two_ref, mids, tops, logit_ref, biases_ref)


def write_products(out_ref, half, side, rows_ref, one_ref, two_ref, mids, tops, logit_ref, biases_ref):
    chips = rows_ref.shape[0]
    cap, hidden = one_ref.shape
    labels = LANES - biases_ref.shape[0]
    tiles = hidden // LANES
    width = LANES // 2
    count = hidden // PEERS
    for pair in range(chips // 2):
        cells = []
        for chip in (2 * pair, 2 * pair + 1):
            blocks = [lead_dot(rows_ref[chip, pl.ds(line * cap, cap), :], one_ref[...]) for line in (0, 1)]
            cells.append(jnp.concatenate([block[half * width : (half + 1) * width] for block in blocks], axis=0))
        for peer in range(PEERS):
            line, tile = divmod(peer, tiles)
            cell = [both[line * SUB : (line + 1) * SUB, tile * LANES : (tile + 1) * LANES] for both in cells]
            out_ref[peer, pl.ds(pair * 2 * SUB, 2 * SUB), :] = jnp.concatenate(cell, axis=0).astype(BF16)
    two = lead_dot(mids[side], two_ref[...])
    top = lead_dot(logit_ref[...], tops[side])
    top = jnp.concatenate([top[:labels], biases_ref[...]], axis=0).T
    for peer in range(PEERS):
        late = [
            two[peer * count : (peer + 1) * count, tile * LANES : (tile + 1) * LANES] for tile in range(tiles)
        ]
        late.append(top[peer * count : (peer + 1) * count, :])
        out_ref[peer, pl.ds(ONE_ROWS, LATE_ROWS), :] = jnp.concatenate(late, axis=0).astype(BF16)


def keep_kernel(place_ref, rows_ref, one_ref, two_ref, mids, tops, logit_ref, biases_ref, keep_ref):
    write_products(keep_ref, 0, place_ref[0], rows_ref, one_ref, two_ref, mids, tops, logit_ref, biases_ref)


def keep_products(place, rows, grads):
    return pl.pallas_call(
        keep_kernel,
        out_shape=jax.ShapeDtypeStruct((PEERS, CHUNK_ROWS, LANES), BF16),
        in_specs=[pl.BlockSpec(memory_space=SMEM)] + vmem(1 + len(grads)),
        out_specs=pl.BlockSpec(memory_space=VMEM),
        compiler_params=pltpu.CompilerParams(vmem_limit_bytes=24 << 20),
        cost_estimate=pl.CostEstimate(flops=1 << 30, bytes_accessed=8 << 20, transcendentals=0),
        name="keep_products",
    )(place, rows, *grads)


def owner_pass(place, seed_count, rows, w_own, w_other, bias_one, self_two, near_two, self_three, near_three,
               targets, w_two, bias_two, w_three, bias_three, cap):
    hidden = w_two.shape[2]
    labels = w_three.shape[2]
    mid_rows = self_two.shape[0]
    seeds = self_three.shape[0]
    return pl.pallas_call(
        owner_kernel,
        out_shape=(
            jax.ShapeDtypeStruct((PEERS, CHUNK_ROWS, LANES), BF16),
            jax.ShapeDtypeStruct((cap, hidden), BF16),
            jax.ShapeDtypeStruct((mid_rows, hidden), BF16),
            jax.ShapeDtypeStruct((2, mid_rows, hidden), BF16),
            jax.ShapeDtypeStruct((2, seeds, hidden), BF16),
            jax.ShapeDtypeStruct((seeds, LANES), BF16),
            jax.ShapeDtypeStruct((LANES - labels, hidden), F32),
        ),
        in_specs=[pl.BlockSpec(memory_space=SMEM)] * 2 + vmem(14),
        out_specs=tuple(vmem(7)),
        scratch_shapes=[VMEM((cap, hidden), F32)],
        compiler_params=pltpu.CompilerParams(vmem_limit_bytes=24 << 20),
        cost_estimate=pl.CostEstimate(flops=1 << 31, bytes_accessed=10 << 20, transcendentals=1 << 19),
        name="owner_pass",
    )(
        place, seed_count, seed_count.reshape(1, -1), rows, w_own, w_other, bias_one.reshape(1, -1), self_two.reshape(1, -1), near_two,
        self_three.reshape(1, -1), near_three, targets, w_two, bias_two.reshape(1, -1),
        jnp.transpose(w_three, (0, 2, 1)), bias_three.reshape(1, -1),
    )


def sum_kernel(parts_ref, out_ref):
    total = parts_ref[0].astype(F32)
    for peer in range(1, PEERS):
        total = total + parts_ref[peer].astype(F32)
    late = total[ONE_ROWS:]
    chips = ONE_ROWS // SUB
    for chip in range(chips):
        block = jnp.concatenate([total[chip * SUB : (chip + 1) * SUB], late], axis=0).astype(BF16)
        for group in range(PEERS // chips):
            out_ref[group * chips + chip] = block


def sum_parts(parts):
    return pl.pallas_call(
        sum_kernel,
        out_shape=jax.ShapeDtypeStruct((PEERS, SUB + LATE_ROWS, LANES), BF16),
        in_specs=vmem(1),
        out_specs=pl.BlockSpec(memory_space=VMEM),
        compiler_params=pltpu.CompilerParams(vmem_limit_bytes=24 << 20),
        name="sum_parts",
    )(parts)


def write_late(ref, side, grad_two, grad_three, two, top, three, sems):
    hidden = two.shape[0]
    labels = three.shape[0]
    count = hidden // PEERS
    pieces = sems.shape[0] - 1
    step = hidden // pieces
    copies = []
    for peer in range(PEERS):
        cells = ref[peer].astype(F32)
        for tile in range(hidden // LANES):
            two[pl.ds(peer * count, count), pl.ds(tile * LANES, LANES)] = cells[
                SUB + tile * count : SUB + (tile + 1) * count
            ]
        top[pl.ds(peer * count, count), :] = cells[SUB + TWO_ROWS :]
        done = (peer + 1) * count
        if done % step == 0:
            spot = pl.ds(done - step, step)
            copies.append(pltpu.make_async_copy(two.at[spot], grad_two.at[side, spot], sems.at[len(copies)]))
            copies[-1].start()
    flipped = top[...].T
    three[...] = flipped[:labels]
    copies.append(pltpu.make_async_copy(three, grad_three.at[side], sems.at[pieces]))
    copies[-1].start()
    return flipped[labels:], copies


def own_kernel(
    place_ref,
    own_ref,
    grad_one,
    grad_two,
    grad_three,
    bias_one,
    bias_two,
    bias_three,
    one,
    two,
    top,
    three,
    first,
    second,
    third,
    sems,
    late_sems,
):
    cut_rows, hidden = one.shape[1:]
    tiles = hidden // LANES
    for peer in range(PEERS):
        line, tile = divmod(peer, tiles)
        layer, line = divmod(line * SUB, cut_rows)
        one[layer, pl.ds(line, SUB), pl.ds(tile * LANES, LANES)] = own_ref[peer].astype(F32)[:SUB]
    one_copy = pltpu.make_async_copy(one, grad_one, late_sems.at[0])
    one_copy.start()
    kept, copies = write_late(own_ref, place_ref[0], grad_two, grad_three, two, top, three, sems)
    first[...] = kept[0:1]
    second[...] = kept[1:2]
    third[...] = kept[2:3, : three.shape[0]]
    for slot, (held, out) in enumerate(((first, bias_one), (second, bias_two), (third, bias_three))):
        copies.append(pltpu.make_async_copy(held, out, late_sems.at[1 + slot]))
        copies[-1].start()
    for copy in [one_copy] + copies:
        copy.wait()


def other_kernel(place_ref, other_ref, two_in, three_in, grad_two, grad_three, two, top, three, sems):
    _, copies = write_late(other_ref, 1 - place_ref[0], grad_two, grad_three, two, top, three, sems)
    for copy in copies:
        copy.wait()


def unpack_own(place, own, cut_rows, hidden, labels):
    anywhere = pl.BlockSpec(memory_space=pl.ANY)
    return pl.pallas_call(
        own_kernel,
        out_shape=(
            jax.ShapeDtypeStruct((2, cut_rows, hidden), F32),
            jax.ShapeDtypeStruct((2, hidden, hidden), F32),
            jax.ShapeDtypeStruct((2, labels, hidden), F32),
            jax.ShapeDtypeStruct((1, hidden), F32),
            jax.ShapeDtypeStruct((1, hidden), F32),
            jax.ShapeDtypeStruct((1, labels), F32),
        ),
        in_specs=[pl.BlockSpec(memory_space=SMEM)] + vmem(1),
        out_specs=(anywhere,) * 6,
        scratch_shapes=[
            VMEM((2, cut_rows, hidden), F32),
            VMEM((hidden, hidden), F32),
            VMEM((hidden, LANES), F32),
            VMEM((labels, hidden), F32),
            VMEM((1, hidden), F32),
            VMEM((1, hidden), F32),
            VMEM((1, labels), F32),
            pltpu.SemaphoreType.DMA((9,)),
            pltpu.SemaphoreType.DMA((4,)),
        ],
        compiler_params=pltpu.CompilerParams(vmem_limit_bytes=16 << 20),
        cost_estimate=pl.CostEstimate(flops=1 << 22, bytes_accessed=4 << 20, transcendentals=0),
        name="unpack_own",
    )(place, own)


def unpack_other(place, other, grad_two, grad_three):
    hidden = grad_two.shape[2]
    labels = grad_three.shape[1]
    anywhere = pl.BlockSpec(memory_space=pl.ANY)
    return pl.pallas_call(
        other_kernel,
        out_shape=(
            jax.ShapeDtypeStruct(grad_two.shape, F32),
            jax.ShapeDtypeStruct(grad_three.shape, F32),
        ),
        in_specs=[pl.BlockSpec(memory_space=SMEM)] + vmem(1) + [anywhere] * 2,
        out_specs=(anywhere, anywhere),
        scratch_shapes=[
            VMEM((hidden, hidden), F32),
            VMEM((hidden, LANES), F32),
            VMEM((labels, hidden), F32),
            pltpu.SemaphoreType.DMA((9,)),
        ],
        input_output_aliases={2: 0, 3: 1},
        compiler_params=pltpu.CompilerParams(vmem_limit_bytes=16 << 20),
        name="unpack_other",
    )(place, other, grad_two, grad_three)


def exchange(values, axes):
    return lax.all_to_all(values, axes, 0, 0, tiled=True)


def swap_core(values):
    return lax.ppermute(values, "core", [(0, 1), (1, 0)])


def local(
    feat_table,
    self_one,
    near_one,
    self_two,
    near_two,
    self_three,
    near_three,
    targets,
    seed_count,
    w_one,
    bias_one,
    w_two,
    bias_two,
    w_three,
    bias_three,
):
    cut_rows, hidden = w_one.shape[1:]
    labels = w_three.shape[2]
    chips = lax.axis_size(CHIPS)
    cap = self_one.shape[0] // (2 * chips)
    owner = lax.axis_index(DP) * lax.axis_size(CUTS) + lax.axis_index(CUTS)
    place = jnp.stack([lax.axis_index("core"), owner]).astype(jnp.int32)
    other_table = swap_core(feat_table)
    w_own = exchange(spread(w_one.reshape(-1, hidden), chips), CHIPS)
    rows = gather_rows(place, feat_table, other_table, self_one, near_one, chips)
    w_own, rows = lax.optimization_barrier((w_own, rows))
    w_other = swap_core(w_own)
    rows = exchange(rows, CHIPS)
    send, *grads = owner_pass(
        place, seed_count, rows, w_own, w_other, bias_one, self_two, near_two, self_three, near_three,
        targets, w_two, bias_two, w_three, bias_three, cap,
    )
    other = swap_core(send)
    keep = keep_products(place, rows, grads)
    parts = (keep.astype(F32) + other.astype(F32)).astype(BF16)
    sums = sum_parts(exchange(parts, SAME_CORE))
    own = exchange(sums, SAME_CORE)
    other = swap_core(own)
    grad_one, grad_two, grad_three, bias_one, bias_two, bias_three = unpack_own(place, own, cut_rows, hidden, labels)
    grad_two, grad_three = unpack_other(place, other, grad_two, grad_three)
    return (
        grad_one,
        bias_one.reshape(-1),
        grad_two,
        bias_two.reshape(-1),
        jnp.transpose(grad_three, (0, 2, 1)),
        bias_three.reshape(-1),
    )


def solution(mesh):
    fine = Mesh(mesh.devices.reshape(2, 4, 4, 2, 2), ("y_hi", "x", "z", "y_lo", "core"))
    both = DP + CUTS
    return jax.shard_map(
        local,
        mesh=fine,
        in_specs=(
            P(CUTS, DP),
            P(DP),
            P(None, DP),
            P(both),
            P(None, both),
            P(both),
            P(None, both),
            P(both, None),
            P(),
            P(None, CUTS, None),
            P(),
            P(),
            P(),
            P(),
            P(),
        ),
        out_specs=(P(None, CUTS, None), P(), P(), P(), P(), P()),
        check_vma=False,
    )
```

```python
import functools

import jax
import jax.numpy as jnp
from jax import lax
from jax.experimental import pallas as pl
from jax.experimental.pallas import tpu as pltpu
from jax.sharding import Mesh, PartitionSpec as P

BF16 = jnp.bfloat16
F32 = jnp.float32
VMEM = pltpu.VMEM
SMEM = pltpu.SMEM
HBM = pltpu.MemorySpace.HBM

LANES = 128
SUB = 8
SPARE = 16
GATHER_UNROLL = 32
TABLE_PIECES = 8
ONE_ROWS = 64
TWO_ROWS = 32
TOP_ROWS = 8
LATE_ROWS = TWO_ROWS + TOP_ROWS
CHUNK_ROWS = ONE_ROWS + LATE_ROWS
PEERS = 64

DP = ("y_hi", "x")
CUTS = ("z", "y_lo", "core")
CHIPS = ("z", "y_lo")
SAME_CORE = DP + CHIPS


def dot(first, second, contract=((1,), (0,))):
    return lax.dot_general(first, second, (contract, ((), ())), preferred_element_type=F32)


def lead_dot(first, second):
    return dot(first, second, ((0,), (0,)))


def back_dot(first, second):
    return dot(first, second, ((1,), (1,)))


def exact_dot(picks, values):
    high = values.astype(BF16)
    low = (values - high.astype(F32)).astype(BF16)
    return dot(picks, high) + dot(picks, low)


def gelu_and_slope(values):
    square = values * values
    tanh = jnp.tanh(0.7978845608028654 * (values + 0.044715 * values * square))
    cdf = 0.5 * (1.0 + tanh)
    inner_slope = 0.7978845608028654 * (1.0 + 3.0 * 0.044715 * square)
    return values * cdf, cdf + 0.5 * values * (1.0 - tanh * tanh) * inner_slope


def vmem(count):
    return [pl.BlockSpec(memory_space=VMEM)] * count


def write_picks(self_ref, near_ref, back, pick):
    def counts(ids):
        total = jnp.zeros(spots.shape, F32)
        for offset in range(ids.shape[0]):
            total += (spots == ids[pl.ds(offset, 1), :]).astype(F32)
        return total

    spots = lax.broadcasted_iota(jnp.int32, (back.shape[0], self_ref.shape[1]), 0)
    both = jnp.concatenate([counts(self_ref), counts(near_ref)], axis=1)
    back[...] = both.astype(BF16)
    pick[...] = both.T.astype(BF16)


def gather_kernel(
    place_ref,
    own_ref,
    other_ref,
    self_ref,
    near_ref,
    out_ref,
    own,
    other,
    self_ids,
    near_ids,
    table,
    rows,
    sems,
    id_sems,
):
    core = place_ref[0]
    nodes = own_ref.shape[1]
    targets = self_ref.shape[0]
    fan = near_ref.shape[0] // targets
    chips = out_ref.shape[0]
    cap = targets // (2 * chips)
    width = nodes // TABLE_PIECES

    fetches = []
    for piece in range(TABLE_PIECES):
        spot = pl.ds(piece * width, width)
        for slot, (source, held) in enumerate(((own_ref, own), (other_ref, other))):
            fetch = pltpu.make_async_copy(source.at[:, spot], held.at[:, spot], sems.at[slot, piece])
            fetch.start()
            fetches.append(fetch)
    id_fetches = [
        pltpu.make_async_copy(self_ref, self_ids, id_sems.at[0]),
        pltpu.make_async_copy(near_ref, near_ids, id_sems.at[1]),
    ]
    for fetch in id_fetches:
        fetch.start()

    for piece in range(TABLE_PIECES):
        fetches[2 * piece].wait()
        fetches[2 * piece + 1].wait()

        @pl.loop(0, width // LANES, unroll=4)
        def _(block):
            spot = pl.ds(pl.multiple_of(piece * width + block * LANES, LANES), LANES)
            table[spot, :] = jnp.concatenate([own[:, spot], other[:, spot]], axis=0).T.astype(F32)

    for fetch in id_fetches:
        fetch.wait()

    @pl.loop(0, chips)
    def _(chip):
        first = (2 * chip + core) * cap

        @pl.loop(0, cap // GATHER_UNROLL)
        def _(group):
            start = group * GATHER_UNROLL
            mine = self_ids.at[pl.ds(first + start, GATHER_UNROLL)]
            others = [near_ids.at[pl.ds(offset * targets + first + start, GATHER_UNROLL)] for offset in range(fan)]
            for step in range(GATHER_UNROLL):
                total = table[pl.ds(others[0][step], 1), :]
                for ids in others[1:]:
                    total = total + table[pl.ds(ids[step], 1), :]
                rows[pl.ds(start + step, 1), :] = table[pl.ds(mine[step], 1), :]
                rows[pl.ds(cap + start + step, 1), :] = total

        half = lax.broadcasted_iota(jnp.int32, (cap, LANES), 1) < LANES // 2
        straight = rows[pl.ds(pl.multiple_of(core * cap, cap), cap), :] * jnp.where(core == 0, 1.0, 1.0 / fan)
        turned = rows[pl.ds(pl.multiple_of((1 - core) * cap, cap), cap), :] * jnp.where(core == 0, 1.0 / fan, 1.0)
        turned = pltpu.roll(turned, LANES // 2, 1)
        out_ref[chip, pl.ds(0, cap), :] = jnp.where(half, straight, turned).astype(BF16)
        out_ref[chip, pl.ds(cap, cap), :] = jnp.where(half, turned, straight).astype(BF16)


def gather_rows(place, own_table, other_table, self_one, near_one, chips):
    features, nodes = own_table.shape
    targets = self_one.shape[0]
    near_one = near_one.reshape(-1)
    cap = targets // (2 * chips)
    return pl.pallas_call(
        gather_kernel,
        out_shape=jax.ShapeDtypeStruct((chips, 2 * cap, LANES), BF16),
        in_specs=[pl.BlockSpec(memory_space=SMEM)] + [pl.BlockSpec(memory_space=pl.ANY)] * 4,
        out_specs=pl.BlockSpec(memory_space=VMEM),
        scratch_shapes=[
            VMEM((features, nodes), BF16),
            VMEM((features, nodes), BF16),
            SMEM(self_one.shape, jnp.int32),
            SMEM(near_one.shape, jnp.int32),
            VMEM((nodes, LANES), F32),
            VMEM((2 * cap, LANES), F32),
            pltpu.SemaphoreType.DMA((2, TABLE_PIECES)),
            pltpu.SemaphoreType.DMA((2,)),
        ],
        compiler_params=pltpu.CompilerParams(vmem_limit_bytes=24 << 20),
        cost_estimate=pl.CostEstimate(flops=1 << 27, bytes_accessed=40 << 20, transcendentals=0),
        name="gather_rows",
    )(place, own_table, other_table, self_one, near_one)


def spread_kernel(part_ref, out_ref, sems):
    copies = [pltpu.make_async_copy(part_ref, out_ref.at[chip], sems.at[chip]) for chip in range(out_ref.shape[0])]
    for copy in copies:
        copy.start()
    for copy in copies:
        copy.wait()


def spread(part, chips):
    return pl.pallas_call(
        spread_kernel,
        out_shape=jax.ShapeDtypeStruct((chips,) + part.shape, part.dtype),
        in_specs=vmem(1),
        out_specs=pl.BlockSpec(memory_space=pl.ANY),
        scratch_shapes=[pltpu.SemaphoreType.DMA((chips,))],
        name="spread",
    )(part)


def picks_kernel(self_two_ref, near_two_ref, self_three_ref, near_three_ref, back_two, pick_two, back_three, pick_three):
    write_picks(self_two_ref, near_two_ref, back_two, pick_two)
    write_picks(self_three_ref, near_three_ref, back_three, pick_three)


def make_picks(self_two, near_two, self_three, near_three, cap):
    mid_rows = self_two.shape[0]
    seeds = self_three.shape[0]
    shapes = [(cap, 2 * mid_rows), (2 * mid_rows, cap), (mid_rows, 2 * seeds), (2 * seeds, mid_rows)]
    return pl.pallas_call(
        picks_kernel,
        out_shape=tuple(jax.ShapeDtypeStruct(shape, BF16) for shape in shapes),
        in_specs=vmem(4),
        out_specs=tuple(vmem(4)),
        compiler_params=pltpu.CompilerParams(vmem_limit_bytes=8 << 20),
        name="make_picks",
    )(self_two.reshape(1, -1), near_two, self_three.reshape(1, -1), near_three)


def owner_kernel(
    fan_two,
    fan_three,
    place_ref,
    count_ref,
    counts_ref,
    rows_ref,
    w_own_ref,
    w_other_ref,
    bias_one_ref,
    pick_two,
    back_three,
    pick_three,
    targets_ref,
    w_two_ref,
    bias_two_ref,
    w_three_ref,
    bias_three_ref,
    slope_one,
    two_ref,
    mids,
    tops,
    logit_ref,
    ship_ref,
):
    core = place_ref[0]
    owner = place_ref[1]
    chips = rows_ref.shape[0]
    cap, hidden = slope_one.shape
    labels = w_three_ref.shape[1]
    mid_rows = mids.shape[1]
    seeds = tops.shape[1]
    half = LANES // 2
    front = pl.ds(pl.multiple_of(core * half, half), half)
    back = pl.ds(pl.multiple_of((1 - core) * half, half), half)

    total = None
    for chip in range(chips):
        wide = jnp.concatenate([rows_ref[chip, pl.ds(0, cap), :], rows_ref[chip, pl.ds(cap, cap), :]], axis=1)
        depth = [
            w_own_ref[chip, front, :],
            w_own_ref[chip, back, :],
            w_other_ref[chip, back, :],
            w_other_ref[chip, front, :],
        ]
        part = dot(wide, jnp.concatenate(depth, axis=0))
        total = part if total is None else total + part
    hidden_one, slope = gelu_and_slope(total + bias_one_ref[...])
    slope_one[...] = slope

    mid = dot(pick_two[...], hidden_one.astype(BF16))
    self_mid = mid[:mid_rows].astype(BF16)
    near_mid = (mid[mid_rows:] / fan_two).astype(BF16)
    mids[0] = self_mid
    mids[1] = near_mid
    pre_two = dot(self_mid, w_two_ref[0]) + dot(near_mid, w_two_ref[1]) + bias_two_ref[...]
    hidden_two, slope_two = gelu_and_slope(pre_two)

    top = dot(pick_three[...], hidden_two.astype(BF16))
    self_top = top[:seeds].astype(BF16)
    near_top = (top[seeds:] / fan_three).astype(BF16)
    tops[0] = self_top
    tops[1] = near_top
    logits = back_dot(self_top, w_three_ref[0]) + back_dot(near_top, w_three_ref[1]) + bias_three_ref[...]

    scale = 1.0 / jnp.sqrt(jnp.sum(counts_ref[...].astype(F32), axis=1, keepdims=True))
    live = lax.broadcasted_iota(jnp.int32, (seeds, labels), 0) < count_ref[owner]
    slope = jax.nn.sigmoid(logits) - targets_ref[...].astype(F32)
    logit_grad = jnp.where(live, slope * scale, 0.0).astype(BF16)

    grads = [dot(logit_grad, w_three_ref[0]), dot(logit_grad, w_three_ref[1]) / fan_three]
    upstream = exact_dot(back_three[...], jnp.concatenate(grads, axis=0))
    pre_grad_two = (slope_two * upstream).astype(BF16)

    wide_logit = jnp.concatenate([logit_grad, jnp.zeros((seeds, LANES - labels), BF16)], axis=1)
    two_ref[...] = pre_grad_two
    logit_ref[...] = wide_logit
    ship_ref[pl.ds(0, mid_rows), :] = mids[1 - core]
    ship_ref[pl.ds(mid_rows, mid_rows), :] = pre_grad_two
    ship_ref[pl.ds(2 * mid_rows, seeds), :] = tops[1 - core]
    ship_ref[pl.ds(2 * mid_rows + seeds, seeds), pl.ds(0, LANES)] = wide_logit


def write_one(out_ref, half, one, rows_ref):
    chips = rows_ref.shape[0]
    cap, hidden = one.shape
    count = hidden // PEERS
    spot = pl.ds(half * cap, cap)
    flipped = one.T
    for pair in range(chips // 2):
        wide = jnp.concatenate([rows_ref[2 * pair, spot, :], rows_ref[2 * pair + 1, spot, :]], axis=1)
        block = dot(flipped, wide)
        for peer in range(PEERS):
            line = block[peer * count : (peer + 1) * count]
            cell = jnp.concatenate([line[:, :LANES], line[:, LANES:]], axis=0)
            out_ref[peer, pl.ds(pair * 2 * SUB, 2 * SUB), :] = cell.astype(BF16)


def send_kernel(fan_two, slope_one, two_ref, back_two, w_two_ref, rows_ref, send_ref, one_ref):
    grads = [back_dot(two_ref[...], w_two_ref[0]), back_dot(two_ref[...], w_two_ref[1]) / fan_two]
    upstream = exact_dot(back_two[...], jnp.concatenate(grads, axis=0))
    pre_grad_one = (slope_one[...] * upstream).astype(BF16)
    one_ref[...] = pre_grad_one
    write_one(send_ref, 1, pre_grad_one, rows_ref)


def send_products(slope_one, two, back_two, w_two, rows, fan_two):
    return pl.pallas_call(
        functools.partial(send_kernel, fan_two),
        out_shape=(
            jax.ShapeDtypeStruct((PEERS, ONE_ROWS, LANES), BF16),
            jax.ShapeDtypeStruct(slope_one.shape, BF16),
        ),
        in_specs=vmem(5),
        out_specs=tuple(vmem(2)),
        compiler_params=pltpu.CompilerParams(vmem_limit_bytes=24 << 20),
        cost_estimate=pl.CostEstimate(flops=1 << 29, bytes_accessed=4 << 20, transcendentals=0),
        name="send_products",
    )(slope_one, two, back_two, w_two, rows)


def keep_kernel(place_ref, rows_ref, one_ref, two_ref, mids, tops, logit_ref, ship_ref, keep_ref):
    core = place_ref[0]
    hidden = one_ref.shape[1]
    mid_rows = two_ref.shape[0]
    seeds = logit_ref.shape[0]
    tiles = hidden // LANES
    count = hidden // PEERS
    write_one(keep_ref, 0, one_ref[...], rows_ref)

    other_mid = ship_ref[pl.ds(0, mid_rows), :]
    other_two = ship_ref[pl.ds(mid_rows, mid_rows), :]
    other_top = ship_ref[pl.ds(2 * mid_rows, seeds), :]
    other_logit = ship_ref[pl.ds(2 * mid_rows + seeds, seeds), pl.ds(0, LANES)]
    both_two = jnp.concatenate([two_ref[...], other_two], axis=0)
    two = lead_dot(jnp.concatenate([mids[core], other_mid], axis=0), both_two)
    both_logit = jnp.concatenate([logit_ref[...], other_logit], axis=0)
    top = lead_dot(both_logit, jnp.concatenate([tops[core], other_top], axis=0))
    bias_three = jnp.sum(logit_ref[...].astype(F32), axis=0, keepdims=True)
    biases = [
        jnp.sum(one_ref[...].astype(F32), axis=0, keepdims=True),
        jnp.sum(two_ref[...].astype(F32), axis=0, keepdims=True),
        jnp.concatenate([bias_three, jnp.zeros((1, hidden - LANES), F32)], axis=1),
        jnp.zeros((SPARE - 3, hidden), F32),
    ]
    top = jnp.concatenate([top[: LANES - SPARE]] + biases, axis=0).T
    for peer in range(PEERS):
        late = [
            two[peer * count : (peer + 1) * count, tile * LANES : (tile + 1) * LANES] for tile in range(tiles)
        ]
        late.append(top[peer * count : (peer + 1) * count, :])
        keep_ref[peer, pl.ds(ONE_ROWS, LATE_ROWS), :] = jnp.concatenate(late, axis=0).astype(BF16)


def keep_products(place, rows, one, grads):
    return pl.pallas_call(
        keep_kernel,
        out_shape=jax.ShapeDtypeStruct((PEERS, CHUNK_ROWS, LANES), BF16),
        in_specs=[pl.BlockSpec(memory_space=SMEM)] + vmem(2 + len(grads)),
        out_specs=pl.BlockSpec(memory_space=VMEM),
        compiler_params=pltpu.CompilerParams(vmem_limit_bytes=24 << 20),
        cost_estimate=pl.CostEstimate(flops=1 << 30, bytes_accessed=8 << 20, transcendentals=0),
        name="keep_products",
    )(place, rows, one, *grads)


def merge_kernel(keep_ref, other_ref, out_ref):
    spot = pl.ds(0, ONE_ROWS)
    out_ref[:, spot, :] = keep_ref[:, spot, :] + other_ref[...]


def merge(keep, other):
    return pl.pallas_call(
        merge_kernel,
        out_shape=jax.ShapeDtypeStruct(keep.shape, BF16),
        in_specs=vmem(2),
        out_specs=pl.BlockSpec(memory_space=VMEM),
        input_output_aliases={0: 0},
        compiler_params=pltpu.CompilerParams(vmem_limit_bytes=24 << 20),
        name="merge",
    )(keep, other)


def owner_pass(place, seed_count, rows, w_own, w_other, bias_one, picks, targets, w_two, bias_two, w_three, bias_three,
               fans):
    hidden = w_two.shape[2]
    labels = w_three.shape[2]
    cap = picks[1].shape[1]
    mid_rows = picks[2].shape[0]
    seeds = targets.shape[0]
    return pl.pallas_call(
        functools.partial(owner_kernel, *fans),
        out_shape=(
            jax.ShapeDtypeStruct((cap, hidden), F32),
            jax.ShapeDtypeStruct((mid_rows, hidden), BF16),
            jax.ShapeDtypeStruct((2, mid_rows, hidden), BF16),
            jax.ShapeDtypeStruct((2, seeds, hidden), BF16),
            jax.ShapeDtypeStruct((seeds, LANES), BF16),
            jax.ShapeDtypeStruct((2 * (mid_rows + seeds), hidden), BF16),
        ),
        in_specs=[pl.BlockSpec(memory_space=SMEM)] * 2 + vmem(13),
        out_specs=tuple(vmem(6)),
        compiler_params=pltpu.CompilerParams(vmem_limit_bytes=24 << 20),
        cost_estimate=pl.CostEstimate(flops=1 << 31, bytes_accessed=10 << 20, transcendentals=1 << 19),
        name="owner_pass",
    )(
        place, seed_count, seed_count.reshape(1, -1), rows, w_own, w_other, bias_one.reshape(1, -1), *picks[1:],
        targets, w_two, bias_two.reshape(1, -1), jnp.transpose(w_three, (0, 2, 1)), bias_three.reshape(1, -1),
    )


def sum_kernel(parts_ref, out_ref):
    total = parts_ref[0].astype(F32)
    for peer in range(1, PEERS):
        total = total + parts_ref[peer].astype(F32)
    late = total[ONE_ROWS:]
    chips = ONE_ROWS // SUB
    for chip in range(chips):
        block = jnp.concatenate([total[chip * SUB : (chip + 1) * SUB], late], axis=0).astype(BF16)
        for group in range(PEERS // chips):
            out_ref[group * chips + chip] = block


def sum_parts(parts):
    return pl.pallas_call(
        sum_kernel,
        out_shape=jax.ShapeDtypeStruct((PEERS, SUB + LATE_ROWS, LANES), BF16),
        in_specs=vmem(1),
        out_specs=pl.BlockSpec(memory_space=VMEM),
        compiler_params=pltpu.CompilerParams(vmem_limit_bytes=24 << 20),
        name="sum_parts",
    )(parts)


def write_late(ref, side, grad_two, grad_three, two, top, three, sems):
    hidden = two.shape[0]
    labels = three.shape[0]
    count = hidden // PEERS
    pieces = sems.shape[0] - 1
    step = hidden // pieces
    copies = []
    for peer in range(PEERS):
        cells = ref[peer].astype(F32)
        for tile in range(hidden // LANES):
            two[pl.ds(peer * count, count), pl.ds(tile * LANES, LANES)] = cells[
                SUB + tile * count : SUB + (tile + 1) * count
            ]
        top[pl.ds(peer * count, count), :] = cells[SUB + TWO_ROWS :]
        done = (peer + 1) * count
        if done % step == 0:
            spot = pl.ds(done - step, step)
            copies.append(pltpu.make_async_copy(two.at[spot], grad_two.at[side, spot], sems.at[len(copies)]))
            copies[-1].start()
    flipped = top[...].T
    three[...] = flipped[:labels]
    copies.append(pltpu.make_async_copy(three, grad_three.at[side], sems.at[pieces]))
    copies[-1].start()
    return flipped[labels:], copies


def own_kernel(
    place_ref,
    own_ref,
    grad_one,
    grad_two,
    grad_three,
    biases,
    flat,
    one,
    two,
    top,
    three,
    sems,
    one_sem,
):
    cut_rows, hidden = one.shape[1:]
    count = hidden // PEERS
    for peer in range(PEERS):
        flat[pl.ds(peer * count, count), :] = own_ref[peer].astype(F32)[:SUB]
    turned = flat[...].T
    one[place_ref[0]] = turned[:cut_rows]
    one[1 - place_ref[0]] = turned[cut_rows:]
    one_copy = pltpu.make_async_copy(one, grad_one, one_sem)
    one_copy.start()
    kept, copies = write_late(own_ref, place_ref[0], grad_two, grad_three, two, top, three, sems)
    biases[...] = kept
    for copy in [one_copy] + copies:
        copy.wait()


def other_kernel(
    place_ref,
    other_ref,
    biases,
    two_in,
    three_in,
    grad_two,
    grad_three,
    bias_one,
    bias_two,
    bias_three,
    two,
    top,
    three,
    first,
    second,
    third,
    sems,
    bias_sems,
):
    kept, copies = write_late(other_ref, 1 - place_ref[0], grad_two, grad_three, two, top, three, sems)
    kept = kept + biases[...]
    first[...] = kept[0:1]
    second[...] = kept[1:2]
    third[...] = kept[2:3, : three.shape[0]]
    for slot, (held, out) in enumerate(((first, bias_one), (second, bias_two), (third, bias_three))):
        copies.append(pltpu.make_async_copy(held, out, bias_sems.at[slot]))
        copies[-1].start()
    for copy in copies:
        copy.wait()


def unpack_own(place, own, cut_rows, hidden, labels):
    anywhere = pl.BlockSpec(memory_space=pl.ANY)
    return pl.pallas_call(
        own_kernel,
        out_shape=(
            jax.ShapeDtypeStruct((2, cut_rows, hidden), F32),
            jax.ShapeDtypeStruct((2, hidden, hidden), F32),
            jax.ShapeDtypeStruct((2, labels, hidden), F32),
            jax.ShapeDtypeStruct((SPARE, hidden), F32),
        ),
        in_specs=[pl.BlockSpec(memory_space=SMEM)] + vmem(1),
        out_specs=(anywhere,) * 3 + tuple(vmem(1)),
        scratch_shapes=[
            VMEM((hidden, LANES), F32),
            VMEM((2, cut_rows, hidden), F32),
            VMEM((hidden, hidden), F32),
            VMEM((hidden, LANES), F32),
            VMEM((labels, hidden), F32),
            pltpu.SemaphoreType.DMA((9,)),
            pltpu.SemaphoreType.DMA,
        ],
        compiler_params=pltpu.CompilerParams(vmem_limit_bytes=16 << 20),
        cost_estimate=pl.CostEstimate(flops=1 << 22, bytes_accessed=4 << 20, transcendentals=0),
        name="unpack_own",
    )(place, own)


def unpack_other(place, other, biases, grad_two, grad_three):
    hidden = grad_two.shape[2]
    labels = grad_three.shape[1]
    anywhere = pl.BlockSpec(memory_space=pl.ANY)
    return pl.pallas_call(
        other_kernel,
        out_shape=(
            jax.ShapeDtypeStruct(grad_two.shape, F32),
            jax.ShapeDtypeStruct(grad_three.shape, F32),
            jax.ShapeDtypeStruct((1, hidden), F32),
            jax.ShapeDtypeStruct((1, hidden), F32),
            jax.ShapeDtypeStruct((1, labels), F32),
        ),
        in_specs=[pl.BlockSpec(memory_space=SMEM)] + vmem(2) + [anywhere] * 2,
        out_specs=(anywhere,) * 5,
        scratch_shapes=[
            VMEM((hidden, hidden), F32),
            VMEM((hidden, LANES), F32),
            VMEM((labels, hidden), F32),
            VMEM((1, hidden), F32),
            VMEM((1, hidden), F32),
            VMEM((1, labels), F32),
            pltpu.SemaphoreType.DMA((9,)),
            pltpu.SemaphoreType.DMA((3,)),
        ],
        input_output_aliases={3: 0, 4: 1},
        compiler_params=pltpu.CompilerParams(vmem_limit_bytes=16 << 20),
        name="unpack_other",
    )(place, other, biases, grad_two, grad_three)


def exchange(values, axes):
    return lax.all_to_all(values, axes, 0, 0, tiled=True)


def swap_core(values):
    return lax.ppermute(values, "core", [(0, 1), (1, 0)])


def local(
    feat_table,
    self_one,
    near_one,
    self_two,
    near_two,
    self_three,
    near_three,
    targets,
    seed_count,
    w_one,
    bias_one,
    w_two,
    bias_two,
    w_three,
    bias_three,
):
    cut_rows, hidden = w_one.shape[1:]
    labels = w_three.shape[2]
    chips = lax.axis_size(CHIPS)
    cap = self_one.shape[0] // (2 * chips)
    owner = lax.axis_index(DP) * lax.axis_size(CUTS) + lax.axis_index(CUTS)
    place = jnp.stack([lax.axis_index("core"), owner]).astype(jnp.int32)
    other_table = swap_core(feat_table)
    w_own = exchange(spread(w_one.reshape(-1, hidden), chips), CHIPS)
    rows = gather_rows(place, feat_table, other_table, self_one, near_one, chips)
    self_two, rows = lax.optimization_barrier((self_two, rows))
    picks = make_picks(self_two, near_two, self_three, near_three, cap)
    w_own, rows, picks = lax.optimization_barrier((w_own, rows, picks))
    w_other = swap_core(w_own)
    rows = exchange(rows, CHIPS)
    fans = (near_two.shape[0], near_three.shape[0])
    slope_one, *grads, ship = owner_pass(
        place, seed_count, rows, w_own, w_other, bias_one, picks, targets, w_two, bias_two, w_three, bias_three, fans
    )
    ship = swap_core(ship)
    send, one = send_products(slope_one, grads[0], picks[0], w_two, rows, fans[0])
    send, ship = lax.optimization_barrier((send, ship))
    other = swap_core(send)
    keep = keep_products(place, rows, one, (*grads, ship))
    parts = merge(keep, other)
    sums = sum_parts(exchange(parts, SAME_CORE))
    own = exchange(sums, SAME_CORE)
    other = swap_core(own)
    grad_one, grad_two, grad_three, biases = unpack_own(place, own, cut_rows, hidden, labels)
    grad_two, grad_three, bias_one, bias_two, bias_three = unpack_other(place, other, biases, grad_two, grad_three)
    return (
        grad_one,
        bias_one.reshape(-1),
        grad_two,
        bias_two.reshape(-1),
        jnp.transpose(grad_three, (0, 2, 1)),
        bias_three.reshape(-1),
    )


def solution(mesh):
    fine = Mesh(mesh.devices.reshape(2, 4, 4, 2, 2), ("y_hi", "x", "z", "y_lo", "core"))
    both = DP + CUTS
    return jax.shard_map(
        local,
        mesh=fine,
        in_specs=(
            P(CUTS, DP),
            P(DP),
            P(None, DP),
            P(both),
            P(None, both),
            P(both),
            P(None, both),
            P(both, None),
            P(),
            P(None, CUTS, None),
            P(),
            P(),
            P(),
            P(),
            P(),
        ),
        out_specs=(P(None, CUTS, None), P(), P(), P(), P(), P()),
        check_vma=False,
    )
```

```python
import functools

import jax
import jax.numpy as jnp
from jax import lax
from jax.experimental import pallas as pl
from jax.experimental.pallas import tpu as pltpu
from jax.sharding import Mesh, PartitionSpec as P

BF16 = jnp.bfloat16
F32 = jnp.float32
VMEM = pltpu.VMEM
SMEM = pltpu.SMEM
HBM = pltpu.MemorySpace.HBM

LANES = 128
SUB = 8
SPARE = 16
GATHER_UNROLL = 32
TABLE_PIECES = 8
ONE_ROWS = 64
TWO_ROWS = 32
TOP_ROWS = 8
LATE_ROWS = TWO_ROWS + TOP_ROWS
CHUNK_ROWS = ONE_ROWS + LATE_ROWS
PEERS = 64

DP = ("y_hi", "x")
CUTS = ("z", "y_lo", "core")
CHIPS = ("z", "y_lo")
SAME_CORE = DP + CHIPS


def dot(first, second, contract=((1,), (0,))):
    return lax.dot_general(first, second, (contract, ((), ())), preferred_element_type=F32)


def lead_dot(first, second):
    return dot(first, second, ((0,), (0,)))


def back_dot(first, second):
    return dot(first, second, ((1,), (1,)))


def exact_dot(picks, values):
    high = values.astype(BF16)
    low = (values - high.astype(F32)).astype(BF16)
    return dot(picks, high) + dot(picks, low)


def gelu_and_slope(values):
    square = values * values
    tanh = jnp.tanh(0.7978845608028654 * (values + 0.044715 * values * square))
    cdf = 0.5 * (1.0 + tanh)
    inner_slope = 0.7978845608028654 * (1.0 + 3.0 * 0.044715 * square)
    return values * cdf, cdf + 0.5 * values * (1.0 - tanh * tanh) * inner_slope


def vmem(count):
    return [pl.BlockSpec(memory_space=VMEM)] * count


def write_picks(self_ref, near_ref, back, pick):
    def counts(ids):
        total = jnp.zeros(spots.shape, F32)
        for offset in range(ids.shape[0]):
            total += (spots == ids[pl.ds(offset, 1), :]).astype(F32)
        return total

    spots = lax.broadcasted_iota(jnp.int32, (back.shape[0], self_ref.shape[1]), 0)
    both = jnp.concatenate([counts(self_ref), counts(near_ref)], axis=1)
    back[...] = both.astype(BF16)
    pick[...] = both.T.astype(BF16)


def gather_kernel(
    place_ref,
    own_ref,
    other_ref,
    self_ref,
    near_ref,
    out_ref,
    own,
    other,
    self_ids,
    near_ids,
    table,
    rows,
    sems,
    id_sems,
):
    core = place_ref[0]
    nodes = own_ref.shape[1]
    targets = self_ref.shape[0]
    fan = near_ref.shape[0] // targets
    chips = out_ref.shape[0]
    cap = targets // (2 * chips)
    width = nodes // TABLE_PIECES

    fetches = []
    for piece in range(TABLE_PIECES):
        spot = pl.ds(piece * width, width)
        for slot, (source, held) in enumerate(((own_ref, own), (other_ref, other))):
            fetch = pltpu.make_async_copy(source.at[:, spot], held.at[:, spot], sems.at[slot, piece])
            fetch.start()
            fetches.append(fetch)
    id_fetches = [
        pltpu.make_async_copy(self_ref, self_ids, id_sems.at[0]),
        pltpu.make_async_copy(near_ref, near_ids, id_sems.at[1]),
    ]
    for fetch in id_fetches:
        fetch.start()

    for piece in range(TABLE_PIECES):
        fetches[2 * piece].wait()
        fetches[2 * piece + 1].wait()

        @pl.loop(0, width // LANES, unroll=4)
        def _(block):
            spot = pl.ds(pl.multiple_of(piece * width + block * LANES, LANES), LANES)
            table[spot, :] = jnp.concatenate([own[:, spot], other[:, spot]], axis=0).T.astype(F32)

    for fetch in id_fetches:
        fetch.wait()

    @pl.loop(0, chips)
    def _(chip):
        first = (2 * chip + core) * cap

        @pl.loop(0, cap // GATHER_UNROLL)
        def _(group):
            start = group * GATHER_UNROLL
            mine = self_ids.at[pl.ds(first + start, GATHER_UNROLL)]
            others = [near_ids.at[pl.ds(offset * targets + first + start, GATHER_UNROLL)] for offset in range(fan)]
            for step in range(GATHER_UNROLL):
                total = table[pl.ds(others[0][step], 1), :]
                for ids in others[1:]:
                    total = total + table[pl.ds(ids[step], 1), :]
                rows[pl.ds(start + step, 1), :] = table[pl.ds(mine[step], 1), :]
                rows[pl.ds(cap + start + step, 1), :] = total

        half = lax.broadcasted_iota(jnp.int32, (cap, LANES), 1) < LANES // 2
        straight = rows[pl.ds(pl.multiple_of(core * cap, cap), cap), :] * jnp.where(core == 0, 1.0, 1.0 / fan)
        turned = rows[pl.ds(pl.multiple_of((1 - core) * cap, cap), cap), :] * jnp.where(core == 0, 1.0 / fan, 1.0)
        turned = pltpu.roll(turned, LANES // 2, 1)
        out_ref[chip, pl.ds(0, cap), :] = jnp.where(half, straight, turned).astype(BF16)
        out_ref[chip, pl.ds(cap, cap), :] = jnp.where(half, turned, straight).astype(BF16)


def gather_rows(place, own_table, other_table, self_one, near_one, chips):
    features, nodes = own_table.shape
    targets = self_one.shape[0]
    near_one = near_one.reshape(-1)
    cap = targets // (2 * chips)
    return pl.pallas_call(
        gather_kernel,
        out_shape=jax.ShapeDtypeStruct((chips, 2 * cap, LANES), BF16),
        in_specs=[pl.BlockSpec(memory_space=SMEM)] + [pl.BlockSpec(memory_space=pl.ANY)] * 4,
        out_specs=pl.BlockSpec(memory_space=VMEM),
        scratch_shapes=[
            VMEM((features, nodes), BF16),
            VMEM((features, nodes), BF16),
            SMEM(self_one.shape, jnp.int32),
            SMEM(near_one.shape, jnp.int32),
            VMEM((nodes, LANES), F32),
            VMEM((2 * cap, LANES), F32),
            pltpu.SemaphoreType.DMA((2, TABLE_PIECES)),
            pltpu.SemaphoreType.DMA((2,)),
        ],
        compiler_params=pltpu.CompilerParams(vmem_limit_bytes=24 << 20),
        cost_estimate=pl.CostEstimate(flops=1 << 27, bytes_accessed=40 << 20, transcendentals=0),
        name="gather_rows",
    )(place, own_table, other_table, self_one, near_one)


def spread_kernel(part_ref, out_ref, sems):
    copies = [pltpu.make_async_copy(part_ref, out_ref.at[chip], sems.at[chip]) for chip in range(out_ref.shape[0])]
    for copy in copies:
        copy.start()
    for copy in copies:
        copy.wait()


def spread(part, chips):
    return pl.pallas_call(
        spread_kernel,
        out_shape=jax.ShapeDtypeStruct((chips,) + part.shape, part.dtype),
        in_specs=vmem(1),
        out_specs=pl.BlockSpec(memory_space=pl.ANY),
        scratch_shapes=[pltpu.SemaphoreType.DMA((chips,))],
        name="spread",
    )(part)


def picks_kernel(self_two_ref, near_two_ref, self_three_ref, near_three_ref, back_two, pick_two, back_three, pick_three):
    write_picks(self_two_ref, near_two_ref, back_two, pick_two)
    write_picks(self_three_ref, near_three_ref, back_three, pick_three)


def make_picks(self_two, near_two, self_three, near_three, cap):
    mid_rows = self_two.shape[0]
    seeds = self_three.shape[0]
    shapes = [(cap, 2 * mid_rows), (2 * mid_rows, cap), (mid_rows, 2 * seeds), (2 * seeds, mid_rows)]
    return pl.pallas_call(
        picks_kernel,
        out_shape=tuple(jax.ShapeDtypeStruct(shape, BF16) for shape in shapes),
        in_specs=vmem(4),
        out_specs=tuple(vmem(4)),
        compiler_params=pltpu.CompilerParams(vmem_limit_bytes=8 << 20),
        name="make_picks",
    )(self_two.reshape(1, -1), near_two, self_three.reshape(1, -1), near_three)


def owner_kernel(
    fan_two,
    fan_three,
    place_ref,
    count_ref,
    counts_ref,
    rows_ref,
    w_own_ref,
    w_other_ref,
    bias_one_ref,
    pick_two,
    back_three,
    pick_three,
    targets_ref,
    w_two_ref,
    bias_two_ref,
    w_three_ref,
    bias_three_ref,
    slope_one,
    two_ref,
    mids,
    tops,
    logit_ref,
    ship_ref,
):
    core = place_ref[0]
    owner = place_ref[1]
    chips = rows_ref.shape[0]
    cap, hidden = slope_one.shape
    labels = w_three_ref.shape[1]
    mid_rows = mids.shape[1]
    seeds = tops.shape[1]
    half = LANES // 2
    front = pl.ds(pl.multiple_of(core * half, half), half)
    back = pl.ds(pl.multiple_of((1 - core) * half, half), half)

    total = None
    for chip in range(chips):
        wide = jnp.concatenate([rows_ref[chip, pl.ds(0, cap), :], rows_ref[chip, pl.ds(cap, cap), :]], axis=1)
        depth = [
            w_own_ref[chip, front, :],
            w_own_ref[chip, back, :],
            w_other_ref[chip, back, :],
            w_other_ref[chip, front, :],
        ]
        part = dot(wide, jnp.concatenate(depth, axis=0))
        total = part if total is None else total + part
    hidden_one, slope = gelu_and_slope(total + bias_one_ref[...])
    slope_one[...] = slope

    mid = dot(pick_two[...], hidden_one.astype(BF16))
    self_mid = mid[:mid_rows].astype(BF16)
    near_mid = (mid[mid_rows:] / fan_two).astype(BF16)
    mids[0] = self_mid
    mids[1] = near_mid
    pre_two = dot(self_mid, w_two_ref[0]) + dot(near_mid, w_two_ref[1]) + bias_two_ref[...]
    hidden_two, slope_two = gelu_and_slope(pre_two)

    top = dot(pick_three[...], hidden_two.astype(BF16))
    self_top = top[:seeds].astype(BF16)
    near_top = (top[seeds:] / fan_three).astype(BF16)
    tops[0] = self_top
    tops[1] = near_top
    logits = back_dot(self_top, w_three_ref[0]) + back_dot(near_top, w_three_ref[1]) + bias_three_ref[...]

    scale = 1.0 / jnp.sqrt(jnp.sum(counts_ref[...].astype(F32), axis=1, keepdims=True))
    live = lax.broadcasted_iota(jnp.int32, (seeds, labels), 0) < count_ref[owner]
    slope = jax.nn.sigmoid(logits) - targets_ref[...].astype(F32)
    logit_grad = jnp.where(live, slope * scale, 0.0).astype(BF16)

    grads = [dot(logit_grad, w_three_ref[0]), dot(logit_grad, w_three_ref[1]) / fan_three]
    upstream = exact_dot(back_three[...], jnp.concatenate(grads, axis=0))
    pre_grad_two = (slope_two * upstream).astype(BF16)

    wide_logit = jnp.concatenate([logit_grad, jnp.zeros((seeds, LANES - labels), BF16)], axis=1)
    two_ref[...] = pre_grad_two
    logit_ref[...] = wide_logit
    ship_ref[pl.ds(0, mid_rows), :] = mids[1 - core]
    ship_ref[pl.ds(mid_rows, mid_rows), :] = pre_grad_two
    ship_ref[pl.ds(2 * mid_rows, seeds), :] = tops[1 - core]
    ship_ref[pl.ds(2 * mid_rows + seeds, seeds), pl.ds(0, LANES)] = wide_logit


def first_kernel(fan_two, slope_one, two_ref, back_two, w_two_ref, one_ref):
    grads = [back_dot(two_ref[...], w_two_ref[0]), back_dot(two_ref[...], w_two_ref[1]) / fan_two]
    upstream = exact_dot(back_two[...], jnp.concatenate(grads, axis=0))
    one_ref[...] = (slope_one[...] * upstream).astype(BF16)


def first_grad(slope_one, two, back_two, w_two, fan_two):
    return pl.pallas_call(
        functools.partial(first_kernel, fan_two),
        out_shape=jax.ShapeDtypeStruct(slope_one.shape, BF16),
        in_specs=vmem(4),
        out_specs=pl.BlockSpec(memory_space=VMEM),
        compiler_params=pltpu.CompilerParams(vmem_limit_bytes=24 << 20),
        cost_estimate=pl.CostEstimate(flops=1 << 29, bytes_accessed=4 << 20, transcendentals=0),
        name="first_grad",
    )(slope_one, two, back_two, w_two)


def late_kernel(place_ref, two_ref, mids, tops, logit_ref, ship_ref, one_ref, parts_ref):
    core = place_ref[0]
    hidden = one_ref.shape[1]
    mid_rows = two_ref.shape[0]
    seeds = logit_ref.shape[0]
    tiles = hidden // LANES
    count = hidden // PEERS
    other_mid = ship_ref[pl.ds(0, mid_rows), :]
    other_two = ship_ref[pl.ds(mid_rows, mid_rows), :]
    other_top = ship_ref[pl.ds(2 * mid_rows, seeds), :]
    other_logit = ship_ref[pl.ds(2 * mid_rows + seeds, seeds), pl.ds(0, LANES)]
    both_two = jnp.concatenate([two_ref[...], other_two], axis=0)
    two = lead_dot(jnp.concatenate([mids[core], other_mid], axis=0), both_two)
    both_logit = jnp.concatenate([logit_ref[...], other_logit], axis=0)
    top = lead_dot(both_logit, jnp.concatenate([tops[core], other_top], axis=0))
    bias_three = jnp.sum(logit_ref[...].astype(F32), axis=0, keepdims=True)
    biases = [
        jnp.sum(one_ref[...].astype(F32), axis=0, keepdims=True),
        jnp.sum(two_ref[...].astype(F32), axis=0, keepdims=True),
        jnp.concatenate([bias_three, jnp.zeros((1, hidden - LANES), F32)], axis=1),
        jnp.zeros((SPARE - 3, hidden), F32),
    ]
    top = jnp.concatenate([top[: LANES - SPARE]] + biases, axis=0).T
    for peer in range(PEERS):
        late = [
            two[peer * count : (peer + 1) * count, tile * LANES : (tile + 1) * LANES] for tile in range(tiles)
        ]
        late.append(top[peer * count : (peer + 1) * count, :])
        parts_ref[peer, pl.ds(ONE_ROWS, LATE_ROWS), :] = jnp.concatenate(late, axis=0).astype(BF16)


def late_products(place, one, grads):
    return pl.pallas_call(
        late_kernel,
        out_shape=jax.ShapeDtypeStruct((PEERS, CHUNK_ROWS, LANES), BF16),
        in_specs=[pl.BlockSpec(memory_space=SMEM)] + vmem(1 + len(grads)),
        out_specs=pl.BlockSpec(memory_space=VMEM),
        compiler_params=pltpu.CompilerParams(vmem_limit_bytes=24 << 20),
        cost_estimate=pl.CostEstimate(flops=1 << 29, bytes_accessed=4 << 20, transcendentals=0),
        name="late_products",
    )(place, *grads, one)


def one_kernel(rows_ref, other_rows_ref, one_ref, other_one_ref, late_ref, parts_ref):
    chips = rows_ref.shape[0]
    cap, hidden = one_ref.shape
    count = hidden // PEERS
    mine = pl.ds(0, cap)
    theirs = pl.ds(cap, cap)
    flipped = jnp.concatenate([one_ref[...].T, other_one_ref[...].T], axis=1)
    for pair in range(chips // 2):
        blocks = [
            jnp.concatenate([rows_ref[chip, mine, :], other_rows_ref[chip, theirs, :]], axis=0)
            for chip in (2 * pair, 2 * pair + 1)
        ]
        block = dot(flipped, jnp.concatenate(blocks, axis=1))
        for peer in range(PEERS):
            line = block[peer * count : (peer + 1) * count]
            cell = jnp.concatenate([line[:, :LANES], line[:, LANES:]], axis=0)
            parts_ref[peer, pl.ds(pair * 2 * SUB, 2 * SUB), :] = cell.astype(BF16)


def one_products(rows, other_rows, one, other_one, late):
    return pl.pallas_call(
        one_kernel,
        out_shape=jax.ShapeDtypeStruct(late.shape, BF16),
        in_specs=vmem(5),
        out_specs=pl.BlockSpec(memory_space=VMEM),
        input_output_aliases={4: 0},
        compiler_params=pltpu.CompilerParams(vmem_limit_bytes=24 << 20),
        cost_estimate=pl.CostEstimate(flops=1 << 30, bytes_accessed=8 << 20, transcendentals=0),
        name="one_products",
    )(rows, other_rows, one, other_one, late)


def owner_pass(place, seed_count, rows, w_own, w_other, bias_one, picks, targets, w_two, bias_two, w_three, bias_three,
               fans):
    hidden = w_two.shape[2]
    labels = w_three.shape[2]
    cap = picks[1].shape[1]
    mid_rows = picks[2].shape[0]
    seeds = targets.shape[0]
    return pl.pallas_call(
        functools.partial(owner_kernel, *fans),
        out_shape=(
            jax.ShapeDtypeStruct((cap, hidden), F32),
            jax.ShapeDtypeStruct((mid_rows, hidden), BF16),
            jax.ShapeDtypeStruct((2, mid_rows, hidden), BF16),
            jax.ShapeDtypeStruct((2, seeds, hidden), BF16),
            jax.ShapeDtypeStruct((seeds, LANES), BF16),
            jax.ShapeDtypeStruct((2 * (mid_rows + seeds), hidden), BF16),
        ),
        in_specs=[pl.BlockSpec(memory_space=SMEM)] * 2 + vmem(13),
        out_specs=tuple(vmem(6)),
        compiler_params=pltpu.CompilerParams(vmem_limit_bytes=24 << 20),
        cost_estimate=pl.CostEstimate(flops=1 << 31, bytes_accessed=10 << 20, transcendentals=1 << 19),
        name="owner_pass",
    )(
        place, seed_count, seed_count.reshape(1, -1), rows, w_own, w_other, bias_one.reshape(1, -1), *picks[1:],
        targets, w_two, bias_two.reshape(1, -1), jnp.transpose(w_three, (0, 2, 1)), bias_three.reshape(1, -1),
    )


def sum_kernel(parts_ref, out_ref):
    total = parts_ref[0].astype(F32)
    for peer in range(1, PEERS):
        total = total + parts_ref[peer].astype(F32)
    late = total[ONE_ROWS:]
    chips = ONE_ROWS // SUB
    for chip in range(chips):
        block = jnp.concatenate([total[chip * SUB : (chip + 1) * SUB], late], axis=0).astype(BF16)
        for group in range(PEERS // chips):
            out_ref[group * chips + chip] = block


def sum_parts(parts):
    return pl.pallas_call(
        sum_kernel,
        out_shape=jax.ShapeDtypeStruct((PEERS, SUB + LATE_ROWS, LANES), BF16),
        in_specs=vmem(1),
        out_specs=pl.BlockSpec(memory_space=VMEM),
        compiler_params=pltpu.CompilerParams(vmem_limit_bytes=24 << 20),
        name="sum_parts",
    )(parts)


def write_late(ref, side, grad_two, grad_three, two, top, three, sems):
    hidden = two.shape[0]
    labels = three.shape[0]
    count = hidden // PEERS
    pieces = sems.shape[0] - 1
    step = hidden // pieces
    for peer in range(PEERS):
        top[pl.ds(peer * count, count), :] = ref[peer].astype(F32)[SUB + TWO_ROWS :]
    flipped = top[...].T
    three[...] = flipped[:labels]
    copies = [pltpu.make_async_copy(three, grad_three.at[side], sems.at[pieces])]
    copies[0].start()
    for peer in range(PEERS):
        cells = ref[peer].astype(F32)
        for tile in range(hidden // LANES):
            two[pl.ds(peer * count, count), pl.ds(tile * LANES, LANES)] = cells[
                SUB + tile * count : SUB + (tile + 1) * count
            ]
        done = (peer + 1) * count
        if done % step == 0:
            spot = pl.ds(done - step, step)
            copies.append(pltpu.make_async_copy(two.at[spot], grad_two.at[side, spot], sems.at[len(copies) - 1]))
            copies[-1].start()
    return flipped[labels:], copies


def own_kernel(
    place_ref,
    own_ref,
    grad_one,
    grad_two,
    grad_three,
    biases,
    flat,
    one,
    two,
    top,
    three,
    sems,
    one_sem,
):
    cut_rows, hidden = one.shape[1:]
    count = hidden // PEERS
    for peer in range(PEERS):
        flat[pl.ds(peer * count, count), :] = own_ref[peer].astype(F32)[:SUB]
    turned = flat[...].T
    one[place_ref[0]] = turned[:cut_rows]
    one[1 - place_ref[0]] = turned[cut_rows:]
    one_copy = pltpu.make_async_copy(one, grad_one, one_sem)
    one_copy.start()
    kept, copies = write_late(own_ref, place_ref[0], grad_two, grad_three, two, top, three, sems)
    biases[...] = kept
    for copy in [one_copy] + copies:
        copy.wait()


def other_kernel(
    place_ref,
    other_ref,
    biases,
    two_in,
    three_in,
    grad_two,
    grad_three,
    bias_one,
    bias_two,
    bias_three,
    two,
    top,
    three,
    first,
    second,
    third,
    sems,
    bias_sems,
):
    kept, copies = write_late(other_ref, 1 - place_ref[0], grad_two, grad_three, two, top, three, sems)
    kept = kept + biases[...]
    first[...] = kept[0:1]
    second[...] = kept[1:2]
    third[...] = kept[2:3, : three.shape[0]]
    for slot, (held, out) in enumerate(((first, bias_one), (second, bias_two), (third, bias_three))):
        copies.append(pltpu.make_async_copy(held, out, bias_sems.at[slot]))
        copies[-1].start()
    for copy in copies:
        copy.wait()


def unpack_own(place, own, cut_rows, hidden, labels):
    anywhere = pl.BlockSpec(memory_space=pl.ANY)
    return pl.pallas_call(
        own_kernel,
        out_shape=(
            jax.ShapeDtypeStruct((2, cut_rows, hidden), F32),
            jax.ShapeDtypeStruct((2, hidden, hidden), F32),
            jax.ShapeDtypeStruct((2, labels, hidden), F32),
            jax.ShapeDtypeStruct((SPARE, hidden), F32),
        ),
        in_specs=[pl.BlockSpec(memory_space=SMEM)] + vmem(1),
        out_specs=(anywhere,) * 3 + tuple(vmem(1)),
        scratch_shapes=[
            VMEM((hidden, LANES), F32),
            VMEM((2, cut_rows, hidden), F32),
            VMEM((hidden, hidden), F32),
            VMEM((hidden, LANES), F32),
            VMEM((labels, hidden), F32),
            pltpu.SemaphoreType.DMA((9,)),
            pltpu.SemaphoreType.DMA,
        ],
        compiler_params=pltpu.CompilerParams(vmem_limit_bytes=16 << 20),
        cost_estimate=pl.CostEstimate(flops=1 << 22, bytes_accessed=4 << 20, transcendentals=0),
        name="unpack_own",
    )(place, own)


def unpack_other(place, other, biases, grad_two, grad_three):
    hidden = grad_two.shape[2]
    labels = grad_three.shape[1]
    anywhere = pl.BlockSpec(memory_space=pl.ANY)
    return pl.pallas_call(
        other_kernel,
        out_shape=(
            jax.ShapeDtypeStruct(grad_two.shape, F32),
            jax.ShapeDtypeStruct(grad_three.shape, F32),
            jax.ShapeDtypeStruct((1, hidden), F32),
            jax.ShapeDtypeStruct((1, hidden), F32),
            jax.ShapeDtypeStruct((1, labels), F32),
        ),
        in_specs=[pl.BlockSpec(memory_space=SMEM)] + vmem(2) + [anywhere] * 2,
        out_specs=(anywhere,) * 5,
        scratch_shapes=[
            VMEM((hidden, hidden), F32),
            VMEM((hidden, LANES), F32),
            VMEM((labels, hidden), F32),
            VMEM((1, hidden), F32),
            VMEM((1, hidden), F32),
            VMEM((1, labels), F32),
            pltpu.SemaphoreType.DMA((9,)),
            pltpu.SemaphoreType.DMA((3,)),
        ],
        input_output_aliases={3: 0, 4: 1},
        compiler_params=pltpu.CompilerParams(vmem_limit_bytes=16 << 20),
        name="unpack_other",
    )(place, other, biases, grad_two, grad_three)


def exchange(values, axes):
    return lax.all_to_all(values, axes, 0, 0, tiled=True)


def swap_core(values):
    return lax.ppermute(values, "core", [(0, 1), (1, 0)])


def local(
    feat_table,
    self_one,
    near_one,
    self_two,
    near_two,
    self_three,
    near_three,
    targets,
    seed_count,
    w_one,
    bias_one,
    w_two,
    bias_two,
    w_three,
    bias_three,
):
    cut_rows, hidden = w_one.shape[1:]
    labels = w_three.shape[2]
    chips = lax.axis_size(CHIPS)
    cap = self_one.shape[0] // (2 * chips)
    owner = lax.axis_index(DP) * lax.axis_size(CUTS) + lax.axis_index(CUTS)
    place = jnp.stack([lax.axis_index("core"), owner]).astype(jnp.int32)
    other_table = swap_core(feat_table)
    w_own = exchange(spread(w_one.reshape(-1, hidden), chips), CHIPS)
    rows = gather_rows(place, feat_table, other_table, self_one, near_one, chips)
    self_two, rows = lax.optimization_barrier((self_two, rows))
    picks = make_picks(self_two, near_two, self_three, near_three, cap)
    w_own, rows, picks = lax.optimization_barrier((w_own, rows, picks))
    w_other = swap_core(w_own)
    rows = exchange(rows, CHIPS)
    fans = (near_two.shape[0], near_three.shape[0])
    slope_one, *grads, ship = owner_pass(
        place, seed_count, rows, w_own, w_other, bias_one, picks, targets, w_two, bias_two, w_three, bias_three, fans
    )
    rows, ship = lax.optimization_barrier((rows, ship))
    ship = swap_core(ship)
    other_rows = swap_core(rows)
    one = first_grad(slope_one, grads[0], picks[0], w_two, fans[0])
    other_one = swap_core(one)
    late = late_products(place, one, (*grads, ship))
    parts = one_products(rows, other_rows, one, other_one, late)
    sums = sum_parts(exchange(parts, SAME_CORE))
    own = exchange(sums, SAME_CORE)
    other = swap_core(own)
    grad_one, grad_two, grad_three, biases = unpack_own(place, own, cut_rows, hidden, labels)
    grad_two, grad_three, bias_one, bias_two, bias_three = unpack_other(place, other, biases, grad_two, grad_three)
    return (
        grad_one,
        bias_one.reshape(-1),
        grad_two,
        bias_two.reshape(-1),
        jnp.transpose(grad_three, (0, 2, 1)),
        bias_three.reshape(-1),
    )


def solution(mesh):
    fine = Mesh(mesh.devices.reshape(2, 4, 4, 2, 2), ("y_hi", "x", "z", "y_lo", "core"))
    both = DP + CUTS
    return jax.shard_map(
        local,
        mesh=fine,
        in_specs=(
            P(CUTS, DP),
            P(DP),
            P(None, DP),
            P(both),
            P(None, both),
            P(both),
            P(None, both),
            P(both, None),
            P(),
            P(None, CUTS, None),
            P(),
            P(),
            P(),
            P(),
            P(),
        ),
        out_specs=(P(None, CUTS, None), P(), P(), P(), P(), P()),
        check_vma=False,
    )
```

```python
import functools

import jax
import jax.numpy as jnp
from jax import lax
from jax.experimental import pallas as pl
from jax.experimental.pallas import tpu as pltpu
from jax.sharding import Mesh, PartitionSpec as P

BF16 = jnp.bfloat16
F32 = jnp.float32
VMEM = pltpu.VMEM
SMEM = pltpu.SMEM
HBM = pltpu.MemorySpace.HBM

LANES = 128
SUB = 8
SPARE = 16
GATHER_UNROLL = 64
TABLE_PIECES = 16
ONE_ROWS = 64
TWO_ROWS = 32
TOP_ROWS = 8
LATE_ROWS = TWO_ROWS + TOP_ROWS
CHUNK_ROWS = ONE_ROWS + LATE_ROWS
PEERS = 64

DP = ("y_hi", "x")
CUTS = ("z", "y_lo", "core")
CHIPS = ("z", "y_lo")
SAME_CORE = DP + CHIPS


def dot(first, second, contract=((1,), (0,))):
    return lax.dot_general(first, second, (contract, ((), ())), preferred_element_type=F32)


def lead_dot(first, second):
    return dot(first, second, ((0,), (0,)))


def back_dot(first, second):
    return dot(first, second, ((1,), (1,)))


def exact_dot(picks, values):
    high = values.astype(BF16)
    low = (values - high.astype(F32)).astype(BF16)
    return dot(picks, high) + dot(picks, low)


def gelu_and_slope(values):
    square = values * values
    tanh = jnp.tanh(0.7978845608028654 * (values + 0.044715 * values * square))
    cdf = 0.5 * (1.0 + tanh)
    inner_slope = 0.7978845608028654 * (1.0 + 3.0 * 0.044715 * square)
    return values * cdf, cdf + 0.5 * values * (1.0 - tanh * tanh) * inner_slope


def vmem(count):
    return [pl.BlockSpec(memory_space=VMEM)] * count


def write_picks(self_ref, near_ref, back, pick):
    def counts(ids):
        total = jnp.zeros(spots.shape, F32)
        for offset in range(ids.shape[0]):
            total += (spots == ids[pl.ds(offset, 1), :]).astype(F32)
        return total

    spots = lax.broadcasted_iota(jnp.int32, (back.shape[0], self_ref.shape[1]), 0)
    both = jnp.concatenate([counts(self_ref), counts(near_ref)], axis=1)
    back[...] = both.astype(BF16)
    pick[...] = both.T.astype(BF16)


def gather_kernel(
    place_ref,
    own_ref,
    other_ref,
    self_ref,
    near_ref,
    out_ref,
    own,
    other,
    self_ids,
    near_ids,
    table,
    rows,
    sems,
    id_sems,
):
    core = place_ref[0]
    nodes = own_ref.shape[1]
    targets = self_ref.shape[0]
    fan = near_ref.shape[0] // targets
    chips = out_ref.shape[0]
    cap = targets // (2 * chips)
    width = nodes // TABLE_PIECES

    fetches = []
    for piece in range(TABLE_PIECES):
        spot = pl.ds(piece * width, width)
        for slot, (source, held) in enumerate(((own_ref, own), (other_ref, other))):
            fetch = pltpu.make_async_copy(source.at[:, spot], held.at[:, spot], sems.at[slot, piece])
            fetch.start()
            fetches.append(fetch)
    id_fetches = [
        pltpu.make_async_copy(self_ref, self_ids, id_sems.at[0]),
        pltpu.make_async_copy(near_ref, near_ids, id_sems.at[1]),
    ]
    for fetch in id_fetches:
        fetch.start()

    for piece in range(TABLE_PIECES):
        fetches[2 * piece].wait()
        fetches[2 * piece + 1].wait()

        @pl.loop(0, width // LANES, unroll=4)
        def _(block):
            spot = pl.ds(pl.multiple_of(piece * width + block * LANES, LANES), LANES)
            table[spot, :] = jnp.concatenate([own[:, spot], other[:, spot]], axis=0).T.astype(F32)

    for fetch in id_fetches:
        fetch.wait()

    @pl.loop(0, chips)
    def _(chip):
        first = (2 * chip + core) * cap

        @pl.loop(0, cap // GATHER_UNROLL)
        def _(group):
            start = group * GATHER_UNROLL
            mine = self_ids.at[pl.ds(first + start, GATHER_UNROLL)]
            others = [near_ids.at[pl.ds(offset * targets + first + start, GATHER_UNROLL)] for offset in range(fan)]
            for step in range(GATHER_UNROLL):
                total = table[pl.ds(others[0][step], 1), :]
                for ids in others[1:]:
                    total = total + table[pl.ds(ids[step], 1), :]
                rows[pl.ds(start + step, 1), :] = table[pl.ds(mine[step], 1), :]
                rows[pl.ds(cap + start + step, 1), :] = total

        half = lax.broadcasted_iota(jnp.int32, (cap, LANES), 1) < LANES // 2
        straight = rows[pl.ds(pl.multiple_of(core * cap, cap), cap), :] * jnp.where(core == 0, 1.0, 1.0 / fan)
        turned = rows[pl.ds(pl.multiple_of((1 - core) * cap, cap), cap), :] * jnp.where(core == 0, 1.0 / fan, 1.0)
        turned = pltpu.roll(turned, LANES // 2, 1)
        out_ref[chip, pl.ds(0, cap), :] = jnp.where(half, straight, turned).astype(BF16)
        out_ref[chip, pl.ds(cap, cap), :] = jnp.where(half, turned, straight).astype(BF16)


def gather_rows(place, own_table, other_table, self_one, near_one, chips):
    features, nodes = own_table.shape
    targets = self_one.shape[0]
    near_one = near_one.reshape(-1)
    cap = targets // (2 * chips)
    return pl.pallas_call(
        gather_kernel,
        out_shape=jax.ShapeDtypeStruct((chips, 2 * cap, LANES), BF16),
        in_specs=[pl.BlockSpec(memory_space=SMEM)] + [pl.BlockSpec(memory_space=pl.ANY)] * 4,
        out_specs=pl.BlockSpec(memory_space=VMEM),
        scratch_shapes=[
            VMEM((features, nodes), BF16),
            VMEM((features, nodes), BF16),
            SMEM(self_one.shape, jnp.int32),
            SMEM(near_one.shape, jnp.int32),
            VMEM((nodes, LANES), F32),
            VMEM((2 * cap, LANES), F32),
            pltpu.SemaphoreType.DMA((2, TABLE_PIECES)),
            pltpu.SemaphoreType.DMA((2,)),
        ],
        compiler_params=pltpu.CompilerParams(vmem_limit_bytes=24 << 20),
        cost_estimate=pl.CostEstimate(flops=1 << 27, bytes_accessed=40 << 20, transcendentals=0),
        name="gather_rows",
    )(place, own_table, other_table, self_one, near_one)


def spread_kernel(part_ref, out_ref, sems):
    copies = [pltpu.make_async_copy(part_ref, out_ref.at[chip], sems.at[chip]) for chip in range(out_ref.shape[0])]
    for copy in copies:
        copy.start()
    for copy in copies:
        copy.wait()


def spread(part, chips):
    return pl.pallas_call(
        spread_kernel,
        out_shape=jax.ShapeDtypeStruct((chips,) + part.shape, part.dtype),
        in_specs=vmem(1),
        out_specs=pl.BlockSpec(memory_space=pl.ANY),
        scratch_shapes=[pltpu.SemaphoreType.DMA((chips,))],
        name="spread",
    )(part)


def picks_kernel(self_two_ref, near_two_ref, self_three_ref, near_three_ref, back_two, pick_two, back_three, pick_three):
    write_picks(self_two_ref, near_two_ref, back_two, pick_two)
    write_picks(self_three_ref, near_three_ref, back_three, pick_three)


def make_picks(self_two, near_two, self_three, near_three, cap):
    mid_rows = self_two.shape[0]
    seeds = self_three.shape[0]
    shapes = [(cap, 2 * mid_rows), (2 * mid_rows, cap), (mid_rows, 2 * seeds), (2 * seeds, mid_rows)]
    return pl.pallas_call(
        picks_kernel,
        out_shape=tuple(jax.ShapeDtypeStruct(shape, BF16) for shape in shapes),
        in_specs=vmem(4),
        out_specs=tuple(vmem(4)),
        compiler_params=pltpu.CompilerParams(vmem_limit_bytes=8 << 20),
        name="make_picks",
    )(self_two.reshape(1, -1), near_two, self_three.reshape(1, -1), near_three)


def owner_kernel(
    fan_two,
    fan_three,
    place_ref,
    count_ref,
    counts_ref,
    rows_ref,
    w_own_ref,
    w_other_ref,
    bias_one_ref,
    pick_two,
    back_three,
    pick_three,
    targets_ref,
    w_two_ref,
    bias_two_ref,
    w_three_ref,
    bias_three_ref,
    slope_one,
    two_ref,
    mids,
    tops,
    logit_ref,
    ship_ref,
):
    core = place_ref[0]
    owner = place_ref[1]
    chips = rows_ref.shape[0]
    cap, hidden = slope_one.shape
    labels = w_three_ref.shape[1]
    mid_rows = mids.shape[1]
    seeds = tops.shape[1]
    half = LANES // 2
    front = pl.ds(pl.multiple_of(core * half, half), half)
    back = pl.ds(pl.multiple_of((1 - core) * half, half), half)

    total = None
    for chip in range(chips):
        wide = jnp.concatenate([rows_ref[chip, pl.ds(0, cap), :], rows_ref[chip, pl.ds(cap, cap), :]], axis=1)
        depth = [
            w_own_ref[chip, front, :],
            w_own_ref[chip, back, :],
            w_other_ref[chip, back, :],
            w_other_ref[chip, front, :],
        ]
        part = dot(wide, jnp.concatenate(depth, axis=0))
        total = part if total is None else total + part
    hidden_one, slope = gelu_and_slope(total + bias_one_ref[...])
    slope_one[...] = slope

    mid = dot(pick_two[...], hidden_one.astype(BF16))
    self_mid = mid[:mid_rows].astype(BF16)
    near_mid = (mid[mid_rows:] / fan_two).astype(BF16)
    mids[0] = self_mid
    mids[1] = near_mid
    pre_two = dot(self_mid, w_two_ref[0]) + dot(near_mid, w_two_ref[1]) + bias_two_ref[...]
    hidden_two, slope_two = gelu_and_slope(pre_two)

    top = dot(pick_three[...], hidden_two.astype(BF16))
    self_top = top[:seeds].astype(BF16)
    near_top = (top[seeds:] / fan_three).astype(BF16)
    tops[0] = self_top
    tops[1] = near_top
    logits = back_dot(self_top, w_three_ref[0]) + back_dot(near_top, w_three_ref[1]) + bias_three_ref[...]

    scale = 1.0 / jnp.sqrt(jnp.sum(counts_ref[...].astype(F32), axis=1, keepdims=True))
    live = lax.broadcasted_iota(jnp.int32, (seeds, labels), 0) < count_ref[owner]
    slope = jax.nn.sigmoid(logits) - targets_ref[...].astype(F32)
    logit_grad = jnp.where(live, slope * scale, 0.0).astype(BF16)

    grads = [dot(logit_grad, w_three_ref[0]), dot(logit_grad, w_three_ref[1]) / fan_three]
    upstream = exact_dot(back_three[...], jnp.concatenate(grads, axis=0))
    pre_grad_two = (slope_two * upstream).astype(BF16)

    wide_logit = jnp.concatenate([logit_grad, jnp.zeros((seeds, LANES - labels), BF16)], axis=1)
    two_ref[...] = pre_grad_two
    logit_ref[...] = wide_logit
    ship_ref[pl.ds(0, mid_rows), :] = mids[1 - core]
    ship_ref[pl.ds(mid_rows, mid_rows), :] = pre_grad_two
    ship_ref[pl.ds(2 * mid_rows, seeds), :] = tops[1 - core]
    ship_ref[pl.ds(2 * mid_rows + seeds, seeds), pl.ds(0, LANES)] = wide_logit


def first_kernel(fan_two, slope_one, two_ref, back_two, w_two_ref, one_ref):
    grads = [back_dot(two_ref[...], w_two_ref[0]), back_dot(two_ref[...], w_two_ref[1]) / fan_two]
    upstream = exact_dot(back_two[...], jnp.concatenate(grads, axis=0))
    one_ref[...] = (slope_one[...] * upstream).astype(BF16)


def first_grad(slope_one, two, back_two, w_two, fan_two):
    return pl.pallas_call(
        functools.partial(first_kernel, fan_two),
        out_shape=jax.ShapeDtypeStruct(slope_one.shape, BF16),
        in_specs=vmem(4),
        out_specs=pl.BlockSpec(memory_space=VMEM),
        compiler_params=pltpu.CompilerParams(vmem_limit_bytes=24 << 20),
        cost_estimate=pl.CostEstimate(flops=1 << 29, bytes_accessed=4 << 20, transcendentals=0),
        name="first_grad",
    )(slope_one, two, back_two, w_two)


def late_kernel(place_ref, two_ref, mids, tops, logit_ref, ship_ref, one_ref, parts_ref):
    core = place_ref[0]
    hidden = one_ref.shape[1]
    mid_rows = two_ref.shape[0]
    seeds = logit_ref.shape[0]
    tiles = hidden // LANES
    count = hidden // PEERS
    other_mid = ship_ref[pl.ds(0, mid_rows), :]
    other_two = ship_ref[pl.ds(mid_rows, mid_rows), :]
    other_top = ship_ref[pl.ds(2 * mid_rows, seeds), :]
    other_logit = ship_ref[pl.ds(2 * mid_rows + seeds, seeds), pl.ds(0, LANES)]
    both_two = jnp.concatenate([two_ref[...], other_two], axis=0)
    two = lead_dot(jnp.concatenate([mids[core], other_mid], axis=0), both_two)
    both_logit = jnp.concatenate([logit_ref[...], other_logit], axis=0)
    top = lead_dot(both_logit, jnp.concatenate([tops[core], other_top], axis=0))
    bias_three = jnp.sum(logit_ref[...].astype(F32), axis=0, keepdims=True)
    biases = [
        jnp.sum(one_ref[...].astype(F32), axis=0, keepdims=True),
        jnp.sum(two_ref[...].astype(F32), axis=0, keepdims=True),
        jnp.concatenate([bias_three, jnp.zeros((1, hidden - LANES), F32)], axis=1),
        jnp.zeros((SPARE - 3, hidden), F32),
    ]
    top = jnp.concatenate([top[: LANES - SPARE]] + biases, axis=0).T
    for peer in range(PEERS):
        late = [
            two[peer * count : (peer + 1) * count, tile * LANES : (tile + 1) * LANES] for tile in range(tiles)
        ]
        late.append(top[peer * count : (peer + 1) * count, :])
        parts_ref[peer, pl.ds(ONE_ROWS, LATE_ROWS), :] = jnp.concatenate(late, axis=0).astype(BF16)


def late_products(place, one, grads):
    return pl.pallas_call(
        late_kernel,
        out_shape=jax.ShapeDtypeStruct((PEERS, CHUNK_ROWS, LANES), BF16),
        in_specs=[pl.BlockSpec(memory_space=SMEM)] + vmem(1 + len(grads)),
        out_specs=pl.BlockSpec(memory_space=VMEM),
        compiler_params=pltpu.CompilerParams(vmem_limit_bytes=24 << 20),
        cost_estimate=pl.CostEstimate(flops=1 << 29, bytes_accessed=4 << 20, transcendentals=0),
        name="late_products",
    )(place, *grads, one)


def one_kernel(rows_ref, other_rows_ref, one_ref, other_one_ref, late_ref, parts_ref):
    chips = rows_ref.shape[0]
    cap, hidden = one_ref.shape
    count = hidden // PEERS
    mine = pl.ds(0, cap)
    theirs = pl.ds(cap, cap)
    flipped = jnp.concatenate([one_ref[...].T, other_one_ref[...].T], axis=1)
    for pair in range(chips // 2):
        blocks = [
            jnp.concatenate([rows_ref[chip, mine, :], other_rows_ref[chip, theirs, :]], axis=0)
            for chip in (2 * pair, 2 * pair + 1)
        ]
        block = dot(flipped, jnp.concatenate(blocks, axis=1))
        for peer in range(PEERS):
            line = block[peer * count : (peer + 1) * count]
            cell = jnp.concatenate([line[:, :LANES], line[:, LANES:]], axis=0)
            parts_ref[peer, pl.ds(pair * 2 * SUB, 2 * SUB), :] = cell.astype(BF16)


def one_products(rows, other_rows, one, other_one, late):
    return pl.pallas_call(
        one_kernel,
        out_shape=jax.ShapeDtypeStruct(late.shape, BF16),
        in_specs=vmem(5),
        out_specs=pl.BlockSpec(memory_space=VMEM),
        input_output_aliases={4: 0},
        compiler_params=pltpu.CompilerParams(vmem_limit_bytes=24 << 20),
        cost_estimate=pl.CostEstimate(flops=1 << 30, bytes_accessed=8 << 20, transcendentals=0),
        name="one_products",
    )(rows, other_rows, one, other_one, late)


def owner_pass(place, seed_count, rows, w_own, w_other, bias_one, picks, targets, w_two, bias_two, w_three, bias_three,
               fans):
    hidden = w_two.shape[2]
    labels = w_three.shape[2]
    cap = picks[1].shape[1]
    mid_rows = picks[2].shape[0]
    seeds = targets.shape[0]
    return pl.pallas_call(
        functools.partial(owner_kernel, *fans),
        out_shape=(
            jax.ShapeDtypeStruct((cap, hidden), F32),
            jax.ShapeDtypeStruct((mid_rows, hidden), BF16),
            jax.ShapeDtypeStruct((2, mid_rows, hidden), BF16),
            jax.ShapeDtypeStruct((2, seeds, hidden), BF16),
            jax.ShapeDtypeStruct((seeds, LANES), BF16),
            jax.ShapeDtypeStruct((2 * (mid_rows + seeds), hidden), BF16),
        ),
        in_specs=[pl.BlockSpec(memory_space=SMEM)] * 2 + vmem(13),
        out_specs=tuple(vmem(6)),
        compiler_params=pltpu.CompilerParams(vmem_limit_bytes=24 << 20),
        cost_estimate=pl.CostEstimate(flops=1 << 31, bytes_accessed=10 << 20, transcendentals=1 << 19),
        name="owner_pass",
    )(
        place, seed_count, seed_count.reshape(1, -1), rows, w_own, w_other, bias_one.reshape(1, -1), *picks[1:],
        targets, w_two, bias_two.reshape(1, -1), jnp.transpose(w_three, (0, 2, 1)), bias_three.reshape(1, -1),
    )


def sum_kernel(parts_ref, out_ref):
    total = parts_ref[0].astype(F32)
    for peer in range(1, PEERS):
        total = total + parts_ref[peer].astype(F32)
    late = total[ONE_ROWS:]
    chips = ONE_ROWS // SUB
    for chip in range(chips):
        block = jnp.concatenate([total[chip * SUB : (chip + 1) * SUB], late], axis=0).astype(BF16)
        for group in range(PEERS // chips):
            out_ref[group * chips + chip] = block


def sum_parts(parts):
    return pl.pallas_call(
        sum_kernel,
        out_shape=jax.ShapeDtypeStruct((PEERS, SUB + LATE_ROWS, LANES), BF16),
        in_specs=vmem(1),
        out_specs=pl.BlockSpec(memory_space=VMEM),
        compiler_params=pltpu.CompilerParams(vmem_limit_bytes=24 << 20),
        name="sum_parts",
    )(parts)


def write_late(ref, side, grad_two, grad_three, two, top, three, sems):
    hidden = two.shape[0]
    labels = three.shape[0]
    count = hidden // PEERS
    pieces = sems.shape[0] - 1
    step = hidden // pieces
    for peer in range(PEERS):
        top[pl.ds(peer * count, count), :] = ref[peer].astype(F32)[SUB + TWO_ROWS :]
    flipped = top[...].T
    three[...] = flipped[:labels]
    copies = [pltpu.make_async_copy(three, grad_three.at[side], sems.at[pieces])]
    copies[0].start()
    for peer in range(PEERS):
        cells = ref[peer].astype(F32)
        for tile in range(hidden // LANES):
            two[pl.ds(peer * count, count), pl.ds(tile * LANES, LANES)] = cells[
                SUB + tile * count : SUB + (tile + 1) * count
            ]
        done = (peer + 1) * count
        if done % step == 0:
            spot = pl.ds(done - step, step)
            copies.append(pltpu.make_async_copy(two.at[spot], grad_two.at[side, spot], sems.at[len(copies) - 1]))
            copies[-1].start()
    return flipped[labels:], copies


def own_kernel(
    place_ref,
    own_ref,
    grad_one,
    grad_two,
    grad_three,
    biases,
    flat,
    one,
    two,
    top,
    three,
    sems,
    one_sem,
):
    cut_rows, hidden = one.shape[1:]
    count = hidden // PEERS
    for peer in range(PEERS):
        flat[pl.ds(peer * count, count), :] = own_ref[peer].astype(F32)[:SUB]
    turned = flat[...].T
    one[place_ref[0]] = turned[:cut_rows]
    one[1 - place_ref[0]] = turned[cut_rows:]
    one_copy = pltpu.make_async_copy(one, grad_one, one_sem)
    one_copy.start()
    kept, copies = write_late(own_ref, place_ref[0], grad_two, grad_three, two, top, three, sems)
    biases[...] = kept
    for copy in [one_copy] + copies:
        copy.wait()


def other_kernel(
    place_ref,
    other_ref,
    biases,
    two_in,
    three_in,
    grad_two,
    grad_three,
    bias_one,
    bias_two,
    bias_three,
    two,
    top,
    three,
    first,
    second,
    third,
    sems,
    bias_sems,
):
    kept, copies = write_late(other_ref, 1 - place_ref[0], grad_two, grad_three, two, top, three, sems)
    kept = kept + biases[...]
    first[...] = kept[0:1]
    second[...] = kept[1:2]
    third[...] = kept[2:3, : three.shape[0]]
    for slot, (held, out) in enumerate(((first, bias_one), (second, bias_two), (third, bias_three))):
        copies.append(pltpu.make_async_copy(held, out, bias_sems.at[slot]))
        copies[-1].start()
    for copy in copies:
        copy.wait()


def unpack_own(place, own, cut_rows, hidden, labels):
    anywhere = pl.BlockSpec(memory_space=pl.ANY)
    return pl.pallas_call(
        own_kernel,
        out_shape=(
            jax.ShapeDtypeStruct((2, cut_rows, hidden), F32),
            jax.ShapeDtypeStruct((2, hidden, hidden), F32),
            jax.ShapeDtypeStruct((2, labels, hidden), F32),
            jax.ShapeDtypeStruct((SPARE, hidden), F32),
        ),
        in_specs=[pl.BlockSpec(memory_space=SMEM)] + vmem(1),
        out_specs=(anywhere,) * 3 + tuple(vmem(1)),
        scratch_shapes=[
            VMEM((hidden, LANES), F32),
            VMEM((2, cut_rows, hidden), F32),
            VMEM((hidden, hidden), F32),
            VMEM((hidden, LANES), F32),
            VMEM((labels, hidden), F32),
            pltpu.SemaphoreType.DMA((9,)),
            pltpu.SemaphoreType.DMA,
        ],
        compiler_params=pltpu.CompilerParams(vmem_limit_bytes=16 << 20),
        cost_estimate=pl.CostEstimate(flops=1 << 22, bytes_accessed=4 << 20, transcendentals=0),
        name="unpack_own",
    )(place, own)


def unpack_other(place, other, biases, grad_two, grad_three):
    hidden = grad_two.shape[2]
    labels = grad_three.shape[1]
    anywhere = pl.BlockSpec(memory_space=pl.ANY)
    return pl.pallas_call(
        other_kernel,
        out_shape=(
            jax.ShapeDtypeStruct(grad_two.shape, F32),
            jax.ShapeDtypeStruct(grad_three.shape, F32),
            jax.ShapeDtypeStruct((1, hidden), F32),
            jax.ShapeDtypeStruct((1, hidden), F32),
            jax.ShapeDtypeStruct((1, labels), F32),
        ),
        in_specs=[pl.BlockSpec(memory_space=SMEM)] + vmem(2) + [anywhere] * 2,
        out_specs=(anywhere,) * 5,
        scratch_shapes=[
            VMEM((hidden, hidden), F32),
            VMEM((hidden, LANES), F32),
            VMEM((labels, hidden), F32),
            VMEM((1, hidden), F32),
            VMEM((1, hidden), F32),
            VMEM((1, labels), F32),
            pltpu.SemaphoreType.DMA((9,)),
            pltpu.SemaphoreType.DMA((3,)),
        ],
        input_output_aliases={3: 0, 4: 1},
        compiler_params=pltpu.CompilerParams(vmem_limit_bytes=16 << 20),
        name="unpack_other",
    )(place, other, biases, grad_two, grad_three)


def exchange(values, axes):
    return lax.all_to_all(values, axes, 0, 0, tiled=True)


def swap_core(values):
    return lax.ppermute(values, "core", [(0, 1), (1, 0)])


def local(
    feat_table,
    self_one,
    near_one,
    self_two,
    near_two,
    self_three,
    near_three,
    targets,
    seed_count,
    w_one,
    bias_one,
    w_two,
    bias_two,
    w_three,
    bias_three,
):
    cut_rows, hidden = w_one.shape[1:]
    labels = w_three.shape[2]
    chips = lax.axis_size(CHIPS)
    cap = self_one.shape[0] // (2 * chips)
    owner = lax.axis_index(DP) * lax.axis_size(CUTS) + lax.axis_index(CUTS)
    place = jnp.stack([lax.axis_index("core"), owner]).astype(jnp.int32)
    other_table = swap_core(feat_table)
    w_own = exchange(spread(w_one.reshape(-1, hidden), chips), CHIPS)
    rows = gather_rows(place, feat_table, other_table, self_one, near_one, chips)
    self_two, rows = lax.optimization_barrier((self_two, rows))
    picks = make_picks(self_two, near_two, self_three, near_three, cap)
    w_own, rows, picks = lax.optimization_barrier((w_own, rows, picks))
    w_other = swap_core(w_own)
    rows = exchange(rows, CHIPS)
    rows, w_own, w_other = lax.optimization_barrier((rows, w_own, w_other))
    other_rows = swap_core(rows)
    fans = (near_two.shape[0], near_three.shape[0])
    slope_one, *grads, ship = owner_pass(
        place, seed_count, rows, w_own, w_other, bias_one, picks, targets, w_two, bias_two, w_three, bias_three, fans
    )
    ship = swap_core(ship)
    one = first_grad(slope_one, grads[0], picks[0], w_two, fans[0])
    other_one = swap_core(one)
    late = late_products(place, one, (*grads, ship))
    parts = one_products(rows, other_rows, one, other_one, late)
    sums = sum_parts(exchange(parts, SAME_CORE))
    own = exchange(sums, SAME_CORE)
    other = swap_core(own)
    grad_one, grad_two, grad_three, biases = unpack_own(place, own, cut_rows, hidden, labels)
    grad_two, grad_three, bias_one, bias_two, bias_three = unpack_other(place, other, biases, grad_two, grad_three)
    return (
        grad_one,
        bias_one.reshape(-1),
        grad_two,
        bias_two.reshape(-1),
        jnp.transpose(grad_three, (0, 2, 1)),
        bias_three.reshape(-1),
    )


def solution(mesh):
    fine = Mesh(mesh.devices.reshape(2, 4, 4, 2, 2), ("y_hi", "x", "z", "y_lo", "core"))
    both = DP + CUTS
    return jax.shard_map(
        local,
        mesh=fine,
        in_specs=(
            P(CUTS, DP),
            P(DP),
            P(None, DP),
            P(both),
            P(None, both),
            P(both),
            P(None, both),
            P(both, None),
            P(),
            P(None, CUTS, None),
            P(),
            P(),
            P(),
            P(),
            P(),
        ),
        out_specs=(P(None, CUTS, None), P(), P(), P(), P(), P()),
        check_vma=False,
    )
```

```python
import functools

import jax
import jax.numpy as jnp
from jax import lax
from jax.experimental import pallas as pl
from jax.experimental.pallas import tpu as pltpu
from jax.sharding import Mesh, PartitionSpec as P

BF16 = jnp.bfloat16
F32 = jnp.float32
VMEM = pltpu.VMEM
SMEM = pltpu.SMEM
HBM = pltpu.MemorySpace.HBM

LANES = 128
SUB = 8
SPARE = 16
GATHER_UNROLL = 64
TABLE_PIECES = 16
ONE_ROWS = 64
TWO_ROWS = 32
TOP_ROWS = 8
LATE_ROWS = TWO_ROWS + TOP_ROWS
CHUNK_ROWS = ONE_ROWS + LATE_ROWS
PEERS = 64

DP = ("y_hi", "x")
CUTS = ("z", "y_lo", "core")
CHIPS = ("z", "y_lo")
SAME_CORE = DP + CHIPS


def dot(first, second, contract=((1,), (0,))):
    return lax.dot_general(first, second, (contract, ((), ())), preferred_element_type=F32)


def lead_dot(first, second):
    return dot(first, second, ((0,), (0,)))


def back_dot(first, second):
    return dot(first, second, ((1,), (1,)))


def exact_dot(picks, values):
    high = values.astype(BF16)
    low = (values - high.astype(F32)).astype(BF16)
    return dot(jnp.concatenate([picks, picks], axis=1), jnp.concatenate([high, low], axis=0))


def gelu_and_slope(values):
    square = values * values
    tanh = jnp.tanh(0.7978845608028654 * (values + 0.044715 * values * square))
    cdf = 0.5 * (1.0 + tanh)
    inner_slope = 0.7978845608028654 * (1.0 + 3.0 * 0.044715 * square)
    return values * cdf, cdf + 0.5 * values * (1.0 - tanh * tanh) * inner_slope


def vmem(count):
    return [pl.BlockSpec(memory_space=VMEM)] * count


def write_picks(self_ref, near_ref, back, pick):
    def counts(ids):
        total = jnp.zeros(spots.shape, F32)
        for offset in range(ids.shape[0]):
            total += (spots == ids[pl.ds(offset, 1), :]).astype(F32)
        return total

    spots = lax.broadcasted_iota(jnp.int32, (back.shape[0], self_ref.shape[1]), 0)
    both = jnp.concatenate([counts(self_ref), counts(near_ref)], axis=1)
    back[...] = both.astype(BF16)
    pick[...] = both.T.astype(BF16)


def gather_kernel(
    place_ref,
    own_ref,
    other_ref,
    self_ref,
    near_ref,
    out_ref,
    own,
    other,
    self_ids,
    near_ids,
    table,
    rows,
    sems,
    id_sems,
):
    core = place_ref[0]
    nodes = own_ref.shape[1]
    targets = self_ref.shape[0]
    fan = near_ref.shape[0] // targets
    chips = out_ref.shape[0]
    cap = targets // (2 * chips)
    width = nodes // TABLE_PIECES

    fetches = []
    for piece in range(TABLE_PIECES):
        spot = pl.ds(piece * width, width)
        for slot, (source, held) in enumerate(((own_ref, own), (other_ref, other))):
            fetch = pltpu.make_async_copy(source.at[:, spot], held.at[:, spot], sems.at[slot, piece])
            fetch.start()
            fetches.append(fetch)
    id_fetches = [
        pltpu.make_async_copy(self_ref, self_ids, id_sems.at[0]),
        pltpu.make_async_copy(near_ref, near_ids, id_sems.at[1]),
    ]
    for fetch in id_fetches:
        fetch.start()

    for piece in range(TABLE_PIECES):
        fetches[2 * piece].wait()
        fetches[2 * piece + 1].wait()

        @pl.loop(0, width // LANES, unroll=4)
        def _(block):
            spot = pl.ds(pl.multiple_of(piece * width + block * LANES, LANES), LANES)
            table[spot, :] = jnp.concatenate([own[:, spot], other[:, spot]], axis=0).T.astype(F32)

    for fetch in id_fetches:
        fetch.wait()

    @pl.loop(0, chips)
    def _(chip):
        first = (2 * chip + core) * cap

        @pl.loop(0, cap // GATHER_UNROLL)
        def _(group):
            start = group * GATHER_UNROLL
            mine = self_ids.at[pl.ds(first + start, GATHER_UNROLL)]
            others = [near_ids.at[pl.ds(offset * targets + first + start, GATHER_UNROLL)] for offset in range(fan)]
            for step in range(GATHER_UNROLL):
                total = table[pl.ds(others[0][step], 1), :]
                for ids in others[1:]:
                    total = total + table[pl.ds(ids[step], 1), :]
                rows[pl.ds(start + step, 1), :] = table[pl.ds(mine[step], 1), :]
                rows[pl.ds(cap + start + step, 1), :] = total

        half = lax.broadcasted_iota(jnp.int32, (cap, LANES), 1) < LANES // 2
        straight = rows[pl.ds(pl.multiple_of(core * cap, cap), cap), :] * jnp.where(core == 0, 1.0, 1.0 / fan)
        turned = rows[pl.ds(pl.multiple_of((1 - core) * cap, cap), cap), :] * jnp.where(core == 0, 1.0 / fan, 1.0)
        turned = pltpu.roll(turned, LANES // 2, 1)
        out_ref[chip, pl.ds(0, cap), :] = jnp.where(half, straight, turned).astype(BF16)
        out_ref[chip, pl.ds(cap, cap), :] = jnp.where(half, turned, straight).astype(BF16)


def gather_rows(place, own_table, other_table, self_one, near_one, chips):
    features, nodes = own_table.shape
    targets = self_one.shape[0]
    near_one = near_one.reshape(-1)
    cap = targets // (2 * chips)
    return pl.pallas_call(
        gather_kernel,
        out_shape=jax.ShapeDtypeStruct((chips, 2 * cap, LANES), BF16),
        in_specs=[pl.BlockSpec(memory_space=SMEM)] + [pl.BlockSpec(memory_space=pl.ANY)] * 4,
        out_specs=pl.BlockSpec(memory_space=VMEM),
        scratch_shapes=[
            VMEM((features, nodes), BF16),
            VMEM((features, nodes), BF16),
            SMEM(self_one.shape, jnp.int32),
            SMEM(near_one.shape, jnp.int32),
            VMEM((nodes, LANES), F32),
            VMEM((2 * cap, LANES), F32),
            pltpu.SemaphoreType.DMA((2, TABLE_PIECES)),
            pltpu.SemaphoreType.DMA((2,)),
        ],
        compiler_params=pltpu.CompilerParams(vmem_limit_bytes=24 << 20),
        cost_estimate=pl.CostEstimate(flops=1 << 27, bytes_accessed=40 << 20, transcendentals=0),
        name="gather_rows",
    )(place, own_table, other_table, self_one, near_one)


def spread_kernel(part_ref, out_ref, sems):
    copies = [pltpu.make_async_copy(part_ref, out_ref.at[chip], sems.at[chip]) for chip in range(out_ref.shape[0])]
    for copy in copies:
        copy.start()
    for copy in copies:
        copy.wait()


def spread(part, chips):
    return pl.pallas_call(
        spread_kernel,
        out_shape=jax.ShapeDtypeStruct((chips,) + part.shape, part.dtype),
        in_specs=vmem(1),
        out_specs=pl.BlockSpec(memory_space=pl.ANY),
        scratch_shapes=[pltpu.SemaphoreType.DMA((chips,))],
        name="spread",
    )(part)


def picks_kernel(self_two_ref, near_two_ref, self_three_ref, near_three_ref, back_two, pick_two, back_three, pick_three):
    write_picks(self_two_ref, near_two_ref, back_two, pick_two)
    write_picks(self_three_ref, near_three_ref, back_three, pick_three)


def make_picks(self_two, near_two, self_three, near_three, cap):
    mid_rows = self_two.shape[0]
    seeds = self_three.shape[0]
    shapes = [(cap, 2 * mid_rows), (2 * mid_rows, cap), (mid_rows, 2 * seeds), (2 * seeds, mid_rows)]
    return pl.pallas_call(
        picks_kernel,
        out_shape=tuple(jax.ShapeDtypeStruct(shape, BF16) for shape in shapes),
        in_specs=vmem(4),
        out_specs=tuple(vmem(4)),
        compiler_params=pltpu.CompilerParams(vmem_limit_bytes=8 << 20),
        name="make_picks",
    )(self_two.reshape(1, -1), near_two, self_three.reshape(1, -1), near_three)


def owner_kernel(
    fan_two,
    fan_three,
    place_ref,
    count_ref,
    counts_ref,
    rows_ref,
    w_own_ref,
    w_other_ref,
    bias_one_ref,
    pick_two,
    back_three,
    pick_three,
    targets_ref,
    w_two_ref,
    bias_two_ref,
    w_three_ref,
    bias_three_ref,
    slope_one,
    two_ref,
    mids,
    tops,
    logit_ref,
    ship_ref,
):
    core = place_ref[0]
    owner = place_ref[1]
    chips = rows_ref.shape[0]
    cap, hidden = slope_one.shape
    labels = w_three_ref.shape[1]
    mid_rows = mids.shape[1]
    seeds = tops.shape[1]
    half = LANES // 2
    front = pl.ds(pl.multiple_of(core * half, half), half)
    back = pl.ds(pl.multiple_of((1 - core) * half, half), half)

    wides = [rows_ref[chip, pl.ds(start, cap), :] for chip in range(chips) for start in (0, cap)]
    depths = [
        weights[chip, spot, :]
        for chip in range(chips)
        for weights, spot in ((w_own_ref, front), (w_own_ref, back), (w_other_ref, back), (w_other_ref, front))
    ]
    total = dot(jnp.concatenate(wides, axis=1), jnp.concatenate(depths, axis=0))
    hidden_one, slope = gelu_and_slope(total + bias_one_ref[...])
    slope_one[...] = slope

    mid = dot(pick_two[...], hidden_one.astype(BF16))
    self_mid = mid[:mid_rows].astype(BF16)
    near_mid = (mid[mid_rows:] / fan_two).astype(BF16)
    mids[0] = self_mid
    mids[1] = near_mid
    both = jnp.concatenate([self_mid, near_mid], axis=1)
    pre_two = dot(both, jnp.concatenate([w_two_ref[0], w_two_ref[1]], axis=0)) + bias_two_ref[...]
    hidden_two, slope_two = gelu_and_slope(pre_two)

    top = dot(pick_three[...], hidden_two.astype(BF16))
    self_top = top[:seeds].astype(BF16)
    near_top = (top[seeds:] / fan_three).astype(BF16)
    tops[0] = self_top
    tops[1] = near_top
    logits = back_dot(self_top, w_three_ref[0]) + back_dot(near_top, w_three_ref[1]) + bias_three_ref[...]

    scale = 1.0 / jnp.sqrt(jnp.sum(counts_ref[...].astype(F32), axis=1, keepdims=True))
    live = lax.broadcasted_iota(jnp.int32, (seeds, labels), 0) < count_ref[owner]
    slope = jax.nn.sigmoid(logits) - targets_ref[...].astype(F32)
    logit_grad = jnp.where(live, slope * scale, 0.0).astype(BF16)

    grads = [dot(logit_grad, w_three_ref[0]), dot(logit_grad, w_three_ref[1]) / fan_three]
    upstream = exact_dot(back_three[...], jnp.concatenate(grads, axis=0))
    pre_grad_two = (slope_two * upstream).astype(BF16)

    wide_logit = jnp.concatenate([logit_grad, jnp.zeros((seeds, LANES - labels), BF16)], axis=1)
    two_ref[...] = pre_grad_two
    logit_ref[...] = wide_logit
    ship_ref[pl.ds(0, mid_rows), :] = mids[1 - core]
    ship_ref[pl.ds(mid_rows, mid_rows), :] = pre_grad_two
    ship_ref[pl.ds(2 * mid_rows, seeds), :] = tops[1 - core]
    ship_ref[pl.ds(2 * mid_rows + seeds, seeds), pl.ds(0, LANES)] = wide_logit


def first_kernel(fan_two, slope_one, two_ref, back_two, w_two_ref, one_ref):
    grads = [back_dot(two_ref[...], w_two_ref[0]), back_dot(two_ref[...], w_two_ref[1]) / fan_two]
    upstream = exact_dot(back_two[...], jnp.concatenate(grads, axis=0))
    one_ref[...] = (slope_one[...] * upstream).astype(BF16)


def first_grad(slope_one, two, back_two, w_two, fan_two):
    return pl.pallas_call(
        functools.partial(first_kernel, fan_two),
        out_shape=jax.ShapeDtypeStruct(slope_one.shape, BF16),
        in_specs=vmem(4),
        out_specs=pl.BlockSpec(memory_space=VMEM),
        compiler_params=pltpu.CompilerParams(vmem_limit_bytes=24 << 20),
        cost_estimate=pl.CostEstimate(flops=1 << 29, bytes_accessed=4 << 20, transcendentals=0),
        name="first_grad",
    )(slope_one, two, back_two, w_two)


def late_kernel(place_ref, two_ref, mids, tops, logit_ref, ship_ref, one_ref, parts_ref):
    core = place_ref[0]
    hidden = one_ref.shape[1]
    mid_rows = two_ref.shape[0]
    seeds = logit_ref.shape[0]
    tiles = hidden // LANES
    count = hidden // PEERS
    other_mid = ship_ref[pl.ds(0, mid_rows), :]
    other_two = ship_ref[pl.ds(mid_rows, mid_rows), :]
    other_top = ship_ref[pl.ds(2 * mid_rows, seeds), :]
    other_logit = ship_ref[pl.ds(2 * mid_rows + seeds, seeds), pl.ds(0, LANES)]
    both_two = jnp.concatenate([two_ref[...], other_two], axis=0)
    two = lead_dot(jnp.concatenate([mids[core], other_mid], axis=0), both_two)
    both_logit = jnp.concatenate([logit_ref[...], other_logit], axis=0)
    top = lead_dot(both_logit, jnp.concatenate([tops[core], other_top], axis=0))
    bias_three = jnp.sum(logit_ref[...].astype(F32), axis=0, keepdims=True)
    biases = [
        jnp.sum(one_ref[...].astype(F32), axis=0, keepdims=True),
        jnp.sum(two_ref[...].astype(F32), axis=0, keepdims=True),
        jnp.concatenate([bias_three, jnp.zeros((1, hidden - LANES), F32)], axis=1),
        jnp.zeros((SPARE - 3, hidden), F32),
    ]
    top = jnp.concatenate([top[: LANES - SPARE]] + biases, axis=0).T
    for peer in range(PEERS):
        late = [
            two[peer * count : (peer + 1) * count, tile * LANES : (tile + 1) * LANES] for tile in range(tiles)
        ]
        late.append(top[peer * count : (peer + 1) * count, :])
        parts_ref[peer, pl.ds(ONE_ROWS, LATE_ROWS), :] = jnp.concatenate(late, axis=0).astype(BF16)


def late_products(place, one, grads):
    return pl.pallas_call(
        late_kernel,
        out_shape=jax.ShapeDtypeStruct((PEERS, CHUNK_ROWS, LANES), BF16),
        in_specs=[pl.BlockSpec(memory_space=SMEM)] + vmem(1 + len(grads)),
        out_specs=pl.BlockSpec(memory_space=VMEM),
        compiler_params=pltpu.CompilerParams(vmem_limit_bytes=24 << 20),
        cost_estimate=pl.CostEstimate(flops=1 << 29, bytes_accessed=4 << 20, transcendentals=0),
        name="late_products",
    )(place, *grads, one)


def one_kernel(rows_ref, other_rows_ref, one_ref, other_one_ref, late_ref, parts_ref):
    chips = rows_ref.shape[0]
    cap, hidden = one_ref.shape
    count = hidden // PEERS
    mine = pl.ds(0, cap)
    theirs = pl.ds(cap, cap)
    flipped = jnp.concatenate([one_ref[...].T, other_one_ref[...].T], axis=1)
    for pair in range(chips // 2):
        blocks = [
            jnp.concatenate([rows_ref[chip, mine, :], other_rows_ref[chip, theirs, :]], axis=0)
            for chip in (2 * pair, 2 * pair + 1)
        ]
        block = dot(flipped, jnp.concatenate(blocks, axis=1))
        for peer in range(PEERS):
            line = block[peer * count : (peer + 1) * count]
            cell = jnp.concatenate([line[:, :LANES], line[:, LANES:]], axis=0)
            parts_ref[peer, pl.ds(pair * 2 * SUB, 2 * SUB), :] = cell.astype(BF16)


def one_products(rows, other_rows, one, other_one, late):
    return pl.pallas_call(
        one_kernel,
        out_shape=jax.ShapeDtypeStruct(late.shape, BF16),
        in_specs=vmem(5),
        out_specs=pl.BlockSpec(memory_space=VMEM),
        input_output_aliases={4: 0},
        compiler_params=pltpu.CompilerParams(vmem_limit_bytes=24 << 20),
        cost_estimate=pl.CostEstimate(flops=1 << 30, bytes_accessed=8 << 20, transcendentals=0),
        name="one_products",
    )(rows, other_rows, one, other_one, late)


def owner_pass(place, seed_count, rows, w_own, w_other, bias_one, picks, targets, w_two, bias_two, w_three, bias_three,
               fans):
    hidden = w_two.shape[2]
    labels = w_three.shape[2]
    cap = picks[1].shape[1]
    mid_rows = picks[2].shape[0]
    seeds = targets.shape[0]
    return pl.pallas_call(
        functools.partial(owner_kernel, *fans),
        out_shape=(
            jax.ShapeDtypeStruct((cap, hidden), F32),
            jax.ShapeDtypeStruct((mid_rows, hidden), BF16),
            jax.ShapeDtypeStruct((2, mid_rows, hidden), BF16),
            jax.ShapeDtypeStruct((2, seeds, hidden), BF16),
            jax.ShapeDtypeStruct((seeds, LANES), BF16),
            jax.ShapeDtypeStruct((2 * (mid_rows + seeds), hidden), BF16),
        ),
        in_specs=[pl.BlockSpec(memory_space=SMEM)] * 2 + vmem(13),
        out_specs=tuple(vmem(6)),
        compiler_params=pltpu.CompilerParams(vmem_limit_bytes=24 << 20),
        cost_estimate=pl.CostEstimate(flops=1 << 31, bytes_accessed=10 << 20, transcendentals=1 << 19),
        name="owner_pass",
    )(
        place, seed_count, seed_count.reshape(1, -1), rows, w_own, w_other, bias_one.reshape(1, -1), *picks[1:],
        targets, w_two, bias_two.reshape(1, -1), jnp.transpose(w_three, (0, 2, 1)), bias_three.reshape(1, -1),
    )


def sum_kernel(parts_ref, out_ref):
    total = parts_ref[0].astype(F32)
    for peer in range(1, PEERS):
        total = total + parts_ref[peer].astype(F32)
    late = total[ONE_ROWS:]
    chips = ONE_ROWS // SUB
    for chip in range(chips):
        block = jnp.concatenate([total[chip * SUB : (chip + 1) * SUB], late], axis=0).astype(BF16)
        for group in range(PEERS // chips):
            out_ref[group * chips + chip] = block


def sum_parts(parts):
    return pl.pallas_call(
        sum_kernel,
        out_shape=jax.ShapeDtypeStruct((PEERS, SUB + LATE_ROWS, LANES), BF16),
        in_specs=vmem(1),
        out_specs=pl.BlockSpec(memory_space=VMEM),
        compiler_params=pltpu.CompilerParams(vmem_limit_bytes=24 << 20),
        name="sum_parts",
    )(parts)


def write_late(ref, side, grad_two, grad_three, two, top, three, sems):
    hidden = two.shape[0]
    labels = three.shape[0]
    count = hidden // PEERS
    pieces = sems.shape[0] - 1
    step = hidden // pieces
    for peer in range(PEERS):
        top[pl.ds(peer * count, count), :] = ref[peer].astype(F32)[SUB + TWO_ROWS :]
    flipped = top[...].T
    three[...] = flipped[:labels]
    copies = [pltpu.make_async_copy(three, grad_three.at[side], sems.at[pieces])]
    copies[0].start()
    for peer in range(PEERS):
        cells = ref[peer].astype(F32)
        for tile in range(hidden // LANES):
            two[pl.ds(peer * count, count), pl.ds(tile * LANES, LANES)] = cells[
                SUB + tile * count : SUB + (tile + 1) * count
            ]
        done = (peer + 1) * count
        if done % step == 0:
            spot = pl.ds(done - step, step)
            copies.append(pltpu.make_async_copy(two.at[spot], grad_two.at[side, spot], sems.at[len(copies) - 1]))
            copies[-1].start()
    return flipped[labels:], copies


def own_kernel(
    place_ref,
    own_ref,
    grad_one,
    grad_two,
    grad_three,
    biases,
    flat,
    one,
    two,
    top,
    three,
    sems,
    one_sem,
):
    cut_rows, hidden = one.shape[1:]
    count = hidden // PEERS
    for peer in range(PEERS):
        flat[pl.ds(peer * count, count), :] = own_ref[peer].astype(F32)[:SUB]
    turned = flat[...].T
    one[place_ref[0]] = turned[:cut_rows]
    one[1 - place_ref[0]] = turned[cut_rows:]
    one_copy = pltpu.make_async_copy(one, grad_one, one_sem)
    one_copy.start()
    kept, copies = write_late(own_ref, place_ref[0], grad_two, grad_three, two, top, three, sems)
    biases[...] = kept
    for copy in [one_copy] + copies:
        copy.wait()


def other_kernel(
    place_ref,
    other_ref,
    biases,
    two_in,
    three_in,
    grad_two,
    grad_three,
    bias_one,
    bias_two,
    bias_three,
    two,
    top,
    three,
    first,
    second,
    third,
    sems,
    bias_sems,
):
    kept, copies = write_late(other_ref, 1 - place_ref[0], grad_two, grad_three, two, top, three, sems)
    kept = kept + biases[...]
    first[...] = kept[0:1]
    second[...] = kept[1:2]
    third[...] = kept[2:3, : three.shape[0]]
    for slot, (held, out) in enumerate(((first, bias_one), (second, bias_two), (third, bias_three))):
        copies.append(pltpu.make_async_copy(held, out, bias_sems.at[slot]))
        copies[-1].start()
    for copy in copies:
        copy.wait()


def unpack_own(place, own, cut_rows, hidden, labels):
    anywhere = pl.BlockSpec(memory_space=pl.ANY)
    return pl.pallas_call(
        own_kernel,
        out_shape=(
            jax.ShapeDtypeStruct((2, cut_rows, hidden), F32),
            jax.ShapeDtypeStruct((2, hidden, hidden), F32),
            jax.ShapeDtypeStruct((2, labels, hidden), F32),
            jax.ShapeDtypeStruct((SPARE, hidden), F32),
        ),
        in_specs=[pl.BlockSpec(memory_space=SMEM)] + vmem(1),
        out_specs=(anywhere,) * 3 + tuple(vmem(1)),
        scratch_shapes=[
            VMEM((hidden, LANES), F32),
            VMEM((2, cut_rows, hidden), F32),
            VMEM((hidden, hidden), F32),
            VMEM((hidden, LANES), F32),
            VMEM((labels, hidden), F32),
            pltpu.SemaphoreType.DMA((9,)),
            pltpu.SemaphoreType.DMA,
        ],
        compiler_params=pltpu.CompilerParams(vmem_limit_bytes=16 << 20),
        cost_estimate=pl.CostEstimate(flops=1 << 22, bytes_accessed=4 << 20, transcendentals=0),
        name="unpack_own",
    )(place, own)


def unpack_other(place, other, biases, grad_two, grad_three):
    hidden = grad_two.shape[2]
    labels = grad_three.shape[1]
    anywhere = pl.BlockSpec(memory_space=pl.ANY)
    return pl.pallas_call(
        other_kernel,
        out_shape=(
            jax.ShapeDtypeStruct(grad_two.shape, F32),
            jax.ShapeDtypeStruct(grad_three.shape, F32),
            jax.ShapeDtypeStruct((1, hidden), F32),
            jax.ShapeDtypeStruct((1, hidden), F32),
            jax.ShapeDtypeStruct((1, labels), F32),
        ),
        in_specs=[pl.BlockSpec(memory_space=SMEM)] + vmem(2) + [anywhere] * 2,
        out_specs=(anywhere,) * 5,
        scratch_shapes=[
            VMEM((hidden, hidden), F32),
            VMEM((hidden, LANES), F32),
            VMEM((labels, hidden), F32),
            VMEM((1, hidden), F32),
            VMEM((1, hidden), F32),
            VMEM((1, labels), F32),
            pltpu.SemaphoreType.DMA((9,)),
            pltpu.SemaphoreType.DMA((3,)),
        ],
        input_output_aliases={3: 0, 4: 1},
        compiler_params=pltpu.CompilerParams(vmem_limit_bytes=16 << 20),
        name="unpack_other",
    )(place, other, biases, grad_two, grad_three)


def exchange(values, axes):
    return lax.all_to_all(values, axes, 0, 0, tiled=True)


def swap_core(values):
    return lax.ppermute(values, "core", [(0, 1), (1, 0)])


def local(
    feat_table,
    self_one,
    near_one,
    self_two,
    near_two,
    self_three,
    near_three,
    targets,
    seed_count,
    w_one,
    bias_one,
    w_two,
    bias_two,
    w_three,
    bias_three,
):
    cut_rows, hidden = w_one.shape[1:]
    labels = w_three.shape[2]
    chips = lax.axis_size(CHIPS)
    cap = self_one.shape[0] // (2 * chips)
    owner = lax.axis_index(DP) * lax.axis_size(CUTS) + lax.axis_index(CUTS)
    place = jnp.stack([lax.axis_index("core"), owner]).astype(jnp.int32)
    other_table = swap_core(feat_table)
    w_own = exchange(spread(w_one.reshape(-1, hidden), chips), CHIPS)
    rows = gather_rows(place, feat_table, other_table, self_one, near_one, chips)
    self_two, rows = lax.optimization_barrier((self_two, rows))
    picks = make_picks(self_two, near_two, self_three, near_three, cap)
    w_own, rows, picks = lax.optimization_barrier((w_own, rows, picks))
    w_other = swap_core(w_own)
    rows = exchange(rows, CHIPS)
    rows, w_own, w_other = lax.optimization_barrier((rows, w_own, w_other))
    other_rows = swap_core(rows)
    fans = (near_two.shape[0], near_three.shape[0])
    slope_one, *grads, ship = owner_pass(
        place, seed_count, rows, w_own, w_other, bias_one, picks, targets, w_two, bias_two, w_three, bias_three, fans
    )
    ship = swap_core(ship)
    one = first_grad(slope_one, grads[0], picks[0], w_two, fans[0])
    other_one = swap_core(one)
    late = late_products(place, one, (*grads, ship))
    parts = one_products(rows, other_rows, one, other_one, late)
    sums = sum_parts(exchange(parts, SAME_CORE))
    own = exchange(sums, SAME_CORE)
    other = swap_core(own)
    grad_one, grad_two, grad_three, biases = unpack_own(place, own, cut_rows, hidden, labels)
    grad_two, grad_three, bias_one, bias_two, bias_three = unpack_other(place, other, biases, grad_two, grad_three)
    return (
        grad_one,
        bias_one.reshape(-1),
        grad_two,
        bias_two.reshape(-1),
        jnp.transpose(grad_three, (0, 2, 1)),
        bias_three.reshape(-1),
    )


def solution(mesh):
    fine = Mesh(mesh.devices.reshape(2, 4, 4, 2, 2), ("y_hi", "x", "z", "y_lo", "core"))
    both = DP + CUTS
    return jax.shard_map(
        local,
        mesh=fine,
        in_specs=(
            P(CUTS, DP),
            P(DP),
            P(None, DP),
            P(both),
            P(None, both),
            P(both),
            P(None, both),
            P(both, None),
            P(),
            P(None, CUTS, None),
            P(),
            P(),
            P(),
            P(),
            P(),
        ),
        out_specs=(P(None, CUTS, None), P(), P(), P(), P(), P()),
        check_vma=False,
    )
```

```python
import functools

import jax
import jax.numpy as jnp
from jax import lax
from jax.experimental import pallas as pl
from jax.experimental.pallas import tpu as pltpu
from jax.sharding import Mesh, PartitionSpec as P

BF16 = jnp.bfloat16
F32 = jnp.float32
VMEM = pltpu.VMEM
SMEM = pltpu.SMEM
HBM = pltpu.MemorySpace.HBM

LANES = 128
SUB = 8
SPARE = 16
GATHER_UNROLL = 64
TABLE_PIECES = 16
ONE_ROWS = 64
TWO_ROWS = 32
TOP_ROWS = 8
LATE_ROWS = TWO_ROWS + TOP_ROWS
CHUNK_ROWS = ONE_ROWS + LATE_ROWS
PEERS = 64

DP = ("y_hi", "x")
CUTS = ("z", "y_lo", "core")
CHIPS = ("z", "y_lo")
SAME_CORE = DP + CHIPS


def dot(first, second, contract=((1,), (0,))):
    return lax.dot_general(first, second, (contract, ((), ())), preferred_element_type=F32)


def lead_dot(first, second):
    return dot(first, second, ((0,), (0,)))


def back_dot(first, second):
    return dot(first, second, ((1,), (1,)))


def exact_dot(picks, values):
    high = values.astype(BF16)
    low = (values - high.astype(F32)).astype(BF16)
    return dot(jnp.concatenate([picks, picks], axis=1), jnp.concatenate([high, low], axis=0))


def gelu_and_slope(values):
    square = values * values
    tanh = jnp.tanh(0.7978845608028654 * (values + 0.044715 * values * square))
    cdf = 0.5 * (1.0 + tanh)
    inner_slope = 0.7978845608028654 * (1.0 + 3.0 * 0.044715 * square)
    return values * cdf, cdf + 0.5 * values * (1.0 - tanh * tanh) * inner_slope


def vmem(count):
    return [pl.BlockSpec(memory_space=VMEM)] * count


def write_picks(self_ref, near_ref, back, pick):
    def counts(ids):
        total = jnp.zeros(spots.shape, F32)
        for offset in range(ids.shape[0]):
            total += (spots == ids[pl.ds(offset, 1), :]).astype(F32)
        return total

    spots = lax.broadcasted_iota(jnp.int32, (back.shape[0], self_ref.shape[1]), 0)
    both = jnp.concatenate([counts(self_ref), counts(near_ref)], axis=1)
    back[...] = both.astype(BF16)
    pick[...] = both.T.astype(BF16)


def gather_kernel(
    place_ref,
    own_ref,
    other_ref,
    self_ref,
    near_ref,
    out_ref,
    own,
    other,
    self_ids,
    near_ids,
    table,
    rows,
    sems,
    id_sems,
):
    core = place_ref[0]
    nodes = own_ref.shape[1]
    targets = self_ref.shape[0]
    fan = near_ref.shape[0] // targets
    chips = out_ref.shape[0]
    cap = targets // (2 * chips)
    width = nodes // TABLE_PIECES

    fetches = []
    for piece in range(TABLE_PIECES):
        spot = pl.ds(piece * width, width)
        for slot, (source, held) in enumerate(((own_ref, own), (other_ref, other))):
            fetch = pltpu.make_async_copy(source.at[:, spot], held.at[:, spot], sems.at[slot, piece])
            fetch.start()
            fetches.append(fetch)
    id_fetches = [
        pltpu.make_async_copy(self_ref, self_ids, id_sems.at[0]),
        pltpu.make_async_copy(near_ref, near_ids, id_sems.at[1]),
    ]
    for fetch in id_fetches:
        fetch.start()

    for piece in range(TABLE_PIECES):
        fetches[2 * piece].wait()
        fetches[2 * piece + 1].wait()

        @pl.loop(0, width // LANES, unroll=4)
        def _(block):
            spot = pl.ds(pl.multiple_of(piece * width + block * LANES, LANES), LANES)
            table[spot, :] = jnp.concatenate([own[:, spot], other[:, spot]], axis=0).T.astype(F32)

    for fetch in id_fetches:
        fetch.wait()

    @pl.loop(0, chips)
    def _(chip):
        first = (2 * chip + core) * cap

        @pl.loop(0, cap // GATHER_UNROLL)
        def _(group):
            start = group * GATHER_UNROLL
            mine = self_ids.at[pl.ds(first + start, GATHER_UNROLL)]
            others = [near_ids.at[pl.ds(offset * targets + first + start, GATHER_UNROLL)] for offset in range(fan)]
            for step in range(GATHER_UNROLL):
                total = table[pl.ds(others[0][step], 1), :]
                for ids in others[1:]:
                    total = total + table[pl.ds(ids[step], 1), :]
                rows[pl.ds(start + step, 1), :] = table[pl.ds(mine[step], 1), :]
                rows[pl.ds(cap + start + step, 1), :] = total

        half = lax.broadcasted_iota(jnp.int32, (cap, LANES), 1) < LANES // 2
        straight = rows[pl.ds(pl.multiple_of(core * cap, cap), cap), :] * jnp.where(core == 0, 1.0, 1.0 / fan)
        turned = rows[pl.ds(pl.multiple_of((1 - core) * cap, cap), cap), :] * jnp.where(core == 0, 1.0 / fan, 1.0)
        turned = pltpu.roll(turned, LANES // 2, 1)
        out_ref[chip, pl.ds(0, cap), :] = jnp.where(half, straight, turned).astype(BF16)
        out_ref[chip, pl.ds(cap, cap), :] = jnp.where(half, turned, straight).astype(BF16)


def gather_rows(place, own_table, other_table, self_one, near_one, chips):
    features, nodes = own_table.shape
    targets = self_one.shape[0]
    near_one = near_one.reshape(-1)
    cap = targets // (2 * chips)
    return pl.pallas_call(
        gather_kernel,
        out_shape=jax.ShapeDtypeStruct((chips, 2 * cap, LANES), BF16),
        in_specs=[pl.BlockSpec(memory_space=SMEM)] + [pl.BlockSpec(memory_space=pl.ANY)] * 4,
        out_specs=pl.BlockSpec(memory_space=VMEM),
        scratch_shapes=[
            VMEM((features, nodes), BF16),
            VMEM((features, nodes), BF16),
            SMEM(self_one.shape, jnp.int32),
            SMEM(near_one.shape, jnp.int32),
            VMEM((nodes, LANES), F32),
            VMEM((2 * cap, LANES), F32),
            pltpu.SemaphoreType.DMA((2, TABLE_PIECES)),
            pltpu.SemaphoreType.DMA((2,)),
        ],
        compiler_params=pltpu.CompilerParams(vmem_limit_bytes=24 << 20),
        cost_estimate=pl.CostEstimate(flops=1 << 27, bytes_accessed=40 << 20, transcendentals=0),
        name="gather_rows",
    )(place, own_table, other_table, self_one, near_one)


def spread_kernel(part_ref, out_ref, sems):
    copies = [pltpu.make_async_copy(part_ref, out_ref.at[chip], sems.at[chip]) for chip in range(out_ref.shape[0])]
    for copy in copies:
        copy.start()
    for copy in copies:
        copy.wait()


def spread(part, chips):
    return pl.pallas_call(
        spread_kernel,
        out_shape=jax.ShapeDtypeStruct((chips,) + part.shape, part.dtype),
        in_specs=vmem(1),
        out_specs=pl.BlockSpec(memory_space=pl.ANY),
        scratch_shapes=[pltpu.SemaphoreType.DMA((chips,))],
        name="spread",
    )(part)


def picks_kernel(self_two_ref, near_two_ref, self_three_ref, near_three_ref, back_two, pick_two, back_three, pick_three):
    write_picks(self_two_ref, near_two_ref, back_two, pick_two)
    write_picks(self_three_ref, near_three_ref, back_three, pick_three)


def make_picks(self_two, near_two, self_three, near_three, cap):
    mid_rows = self_two.shape[0]
    seeds = self_three.shape[0]
    shapes = [(cap, 2 * mid_rows), (2 * mid_rows, cap), (mid_rows, 2 * seeds), (2 * seeds, mid_rows)]
    return pl.pallas_call(
        picks_kernel,
        out_shape=tuple(jax.ShapeDtypeStruct(shape, BF16) for shape in shapes),
        in_specs=vmem(4),
        out_specs=tuple(vmem(4)),
        compiler_params=pltpu.CompilerParams(vmem_limit_bytes=8 << 20),
        name="make_picks",
    )(self_two.reshape(1, -1), near_two, self_three.reshape(1, -1), near_three)


def owner_kernel(
    fan_two,
    fan_three,
    place_ref,
    count_ref,
    counts_ref,
    rows_ref,
    w_own_ref,
    w_other_ref,
    bias_one_ref,
    pick_two,
    back_three,
    pick_three,
    targets_ref,
    w_two_ref,
    bias_two_ref,
    w_three_ref,
    bias_three_ref,
    slope_one,
    two_ref,
    mids,
    tops,
    logit_ref,
    ship_ref,
):
    core = place_ref[0]
    owner = place_ref[1]
    chips = rows_ref.shape[0]
    cap, hidden = slope_one.shape
    labels = w_three_ref.shape[1]
    mid_rows = mids.shape[1]
    seeds = tops.shape[1]
    half = LANES // 2
    front = pl.ds(pl.multiple_of(core * half, half), half)
    back = pl.ds(pl.multiple_of((1 - core) * half, half), half)

    wides = [rows_ref[chip, pl.ds(start, cap), :] for chip in range(chips) for start in (0, cap)]
    depths = [
        weights[chip, spot, :]
        for chip in range(chips)
        for weights, spot in ((w_own_ref, front), (w_own_ref, back), (w_other_ref, back), (w_other_ref, front))
    ]
    total = dot(jnp.concatenate(wides, axis=1), jnp.concatenate(depths, axis=0))
    hidden_one, slope = gelu_and_slope(total + bias_one_ref[...])
    slope_one[...] = slope

    mid = dot(pick_two[...], hidden_one.astype(BF16))
    self_mid = mid[:mid_rows].astype(BF16)
    near_mid = (mid[mid_rows:] / fan_two).astype(BF16)
    mids[0] = self_mid
    mids[1] = near_mid
    both = jnp.concatenate([self_mid, near_mid], axis=1)
    pre_two = dot(both, jnp.concatenate([w_two_ref[0], w_two_ref[1]], axis=0)) + bias_two_ref[...]
    hidden_two, slope_two = gelu_and_slope(pre_two)

    top = dot(pick_three[...], hidden_two.astype(BF16))
    self_top = top[:seeds].astype(BF16)
    near_top = (top[seeds:] / fan_three).astype(BF16)
    tops[0] = self_top
    tops[1] = near_top
    logits = back_dot(self_top, w_three_ref[0]) + back_dot(near_top, w_three_ref[1]) + bias_three_ref[...]

    scale = 1.0 / jnp.sqrt(jnp.sum(counts_ref[...].astype(F32), axis=1, keepdims=True))
    live = lax.broadcasted_iota(jnp.int32, (seeds, labels), 0) < count_ref[owner]
    slope = jax.nn.sigmoid(logits) - targets_ref[...].astype(F32)
    logit_grad = jnp.where(live, slope * scale, 0.0).astype(BF16)

    grads = [dot(logit_grad, w_three_ref[0]), dot(logit_grad, w_three_ref[1]) / fan_three]
    upstream = exact_dot(back_three[...], jnp.concatenate(grads, axis=0))
    pre_grad_two = (slope_two * upstream).astype(BF16)

    wide_logit = jnp.concatenate([logit_grad, jnp.zeros((seeds, LANES - labels), BF16)], axis=1)
    two_ref[...] = pre_grad_two
    logit_ref[...] = wide_logit
    ship_ref[pl.ds(0, mid_rows), :] = mids[1 - core]
    ship_ref[pl.ds(mid_rows, mid_rows), :] = pre_grad_two
    ship_ref[pl.ds(2 * mid_rows, seeds), :] = tops[1 - core]
    ship_ref[pl.ds(2 * mid_rows + seeds, seeds), pl.ds(0, LANES)] = wide_logit


def first_kernel(fan_two, slope_one, two_ref, back_two, w_two_ref, one_ref):
    grads = [back_dot(two_ref[...], w_two_ref[0]), back_dot(two_ref[...], w_two_ref[1]) / fan_two]
    upstream = exact_dot(back_two[...], jnp.concatenate(grads, axis=0))
    one_ref[...] = (slope_one[...] * upstream).astype(BF16)


def first_grad(slope_one, two, back_two, w_two, fan_two):
    return pl.pallas_call(
        functools.partial(first_kernel, fan_two),
        out_shape=jax.ShapeDtypeStruct(slope_one.shape, BF16),
        in_specs=vmem(4),
        out_specs=pl.BlockSpec(memory_space=VMEM),
        compiler_params=pltpu.CompilerParams(vmem_limit_bytes=24 << 20),
        cost_estimate=pl.CostEstimate(flops=1 << 29, bytes_accessed=4 << 20, transcendentals=0),
        name="first_grad",
    )(slope_one, two, back_two, w_two)


def late_kernel(place_ref, two_ref, mids, tops, logit_ref, ship_ref, one_ref, parts_ref):
    core = place_ref[0]
    hidden = one_ref.shape[1]
    mid_rows = two_ref.shape[0]
    seeds = logit_ref.shape[0]
    tiles = hidden // LANES
    count = hidden // PEERS
    other_mid = ship_ref[pl.ds(0, mid_rows), :]
    other_two = ship_ref[pl.ds(mid_rows, mid_rows), :]
    other_top = ship_ref[pl.ds(2 * mid_rows, seeds), :]
    other_logit = ship_ref[pl.ds(2 * mid_rows + seeds, seeds), pl.ds(0, LANES)]
    both_two = jnp.concatenate([two_ref[...], other_two], axis=0)
    two = lead_dot(jnp.concatenate([mids[core], other_mid], axis=0), both_two)
    both_logit = jnp.concatenate([logit_ref[...], other_logit], axis=0)
    top = lead_dot(both_logit, jnp.concatenate([tops[core], other_top], axis=0))
    bias_three = jnp.sum(logit_ref[...].astype(F32), axis=0, keepdims=True)
    biases = [
        jnp.sum(one_ref[...].astype(F32), axis=0, keepdims=True),
        jnp.sum(two_ref[...].astype(F32), axis=0, keepdims=True),
        jnp.concatenate([bias_three, jnp.zeros((1, hidden - LANES), F32)], axis=1),
        jnp.zeros((SPARE - 3, hidden), F32),
    ]
    top = jnp.concatenate([top[: LANES - SPARE]] + biases, axis=0).T
    for peer in range(PEERS):
        late = [
            two[peer * count : (peer + 1) * count, tile * LANES : (tile + 1) * LANES] for tile in range(tiles)
        ]
        late.append(top[peer * count : (peer + 1) * count, :])
        parts_ref[peer, pl.ds(ONE_ROWS, LATE_ROWS), :] = jnp.concatenate(late, axis=0).astype(BF16)


def late_products(place, one, grads):
    return pl.pallas_call(
        late_kernel,
        out_shape=jax.ShapeDtypeStruct((PEERS, CHUNK_ROWS, LANES), BF16),
        in_specs=[pl.BlockSpec(memory_space=SMEM)] + vmem(1 + len(grads)),
        out_specs=pl.BlockSpec(memory_space=VMEM),
        compiler_params=pltpu.CompilerParams(vmem_limit_bytes=24 << 20),
        cost_estimate=pl.CostEstimate(flops=1 << 29, bytes_accessed=4 << 20, transcendentals=0),
        name="late_products",
    )(place, *grads, one)


def one_kernel(rows_ref, other_rows_ref, one_ref, other_one_ref, late_ref, parts_ref):
    chips = rows_ref.shape[0]
    cap, hidden = one_ref.shape
    count = hidden // PEERS
    mine = pl.ds(0, cap)
    theirs = pl.ds(cap, cap)
    flipped = jnp.concatenate([one_ref[...].T, other_one_ref[...].T], axis=1)
    for pair in range(chips // 2):
        blocks = [
            jnp.concatenate([rows_ref[chip, mine, :], other_rows_ref[chip, theirs, :]], axis=0)
            for chip in (2 * pair, 2 * pair + 1)
        ]
        block = dot(flipped, jnp.concatenate(blocks, axis=1))
        for peer in range(PEERS):
            line = block[peer * count : (peer + 1) * count]
            cell = jnp.concatenate([line[:, :LANES], line[:, LANES:]], axis=0)
            parts_ref[peer, pl.ds(pair * 2 * SUB, 2 * SUB), :] = cell.astype(BF16)


def one_products(rows, other_rows, one, other_one, late):
    return pl.pallas_call(
        one_kernel,
        out_shape=jax.ShapeDtypeStruct(late.shape, BF16),
        in_specs=vmem(5),
        out_specs=pl.BlockSpec(memory_space=VMEM),
        input_output_aliases={4: 0},
        compiler_params=pltpu.CompilerParams(vmem_limit_bytes=24 << 20),
        cost_estimate=pl.CostEstimate(flops=1 << 30, bytes_accessed=8 << 20, transcendentals=0),
        name="one_products",
    )(rows, other_rows, one, other_one, late)


def owner_pass(place, seed_count, rows, w_own, w_other, bias_one, picks, targets, w_two, bias_two, w_three, bias_three,
               fans):
    hidden = w_two.shape[2]
    labels = w_three.shape[2]
    cap = picks[1].shape[1]
    mid_rows = picks[2].shape[0]
    seeds = targets.shape[0]
    return pl.pallas_call(
        functools.partial(owner_kernel, *fans),
        out_shape=(
            jax.ShapeDtypeStruct((cap, hidden), F32),
            jax.ShapeDtypeStruct((mid_rows, hidden), BF16),
            jax.ShapeDtypeStruct((2, mid_rows, hidden), BF16),
            jax.ShapeDtypeStruct((2, seeds, hidden), BF16),
            jax.ShapeDtypeStruct((seeds, LANES), BF16),
            jax.ShapeDtypeStruct((2 * (mid_rows + seeds), hidden), BF16),
        ),
        in_specs=[pl.BlockSpec(memory_space=SMEM)] * 2 + vmem(13),
        out_specs=tuple(vmem(6)),
        compiler_params=pltpu.CompilerParams(vmem_limit_bytes=24 << 20),
        cost_estimate=pl.CostEstimate(flops=1 << 31, bytes_accessed=10 << 20, transcendentals=1 << 19),
        name="owner_pass",
    )(
        place, seed_count, seed_count.reshape(1, -1), rows, w_own, w_other, bias_one.reshape(1, -1), *picks[1:],
        targets, w_two, bias_two.reshape(1, -1), jnp.transpose(w_three, (0, 2, 1)), bias_three.reshape(1, -1),
    )


def sum_kernel(parts_ref, out_ref):
    total = parts_ref[0].astype(F32)
    for peer in range(1, PEERS):
        total = total + parts_ref[peer].astype(F32)
    late = total[ONE_ROWS:]
    chips = ONE_ROWS // SUB
    for chip in range(chips):
        block = jnp.concatenate([total[chip * SUB : (chip + 1) * SUB], late], axis=0).astype(BF16)
        for group in range(PEERS // chips):
            out_ref[group * chips + chip] = block


def sum_parts(parts):
    return pl.pallas_call(
        sum_kernel,
        out_shape=jax.ShapeDtypeStruct((PEERS, SUB + LATE_ROWS, LANES), BF16),
        in_specs=vmem(1),
        out_specs=pl.BlockSpec(memory_space=VMEM),
        compiler_params=pltpu.CompilerParams(vmem_limit_bytes=24 << 20),
        name="sum_parts",
    )(parts)


def write_late(ref, side, grad_two, grad_three, two, top, three, sems):
    hidden = two.shape[0]
    labels = three.shape[0]
    count = hidden // PEERS
    pieces = sems.shape[0] - 1
    step = hidden // pieces
    copies = []
    for peer in range(PEERS):
        cells = ref[peer].astype(F32)
        for tile in range(hidden // LANES):
            two[pl.ds(peer * count, count), pl.ds(tile * LANES, LANES)] = cells[
                SUB + tile * count : SUB + (tile + 1) * count
            ]
        top[pl.ds(peer * count, count), :] = cells[SUB + TWO_ROWS :]
        done = (peer + 1) * count
        if done % step == 0:
            spot = pl.ds(done - step, step)
            copies.append(pltpu.make_async_copy(two.at[spot], grad_two.at[side, spot], sems.at[len(copies)]))
            copies[-1].start()
    flipped = top[...].T
    three[...] = flipped[:labels]
    copies.append(pltpu.make_async_copy(three, grad_three.at[side], sems.at[pieces]))
    copies[-1].start()
    return flipped[labels:], copies


def own_kernel(
    place_ref,
    own_ref,
    grad_one,
    grad_two,
    grad_three,
    biases,
    flat,
    one,
    two,
    top,
    three,
    sems,
    one_sem,
):
    cut_rows, hidden = one.shape[1:]
    count = hidden // PEERS
    for peer in range(PEERS):
        flat[pl.ds(peer * count, count), :] = own_ref[peer].astype(F32)[:SUB]
    turned = flat[...].T
    one[place_ref[0]] = turned[:cut_rows]
    one[1 - place_ref[0]] = turned[cut_rows:]
    one_copy = pltpu.make_async_copy(one, grad_one, one_sem)
    one_copy.start()
    kept, copies = write_late(own_ref, place_ref[0], grad_two, grad_three, two, top, three, sems)
    biases[...] = kept
    for copy in [one_copy] + copies:
        copy.wait()


def other_kernel(
    place_ref,
    other_ref,
    biases,
    two_in,
    three_in,
    grad_two,
    grad_three,
    bias_one,
    bias_two,
    bias_three,
    two,
    top,
    three,
    first,
    second,
    third,
    sems,
    bias_sems,
):
    kept, copies = write_late(other_ref, 1 - place_ref[0], grad_two, grad_three, two, top, three, sems)
    kept = kept + biases[...]
    first[...] = kept[0:1]
    second[...] = kept[1:2]
    third[...] = kept[2:3, : three.shape[0]]
    for slot, (held, out) in enumerate(((first, bias_one), (second, bias_two), (third, bias_three))):
        copies.append(pltpu.make_async_copy(held, out, bias_sems.at[slot]))
        copies[-1].start()
    for copy in copies:
        copy.wait()


def unpack_own(place, own, cut_rows, hidden, labels):
    anywhere = pl.BlockSpec(memory_space=pl.ANY)
    return pl.pallas_call(
        own_kernel,
        out_shape=(
            jax.ShapeDtypeStruct((2, cut_rows, hidden), F32),
            jax.ShapeDtypeStruct((2, hidden, hidden), F32),
            jax.ShapeDtypeStruct((2, labels, hidden), F32),
            jax.ShapeDtypeStruct((SPARE, hidden), F32),
        ),
        in_specs=[pl.BlockSpec(memory_space=SMEM)] + vmem(1),
        out_specs=(anywhere,) * 3 + tuple(vmem(1)),
        scratch_shapes=[
            VMEM((hidden, LANES), F32),
            VMEM((2, cut_rows, hidden), F32),
            VMEM((hidden, hidden), F32),
            VMEM((hidden, LANES), F32),
            VMEM((labels, hidden), F32),
            pltpu.SemaphoreType.DMA((9,)),
            pltpu.SemaphoreType.DMA,
        ],
        compiler_params=pltpu.CompilerParams(vmem_limit_bytes=16 << 20),
        cost_estimate=pl.CostEstimate(flops=1 << 22, bytes_accessed=4 << 20, transcendentals=0),
        name="unpack_own",
    )(place, own)


def unpack_other(place, other, biases, grad_two, grad_three):
    hidden = grad_two.shape[2]
    labels = grad_three.shape[1]
    anywhere = pl.BlockSpec(memory_space=pl.ANY)
    return pl.pallas_call(
        other_kernel,
        out_shape=(
            jax.ShapeDtypeStruct(grad_two.shape, F32),
            jax.ShapeDtypeStruct(grad_three.shape, F32),
            jax.ShapeDtypeStruct((1, hidden), F32),
            jax.ShapeDtypeStruct((1, hidden), F32),
            jax.ShapeDtypeStruct((1, labels), F32),
        ),
        in_specs=[pl.BlockSpec(memory_space=SMEM)] + vmem(2) + [anywhere] * 2,
        out_specs=(anywhere,) * 5,
        scratch_shapes=[
            VMEM((hidden, hidden), F32),
            VMEM((hidden, LANES), F32),
            VMEM((labels, hidden), F32),
            VMEM((1, hidden), F32),
            VMEM((1, hidden), F32),
            VMEM((1, labels), F32),
            pltpu.SemaphoreType.DMA((9,)),
            pltpu.SemaphoreType.DMA((3,)),
        ],
        input_output_aliases={3: 0, 4: 1},
        compiler_params=pltpu.CompilerParams(vmem_limit_bytes=16 << 20),
        name="unpack_other",
    )(place, other, biases, grad_two, grad_three)


def exchange(values, axes):
    return lax.all_to_all(values, axes, 0, 0, tiled=True)


def swap_core(values):
    return lax.ppermute(values, "core", [(0, 1), (1, 0)])


def local(
    feat_table,
    self_one,
    near_one,
    self_two,
    near_two,
    self_three,
    near_three,
    targets,
    seed_count,
    w_one,
    bias_one,
    w_two,
    bias_two,
    w_three,
    bias_three,
):
    cut_rows, hidden = w_one.shape[1:]
    labels = w_three.shape[2]
    chips = lax.axis_size(CHIPS)
    cap = self_one.shape[0] // (2 * chips)
    owner = lax.axis_index(DP) * lax.axis_size(CUTS) + lax.axis_index(CUTS)
    place = jnp.stack([lax.axis_index("core"), owner]).astype(jnp.int32)
    other_table = swap_core(feat_table)
    w_own = exchange(spread(w_one.reshape(-1, hidden), chips), CHIPS)
    rows = gather_rows(place, feat_table, other_table, self_one, near_one, chips)
    self_two, rows = lax.optimization_barrier((self_two, rows))
    picks = make_picks(self_two, near_two, self_three, near_three, cap)
    w_own, rows, picks = lax.optimization_barrier((w_own, rows, picks))
    w_other = swap_core(w_own)
    rows = exchange(rows, CHIPS)
    rows, w_own, w_other = lax.optimization_barrier((rows, w_own, w_other))
    other_rows = swap_core(rows)
    fans = (near_two.shape[0], near_three.shape[0])
    slope_one, *grads, ship = owner_pass(
        place, seed_count, rows, w_own, w_other, bias_one, picks, targets, w_two, bias_two, w_three, bias_three, fans
    )
    ship = swap_core(ship)
    one = first_grad(slope_one, grads[0], picks[0], w_two, fans[0])
    other_one = swap_core(one)
    late = late_products(place, one, (*grads, ship))
    parts = one_products(rows, other_rows, one, other_one, late)
    sums = sum_parts(exchange(parts, SAME_CORE))
    own = exchange(sums, SAME_CORE)
    other = swap_core(own)
    grad_one, grad_two, grad_three, biases = unpack_own(place, own, cut_rows, hidden, labels)
    grad_two, grad_three, bias_one, bias_two, bias_three = unpack_other(place, other, biases, grad_two, grad_three)
    return (
        grad_one,
        bias_one.reshape(-1),
        grad_two,
        bias_two.reshape(-1),
        jnp.transpose(grad_three, (0, 2, 1)),
        bias_three.reshape(-1),
    )


def solution(mesh):
    fine = Mesh(mesh.devices.reshape(2, 4, 4, 2, 2), ("y_hi", "x", "z", "y_lo", "core"))
    both = DP + CUTS
    return jax.shard_map(
        local,
        mesh=fine,
        in_specs=(
            P(CUTS, DP),
            P(DP),
            P(None, DP),
            P(both),
            P(None, both),
            P(both),
            P(None, both),
            P(both, None),
            P(),
            P(None, CUTS, None),
            P(),
            P(),
            P(),
            P(),
            P(),
        ),
        out_specs=(P(None, CUTS, None), P(), P(), P(), P(), P()),
        check_vma=False,
    )
```
